32 devices in a mesh: fsdp: 4 (over y, x), dp: 8 (over z, core).
Axes of the slice: x: 2, y: 2, z: 4, core: 2. Of those that a mesh axis runs over, the one named last changes fastest.
Arguments:
- tokens: bfloat16 [8, 1024, 2048], P('dp', 'fsdp'), may hold values from -6 to 6
- segments: int32 [8, 1024], P('dp'), may hold values from 0 to 4, as said below
- attn_gain: bfloat16 [2048], P('fsdp'), may hold values from 0.25 to 1.75
- w_query: bfloat16 [2048, 2048], P('fsdp'), may hold values from -0.125 to 0.125
- w_key: bfloat16 [2048, 1024], P('fsdp'), may hold values from -0.125 to 0.125
- w_value: bfloat16 [2048, 1024], P('fsdp'), may hold values from -0.125 to 0.125
- query_gain: bfloat16 [128], P('fsdp'), may hold values from 0.25 to 1.75
- key_gain: bfloat16 [128], P('fsdp'), may hold values from 0.25 to 1.75
- w_out: bfloat16 [2048, 2048], P(None, 'fsdp'), may hold values from -1.5 to 1.5
- mlp_gain: bfloat16 [2048], P('fsdp'), may hold values from 0.25 to 1.75
- w_gate: bfloat16 [2048, 6144], P('fsdp'), may hold values from -0.125 to 0.125
- w_up: bfloat16 [2048, 6144], P('fsdp'), may hold values from -0.125 to 0.125
- w_down: bfloat16 [6144, 2048], P(None, 'fsdp'), may hold values from -0.078125 to 0.078125
- cotangent: bfloat16 [8, 1024, 2048], P('dp', 'fsdp'), may hold values from -6 to 6
Outputs:
- output: bfloat16 [8, 1024, 2048], P('dp', 'fsdp')
- input_grad: float32 [8, 1024, 2048], P('dp', 'fsdp')
- grad_attn_gain: float32 [2048], P('fsdp')
- grad_query: float32 [2048, 2048], P('fsdp')
- grad_key: float32 [2048, 1024], P('fsdp')
- grad_value: float32 [2048, 1024], P('fsdp')
- grad_query_gain: float32 [128], P('fsdp')
- grad_key_gain: float32 [128], P('fsdp')
- grad_out: float32 [2048, 2048], P(None, 'fsdp')
- grad_mlp_gain: float32 [2048], P('fsdp')
- grad_gate: float32 [2048, 6144], P('fsdp')
- grad_up: float32 [2048, 6144], P('fsdp')
- grad_down: float32 [6144, 2048], P(None, 'fsdp')
The draws below stay inside these ranges and needn't reach their ends.
Inputs may be any that keep to these rules, and one draw needn't show every extreme that they name: `segments`: document numbers start at 0 and never fall along a sequence; each sequence holds exactly 5 documents: 2 new ones begin within positions 1 to 128 and 2 within the last 128 positions.
All inputs are finite; a program needn't handle non-finite values.
Results may differ from the reference program's by a relative error of at most 0.02.
Values may be sent and summed in bfloat16 or wider, within the bound.
No kernel may reach another device: no remote copies, remote signals or barrier semaphores. Data moves between devices by JAX's collectives and lax.ppermute only.
A program may use at most 576 MiB of HBM per device.

```python
import math
import jax
import jax.numpy as jnp
from jax import lax

D = 2048
HEADS = 16
KV_HEADS = 8
HEAD = 128
FF = 6144
TOK_DEV = 256
EDGE = 2
LEN = 1024
SEQS = 8


def one_sequence(seq_key):
    head_key, tail_key = jax.random.split(seq_key)
    head_span = TOK_DEV // 2
    head_marks = jax.random.permutation(head_key, head_span)[:EDGE] + 1
    tail_marks = LEN - 1 - jax.random.permutation(tail_key, head_span)[:EDGE]
    doc_starts = jnp.zeros((LEN,), jnp.int32).at[head_marks].set(1).at[tail_marks].set(1)
    return jnp.cumsum(doc_starts).astype(jnp.int32)


def draw_segments(key, part):
    key = jax.random.fold_in(key, 11)
    seq_keys = jax.random.split(key, SEQS)
    return jax.vmap(one_sequence)(seq_keys)


def strengthened(values, rng, source, target, parts, factor):
    def block_of(axis_at):
        return (jnp.arange(values.shape[axis_at]) // (values.shape[axis_at] // parts)).reshape((-1,) + (1,) * (values.ndim - 1 - axis_at))

    one_side = jax.random.permutation(rng, parts)[block_of(target)]
    second = (block_of(target) + parts // 2) % parts
    return jnp.where((block_of(source) == one_side) | (block_of(source) == second), factor * values, values)


def shard_levels(rng, extent, cuts, smallest, high):
    def one(dim, blocks):
        draws = jax.random.uniform(jax.random.fold_in(jax.random.fold_in(rng, 6), dim), (blocks,), jnp.float32, smallest / len(cuts), high / len(cuts))
        return jnp.repeat(jnp.exp(draws), extent[dim] // blocks).reshape((-1,) + (1,) * (len(extent) - dim - 1))

    factor_of = one(*cuts[0])
    for cut in cuts[1:]:
        factor_of = factor_of * one(*cut)
    return factor_of


def normal_values(own_key, dims, scale, reach, pieces=(), kind=jnp.bfloat16):
    values = scale * jax.random.normal(own_key, dims, jnp.float32)
    if pieces:
        values = values * shard_levels(own_key, dims, pieces, -0.22, 0.18)
    return jnp.clip(values, -reach, reach).astype(kind)


def noise_with(rng, dims, width, bound, shards, heavy, kind=jnp.bfloat16):
    values = width * jax.random.normal(rng, dims, jnp.float32)
    if shards:
        values = values * shard_levels(rng, dims, shards, -0.22, 0.18)
    return jnp.clip(strengthened(values, jax.random.fold_in(rng, 3), *heavy), -bound, bound).astype(kind)


def setup_inputs(seed: int = 0) -> dict:
    streams_of = jax.random.split(jax.random.key(seed), 15)
    tokens = normal_values(streams_of[0], (SEQS, LEN, D), 1.0, 6.0, ((0, 8), (1, 4)))
    segments = draw_segments(jax.random.fold_in(streams_of[14], 71), 0)
    attn_gain = jnp.clip(1.0 + 0.15 * jax.random.normal(streams_of[2], (D,), jnp.float32), 0.25, 1.75).astype(jnp.bfloat16)
    w_query = normal_values(streams_of[3], (D, HEADS * HEAD), D ** -0.5, 0.125, ((0, 4),))
    w_key = normal_values(streams_of[4], (D, KV_HEADS * HEAD), D ** -0.5, 0.125, ((0, 4),))
    w_value = normal_values(streams_of[5], (D, KV_HEADS * HEAD), D ** -0.5, 0.125, ((0, 4),))
    query_gain = jnp.clip(1.0 + 0.15 * jax.random.normal(streams_of[6], (HEAD,), jnp.float32), 0.25, 1.75).astype(jnp.bfloat16)
    key_gain = jnp.clip(1.0 + 0.15 * jax.random.normal(streams_of[7], (HEAD,), jnp.float32), 0.25, 1.75).astype(jnp.bfloat16)
    w_out = normal_values(streams_of[8], (HEADS * HEAD, D), (max(8 * HEADS * HEAD // LEN, 1)) ** -0.5, 1.5, ((1, 4),))
    mlp_gain = jnp.clip(1.0 + 0.15 * jax.random.normal(streams_of[9], (D,), jnp.float32), 0.25, 1.75).astype(jnp.bfloat16)
    w_gate = normal_values(streams_of[10], (D, FF), D ** -0.5, 0.125, ((0, 4),))
    w_up = normal_values(streams_of[11], (D, FF), D ** -0.5, 0.125, ((0, 4),))
    w_down = normal_values(streams_of[12], (FF, D), FF ** -0.5, 0.078125, ((1, 4),))
    cotangent = noise_with(streams_of[13], (SEQS, LEN, D), 1.0, 6.0, ((0, 8), (1, 4)), (1, 2, 4, 2.0))
    return {"tokens": tokens, "segments": segments, "attn_gain": attn_gain, "w_query": w_query, "w_key": w_key, "w_value": w_value, "query_gain": query_gain, "key_gain": key_gain, "w_out": w_out, "mlp_gain": mlp_gain, "w_gate": w_gate, "w_up": w_up, "w_down": w_down, "cotangent": cotangent}


@jax.custom_vjp
def low(v):
    return lax.optimization_barrier(v.astype(jnp.bfloat16)).astype(jnp.float32)

@jax.custom_vjp
def low_back(v):
    return v

def low_keep(v):
    return (low(v), None)

def low_pass(kept, grad):
    return (grad,)

def back_keep(v):
    return (v, None)

def back_low(kept, grad):
    return (low(grad),)
low.defvjp(low_keep, low_pass)
low_back.defvjp(back_keep, back_low)
epsilon = 1e-06
rope_base = 1000000.0
masked_score = -1e+30
highest = lax.Precision.HIGHEST

def rms_scale(vector):
    return lax.rsqrt(lax.optimization_barrier(jnp.mean(vector * vector, axis=-1, keepdims=True)) + epsilon)

def rotate(vector, cos_table, sin_table):
    half_size = vector.shape[-1] // 2
    turned = jnp.concatenate([-vector[..., half_size:], vector[..., :half_size]], axis=-1)
    return vector * cos_table + turned * sin_table

def rope_tables(positions, head_size):
    freq_index = jnp.arange(head_size // 2).astype(jnp.float32)
    inverse = rope_base ** (-2.0 * freq_index / head_size)
    angles = positions.astype(jnp.float32)[:, None] * inverse[None, :]
    angles = jnp.concatenate([angles, angles], axis=-1)
    return (jnp.cos(angles)[:, None, :], jnp.sin(angles)[:, None, :])

def doc_positions(doc_query, doc_ids, token_index):
    earlier = lax.optimization_barrier(jnp.sum((doc_ids[None, :] < doc_query[:, None]).astype(jnp.int32), axis=1))
    return token_index - earlier

def layer(stream, doc_ids, params):
    attn_gain, w_query, w_key, w_value, query_gain, key_gain, w_out, mlp_gain, w_gate, w_up, w_down = params
    length = stream.shape[0]
    group_size = HEADS // KV_HEADS
    score_scale = 1.0 / math.sqrt(HEAD)
    token_index = jnp.arange(length, dtype=jnp.int32)
    cos_table, sin_table = rope_tables(doc_positions(doc_ids, doc_ids, token_index), HEAD)
    normed = low(stream * rms_scale(stream) * attn_gain)
    query_raw = low_back(jnp.dot(normed, w_query, precision=highest)).reshape(length, HEADS, HEAD)
    key_raw = low_back(jnp.dot(normed, w_key, precision=highest)).reshape(length, KV_HEADS, HEAD)
    values = low(low_back(jnp.dot(normed, w_value, precision=highest))).reshape(length, KV_HEADS, HEAD)
    queries = low(rotate(query_raw * rms_scale(query_raw) * query_gain, cos_table, sin_table))
    key_rows = low(rotate(key_raw * rms_scale(key_raw) * key_gain, cos_table, sin_table))
    grouped = queries.reshape(length, KV_HEADS, group_size, HEAD)
    scores = jnp.einsum('qkgd,skd->kgqs', grouped, key_rows, precision=highest) * score_scale
    allowed = (doc_ids[:, None] == doc_ids[None, :]) & (token_index[None, :] <= token_index[:, None])
    scores = low_back(jnp.where(allowed, scores, masked_score))
    shifted = jnp.exp(scores - lax.optimization_barrier(jnp.max(scores, axis=-1, keepdims=True)))
    attn_probs = low(shifted / lax.optimization_barrier(jnp.sum(shifted, axis=-1, keepdims=True)))
    attended = jnp.einsum('kgqs,skd->qkgd', attn_probs, values, precision=highest).reshape(length, HEADS * HEAD)
    attended = low(low_back(attended))
    middle = stream + low_back(jnp.dot(attended, w_out, precision=highest))
    normed_mlp = low(middle * rms_scale(middle) * mlp_gain)
    gate_act = low_back(jnp.dot(normed_mlp, w_gate, precision=highest))
    upward = low_back(jnp.dot(normed_mlp, w_up, precision=highest))
    hidden = low(gate_act / (1.0 + jnp.exp(-gate_act)) * upward)
    return middle + low_back(jnp.dot(hidden, w_down, precision=highest))

def reference(tokens, segments, attn_gain, w_query, w_key, w_value, query_gain, key_gain, w_out, mlp_gain, w_gate, w_up, w_down, cotangent):
    params = tuple((weight.astype(jnp.float32) for weight in (attn_gain, w_query, w_key, w_value, query_gain, key_gain, w_out, mlp_gain, w_gate, w_up, w_down)))
    stream = tokens.astype(jnp.float32)
    checked = jax.checkpoint(layer)

    def forward(stream_all, weights_all):
        return lax.map(lambda seq_pair: checked(seq_pair[0], seq_pair[1], weights_all), (stream_all, segments))
    result, pullback = jax.vjp(forward, stream, params)
    grad_stream, weight_grads = pullback(cotangent.astype(jnp.float32))
    return (result.astype(jnp.bfloat16), grad_stream, weight_grads[0], weight_grads[1], weight_grads[2], weight_grads[3], weight_grads[4], weight_grads[5], weight_grads[6], weight_grads[7], weight_grads[8], weight_grads[9], weight_grads[10])
```

```python
import math

import jax
import jax.numpy as jnp
from jax import lax
from jax.sharding import Mesh
from jax.sharding import PartitionSpec as P

HEADS = 16
KV_HEADS = 8
HEAD = 128
GROUP = HEADS // KV_HEADS

epsilon = 1e-06
rope_base = 1000000.0
masked_score = -1e30
score_scale = 1.0 / math.sqrt(HEAD)

bf16 = jnp.bfloat16
f32 = jnp.float32


def matmul(first, second):
    return jnp.dot(first, second, preferred_element_type=f32)


def matmul_tn(first, second):
    return lax.dot_general(first, second, (((0,), (0,)), ((), ())), preferred_element_type=f32)


def matmul_nt(first, second):
    return lax.dot_general(first, second, (((1,), (1,)), ((), ())), preferred_element_type=f32)


def rms_scale(vector):
    return lax.rsqrt(jnp.mean(vector * vector, axis=-1, keepdims=True) + epsilon)


def norm_back(vector, scale, gain, incoming):
    scaled = gain * incoming
    d_vector = scale * scaled - vector * (scale**3) * jnp.mean(
        vector * scaled, axis=-1, keepdims=True
    )
    return d_vector, incoming * vector * scale


def swap(value, axis, k):
    return lax.ppermute(value, axis, [(j, j ^ k) for j in range(lax.axis_size(axis))])


def core_swap(value):
    return swap(value, "core", 1)


def rows_of(value, start, size):
    return lax.dynamic_slice_in_dim(value, start, size, axis=0)


def gather_rows(shard):
    n, me = lax.axis_size("fsdp"), lax.axis_index("fsdp")
    size = shard.shape[0]
    blocks = {0: shard}
    if n == 4 and size % 32 == 0:
        half = size // 2
        blocks[1] = swap(shard, "fsdp", 1)
        blocks[2] = swap(shard, "fsdp", 2)
        first = swap(blocks[1][:half], "fsdp", 2)
        second = swap(blocks[2][half:], "fsdp", 1)
        blocks[3] = jnp.concatenate([first, second], axis=0)
    else:
        for k in range(1, n):
            blocks[k] = swap(shard, "fsdp", k)
    out = jnp.zeros((n * size,) + shard.shape[1:], shard.dtype)
    for k, block in blocks.items():
        out = lax.dynamic_update_slice_in_dim(out, block, (me ^ k) * size, axis=0)
    return out


def scatter_rows(partial):
    n, me = lax.axis_size("fsdp"), lax.axis_index("fsdp")
    size = partial.shape[0] // n
    blocks = [rows_of(partial, (me ^ k) * size, size) for k in range(n)]
    total = blocks[0].astype(f32)
    if n == 4 and size % 32 == 0:
        half = size // 2
        first = swap(blocks[3][:half], "fsdp", 1)
        second = swap(blocks[3][half:], "fsdp", 2)
        top = blocks[2][:half].astype(f32) + first.astype(f32)
        low = blocks[1][half:].astype(f32) + second.astype(f32)
        to_x = jnp.concatenate([blocks[1][:half], low.astype(bf16)], axis=0)
        to_y = jnp.concatenate([top.astype(bf16), blocks[2][half:]], axis=0)
        total = total + swap(to_x, "fsdp", 1).astype(f32) + swap(to_y, "fsdp", 2).astype(f32)
    else:
        for k in range(1, n):
            total = total + swap(blocks[k], "fsdp", k).astype(f32)
    return total


def spread_rows(parts):
    n, me, core = lax.axis_size("fsdp"), lax.axis_index("fsdp"), lax.axis_index("core")
    rows = parts[0].shape[0]
    half = rows // 2
    widths = [part.shape[1] // n for part in parts]

    def piece(start, size, block):
        return jnp.concatenate(
            [
                lax.dynamic_slice(part, (start, block * width), (size, width))
                for part, width in zip(parts, widths)
            ],
            axis=1,
        )

    out = jnp.zeros((n * rows, sum(widths)), parts[0].dtype)
    out = lax.dynamic_update_slice(out, piece(0, rows, me), (me * rows, 0))
    for k in range(1, n):
        got = swap(piece(core * half, half, me ^ k), "fsdp", k)
        other = core_swap(got)
        base = (me ^ k) * rows
        out = lax.dynamic_update_slice(out, got, (base + core * half, 0))
        out = lax.dynamic_update_slice(out, other, (base + (1 - core) * half, 0))
    return out


def spread_columns(part):
    n, me, core = lax.axis_size("fsdp"), lax.axis_index("fsdp"), lax.axis_index("core")
    rows, width = part.shape[0] // n, part.shape[1]
    half = rows // 2
    out = jnp.zeros((rows, n * width), part.dtype)
    out = lax.dynamic_update_slice(out, rows_of(part, me * rows, rows), (0, me * width))
    for k in range(1, n):
        got = swap(rows_of(part, (me ^ k) * rows + core * half, half), "fsdp", k)
        other = core_swap(got)
        base = (me ^ k) * width
        out = lax.dynamic_update_slice(out, got, (core * half, base))
        out = lax.dynamic_update_slice(out, other, ((1 - core) * half, base))
    return out


def line_scatter(chunks):
    nz, z = lax.axis_size("z"), lax.axis_index("z")

    def chunk(index):
        return lax.dynamic_index_in_dim(
            chunks, jnp.clip(index, 0, nz - 1), 0, keepdims=False
        ).astype(f32)

    up = down = None
    for s in range(1, nz):
        up_send, down_send = chunk(z + nz - s), chunk(z - nz + s)
        if up is not None:
            up_send, down_send = up_send + up.astype(f32), down_send + down.astype(f32)
        up = lax.ppermute(up_send.astype(bf16), "z", [(j, j + 1) for j in range(s)])
        down = lax.ppermute(down_send.astype(bf16), "z", [(j, j - 1) for j in range(nz - s, nz)])
    total = chunk(z)
    if up is not None:
        total = total + up.astype(f32) + down.astype(f32)
    return total.astype(bf16)


def line_gather(chunk):
    nz, z = lax.axis_size("z"), lax.axis_index("z")
    ups, downs = [chunk], [chunk]
    for s in range(1, nz):
        ups.append(lax.ppermute(ups[-1], "z", [(j, j + 1) for j in range(s - 1, nz - 1)]))
        downs.append(lax.ppermute(downs[-1], "z", [(j, j - 1) for j in range(1, nz - s + 1)]))
    out = jnp.zeros((nz,) + chunk.shape, chunk.dtype)
    out = lax.dynamic_update_index_in_dim(out, chunk, z, 0)
    for s in range(1, nz):
        block = jnp.where(z >= s, ups[s], downs[nz - s])
        out = lax.dynamic_update_index_in_dim(out, block, (z - s) % nz, 0)
    return out


def core_halves(mine):
    core = lax.axis_index("core")
    other = core_swap(mine)
    first = jnp.where(core == 0, mine, other)
    second = jnp.where(core == 0, other, mine)
    return jnp.stack([first, second]).astype(f32)


def reduce_row_grads(grad):
    n, nz = lax.axis_size("fsdp"), lax.axis_size("z")
    me, core = lax.axis_index("fsdp"), lax.axis_index("core")
    width = grad.shape[1]
    piece = grad.shape[0] // (n * 2 * nz)
    split = grad.reshape(n, 2, nz, piece, width)
    keep = lax.dynamic_index_in_dim(split, core, 1, keepdims=False)
    send = lax.dynamic_index_in_dim(split, 1 - core, 1, keepdims=False)
    both = (keep.astype(f32) + core_swap(send).astype(f32)).astype(bf16)
    summed = line_scatter(jnp.swapaxes(both, 0, 1))
    out = jnp.zeros((piece, n, width), bf16)
    for k in range(n):
        block = lax.dynamic_index_in_dim(summed, me ^ k, 0, keepdims=False)
        if k:
            block = swap(block, "fsdp", k)
        out = lax.dynamic_update_index_in_dim(out, block, me ^ k, 1)
    full = core_halves(line_gather(out))
    return full.reshape(2 * nz * piece, n, width)


def reduce_column_grads(grad):
    n, nz = lax.axis_size("fsdp"), lax.axis_size("z")
    me, core = lax.axis_index("fsdp"), lax.axis_index("core")
    rows, wide = grad.shape
    width = wide // n
    piece = rows // (2 * nz)
    keep = rows_of(grad, core * (rows // 2), rows // 2)
    send = rows_of(grad, (1 - core) * (rows // 2), rows // 2)
    both = (keep.astype(f32) + core_swap(send).astype(f32)).astype(bf16)
    summed = line_scatter(both.reshape(nz, piece, wide))
    out = jnp.zeros((n, piece, width), bf16)
    for k in range(n):
        block = lax.dynamic_slice_in_dim(summed, (me ^ k) * width, width, axis=1)
        if k:
            block = swap(block, "fsdp", k)
        out = lax.dynamic_update_index_in_dim(out, block, me ^ k, 0)
    full = core_halves(line_gather(out))
    return jnp.moveaxis(full, 2, 0).reshape(n * rows, width)


def sum_all(value):
    for axis in ("core", "fsdp", "z"):
        size = lax.axis_size(axis)
        k = 1
        while k < size:
            value = value + swap(value, axis, k)
            k *= 2
    return value


def turn(value, cos_table, sin_table):
    half = HEAD // 2
    turned = jnp.concatenate([-value[..., half:], value[..., :half]], axis=-1)
    return value * cos_table + turned * sin_table


def turn_back(value, cos_table, sin_table):
    half = HEAD // 2
    turned = jnp.concatenate(
        [value[..., half:] * sin_table[..., half:], -value[..., :half] * sin_table[..., :half]],
        axis=-1,
    )
    return value * cos_table + turned


def on_device(
    tokens,
    segments,
    attn_gain,
    w_query,
    w_key,
    w_value,
    query_gain,
    key_gain,
    w_out,
    mlp_gain,
    w_gate,
    w_up,
    w_down,
    cotangent,
):
    n, me = lax.axis_size("fsdp"), lax.axis_index("fsdp")
    tok_rows, width = tokens.shape[1], tokens.shape[2]
    doc_ids = segments[0]
    length = doc_ids.shape[0]
    heads, kv_heads = HEADS // n, KV_HEADS // n
    q_width, kv_width = heads * HEAD, kv_heads * HEAD
    ff = w_gate.shape[1] // n

    index = jnp.arange(length, dtype=jnp.int32)
    earlier = jnp.sum((doc_ids[None, :] < doc_ids[:, None]).astype(jnp.int32), axis=1)
    position = index - earlier
    inverse = rope_base ** (-2.0 * jnp.arange(HEAD // 2).astype(f32) / HEAD)
    angles = position.astype(f32)[:, None] * inverse[None, :]
    angles = jnp.concatenate([angles, angles], axis=-1)
    cos_table, sin_table = jnp.cos(angles)[:, None, :], jnp.sin(angles)[:, None, :]
    allowed = (doc_ids[:, None] == doc_ids[None, :]) & (index[None, :] <= index[:, None])

    sizes = [attn_gain.shape[0], mlp_gain.shape[0], query_gain.shape[0], key_gain.shape[0]]
    packed = jnp.concatenate([attn_gain, mlp_gain, query_gain, key_gain])
    gains = gather_rows(packed[None]).astype(f32)
    ends = [sum(sizes[: j + 1]) for j in range(4)]
    gain_attn = gains[:, : ends[0]].reshape(-1)
    gain_mlp = gains[:, ends[0] : ends[1]].reshape(-1)
    gain_query = gains[:, ends[1] : ends[2]].reshape(-1)
    gain_key = gains[:, ends[2] : ends[3]].reshape(-1)

    full_qkv = spread_rows([w_query, w_key, w_value])
    tokens_all = gather_rows(tokens[0])
    full_out = spread_columns(w_out)
    full_gate_up = spread_rows([w_gate, w_up])
    full_down = spread_columns(w_down)
    cot_all = gather_rows(cotangent[0])

    stream_all = tokens_all.astype(f32)
    normed = (stream_all * rms_scale(stream_all) * gain_attn).astype(bf16)
    qkv = matmul(normed, full_qkv)
    query_raw = qkv[:, :q_width].reshape(length, heads, HEAD)
    key_raw = qkv[:, q_width : q_width + kv_width].reshape(length, kv_heads, HEAD)
    values = qkv[:, q_width + kv_width :].astype(bf16).reshape(length, kv_heads, HEAD)
    query_scale, key_scale = rms_scale(query_raw), rms_scale(key_raw)
    queries = turn(query_raw * query_scale * gain_query, cos_table, sin_table).astype(bf16)
    keys = turn(key_raw * key_scale * gain_key, cos_table, sin_table).astype(bf16)
    grouped = queries.reshape(length, kv_heads, GROUP, HEAD)
    scores = (
        jnp.einsum("qkgd,skd->kgqs", grouped, keys, preferred_element_type=f32) * score_scale
    )
    scores = jnp.where(allowed, scores, masked_score)
    top = jnp.max(scores, axis=-1, keepdims=True)
    shifted = jnp.exp(scores - top)
    denominator = jnp.sum(shifted, axis=-1, keepdims=True)
    log_total = top + jnp.log(denominator)
    probs = (shifted / denominator).astype(bf16)
    attended = jnp.einsum("kgqs,skd->qkgd", probs, values, preferred_element_type=f32)
    attended = attended.reshape(length, q_width).astype(bf16)
    stream = tokens[0].astype(f32)
    middle = stream + scatter_rows(matmul(attended, full_out).astype(bf16))

    mlp_scale = rms_scale(middle)
    normed_mlp = gather_rows((middle * mlp_scale * gain_mlp).astype(bf16))
    gate_up = matmul(normed_mlp, full_gate_up)
    gate, up = gate_up[:, :ff], gate_up[:, ff:]
    sg = 1.0 / (1.0 + jnp.exp(-gate))
    hidden = (gate * sg * up).astype(bf16)
    d_hidden = matmul_nt(cot_all, full_down)
    d_gate = d_hidden * up * sg * (1.0 + gate * (1.0 - sg))
    d_up = d_hidden * gate * sg
    d_gate_up = jnp.concatenate([d_gate.astype(bf16), d_up.astype(bf16)], axis=1)
    d_normed_mlp = scatter_rows(matmul_nt(d_gate_up, full_gate_up).astype(bf16))
    output = (middle + scatter_rows(matmul(hidden, full_down).astype(bf16))).astype(bf16)
    grad_down = reduce_column_grads(matmul_tn(hidden, cot_all).astype(bf16))
    grad_gate_up = reduce_row_grads(matmul_tn(normed_mlp, d_gate_up).astype(bf16))
    d_middle, mlp_gain_rows = norm_back(middle, mlp_scale, gain_mlp, d_normed_mlp)
    d_middle = cotangent[0].astype(f32) + d_middle

    d_branch = gather_rows(d_middle.astype(bf16))
    grad_out = reduce_column_grads(matmul_tn(attended, d_branch).astype(bf16))
    d_attended = matmul_nt(d_branch, full_out).astype(bf16).reshape(length, kv_heads, GROUP, HEAD)
    scores = (
        jnp.einsum("qkgd,skd->kgqs", grouped, keys, preferred_element_type=f32) * score_scale
    )
    again = jnp.where(
        allowed, jnp.exp(jnp.where(allowed, scores, masked_score) - log_total), 0.0
    )
    d_probs = jnp.einsum("qkgd,skd->kgqs", d_attended, values, preferred_element_type=f32)
    row_dots = jnp.sum(again * d_probs, axis=-1, keepdims=True)
    d_scores = (again * (d_probs - row_dots)).astype(bf16)
    probs_again = again.astype(bf16)
    d_queries = (
        jnp.einsum("kgqs,skd->qkgd", d_scores, keys, preferred_element_type=f32) * score_scale
    ).reshape(length, heads, HEAD)
    d_keys = (
        jnp.einsum("kgqs,qkgd->skd", d_scores, grouped, preferred_element_type=f32) * score_scale
    )
    d_values = jnp.einsum("kgqs,qkgd->skd", probs_again, d_attended, preferred_element_type=f32)
    d_query_raw, query_gain_rows = norm_back(
        query_raw, query_scale, gain_query, turn_back(d_queries, cos_table, sin_table)
    )
    d_key_raw, key_gain_rows = norm_back(
        key_raw, key_scale, gain_key, turn_back(d_keys, cos_table, sin_table)
    )
    d_qkv = jnp.concatenate(
        [
            d_query_raw.astype(bf16).reshape(length, q_width),
            d_key_raw.astype(bf16).reshape(length, kv_width),
            d_values.astype(bf16).reshape(length, kv_width),
        ],
        axis=1,
    )
    d_normed = scatter_rows(matmul_nt(d_qkv, full_qkv).astype(bf16))
    grad_qkv = reduce_row_grads(matmul_tn(normed, d_qkv).astype(bf16))
    d_stream, attn_gain_rows = norm_back(stream, rms_scale(stream), gain_attn, d_normed)
    input_grad = d_middle + d_stream

    gain_grads = sum_all(
        jnp.concatenate(
            [
                jnp.sum(attn_gain_rows, axis=0),
                jnp.sum(mlp_gain_rows, axis=0),
                jnp.sum(query_gain_rows, axis=(0, 1)),
                jnp.sum(key_gain_rows, axis=(0, 1)),
            ]
        )
    )
    shares, start = [], 0
    for size in sizes:
        shares.append(rows_of(gain_grads, start + me * size, size))
        start += n * size

    rows = width // n
    return (
        output[None],
        input_grad[None],
        shares[0],
        grad_qkv[:, :, :q_width].reshape(rows, n * q_width),
        grad_qkv[:, :, q_width : q_width + kv_width].reshape(rows, n * kv_width),
        grad_qkv[:, :, q_width + kv_width :].reshape(rows, n * kv_width),
        shares[2],
        shares[3],
        grad_out,
        shares[1],
        grad_gate_up[:, :, :ff].reshape(rows, n * ff),
        grad_gate_up[:, :, ff:].reshape(rows, n * ff),
        grad_down,
    )


def solution(mesh):
    n, replicas = mesh.shape["fsdp"], mesh.shape["dp"]
    split = Mesh(mesh.devices.reshape(n, replicas // 2, 2), ("fsdp", "z", "core"))
    dp = ("z", "core")
    in_specs = (
        P(dp, "fsdp", None),
        P(dp, None),
        P("fsdp"),
        P("fsdp", None),
        P("fsdp", None),
        P("fsdp", None),
        P("fsdp"),
        P("fsdp"),
        P(None, "fsdp"),
        P("fsdp"),
        P("fsdp", None),
        P("fsdp", None),
        P(None, "fsdp"),
        P(dp, "fsdp", None),
    )
    out_specs = (
        P(dp, "fsdp", None),
        P(dp, "fsdp", None),
        P("fsdp"),
        P("fsdp", None),
        P("fsdp", None),
        P("fsdp", None),
        P("fsdp"),
        P("fsdp"),
        P(None, "fsdp"),
        P("fsdp"),
        P("fsdp", None),
        P("fsdp", None),
        P(None, "fsdp"),
    )
    return jax.shard_map(
        on_device, mesh=split, in_specs=in_specs, out_specs=out_specs, check_vma=False
    )
```

```python
import math

import jax
import jax.numpy as jnp
from jax import lax
from jax.experimental import pallas as pl
from jax.experimental.pallas import tpu as pltpu
from jax.sharding import Mesh
from jax.sharding import PartitionSpec as P

HEADS = 16
KV_HEADS = 8
HEAD = 128
GROUP = HEADS // KV_HEADS

epsilon = 1e-06
rope_base = 1000000.0
masked_score = -1e30
score_scale = 1.0 / math.sqrt(HEAD)

bf16 = jnp.bfloat16
f32 = jnp.float32


def matmul(first, second):
    return jnp.dot(first, second, preferred_element_type=f32)


def matmul_tn(first, second):
    return lax.dot_general(first, second, (((0,), (0,)), ((), ())), preferred_element_type=f32)


def matmul_nt(first, second):
    return lax.dot_general(first, second, (((1,), (1,)), ((), ())), preferred_element_type=f32)


def rms_scale(vector):
    return lax.rsqrt(jnp.mean(vector * vector, axis=-1, keepdims=True) + epsilon)


def norm_back(vector, scale, gain, incoming):
    scaled = gain * incoming
    d_vector = scale * scaled - vector * (scale**3) * jnp.mean(
        vector * scaled, axis=-1, keepdims=True
    )
    return d_vector, incoming * vector * scale


def swap(value, axis, k):
    return lax.ppermute(value, axis, [(j, j ^ k) for j in range(lax.axis_size(axis))])


def core_swap(value):
    return swap(value, "core", 1)


def rows_of(value, start, size):
    return lax.dynamic_slice_in_dim(value, start, size, axis=0)


def fence(*trees):
    leaves, shape = jax.tree.flatten(trees)
    return jax.tree.unflatten(shape, lax.optimization_barrier(leaves))


def gather_begin(shard):
    n = lax.axis_size("fsdp")
    if n == 4:
        return [swap(shard, "fsdp", 1), swap(shard, "fsdp", 2)]
    return [swap(shard, "fsdp", k) for k in range(1, n)]


def gather_end(shard, begun):
    if lax.axis_size("fsdp") != 4:
        return [shard] + begun
    half = shard.shape[0] // 2
    first = swap(begun[0][:half], "fsdp", 2)
    second = swap(begun[1][half:], "fsdp", 1)
    return [shard] + begun + [jnp.concatenate([first, second], axis=0)]


def scatter_begin(far):
    n = lax.axis_size("fsdp")
    if n == 4:
        half = far.shape[0] // 2
        return [swap(far[:half], "fsdp", 1), swap(far[half:], "fsdp", 2)]
    return [swap(far, "fsdp", n - 1)]


def scatter_middle(near, begun):
    n = lax.axis_size("fsdp")
    if n != 4:
        return begun + [swap(block, "fsdp", k + 1) for k, block in enumerate(near)]
    near_x, near_y = near
    first, second = begun
    half = first.shape[0]
    low = (near_x[half:].astype(f32) + second.astype(f32)).astype(bf16)
    top = (near_y[:half].astype(f32) + first.astype(f32)).astype(bf16)
    return [
        swap(jnp.concatenate([near_x[:half], low], axis=0), "fsdp", 1),
        swap(jnp.concatenate([top, near_y[half:]], axis=0), "fsdp", 2),
    ]


def scatter_end(own, got):
    total = own.astype(f32)
    for block in got:
        total = total + block.astype(f32)
    return total


def assemble(shape, pieces, places):
    count = len(pieces)

    def kernel(place_ref, *refs):
        ins, out, hold = refs[:count], refs[count], refs[count + 1]
        sem_in, sem_out = refs[count + 2], refs[count + 3]

        def window(ref, k):
            row = pl.multiple_of(place_ref[2 * k], 16)
            column = pl.multiple_of(place_ref[2 * k + 1], 128)
            rows, columns = ins[k].shape
            return ref.at[pl.ds(row, rows), pl.ds(column, columns)]

        loads = [
            pltpu.make_async_copy(ins[k], window(hold, k), sem_in.at[k]) for k in range(count)
        ]
        stores = [
            pltpu.make_async_copy(window(hold, k), window(out, k), sem_out.at[k])
            for k in range(count)
        ]
        for load in loads:
            load.start()
        for load, store in zip(loads, stores):
            load.wait()
            store.start()
        for store in stores:
            store.wait()

    size = 2 * math.prod(shape)
    return pl.pallas_call(
        kernel,
        out_shape=jax.ShapeDtypeStruct(shape, bf16),
        in_specs=[pl.BlockSpec(memory_space=pltpu.SMEM)]
        + [pl.BlockSpec(memory_space=pl.ANY)] * count,
        out_specs=pl.BlockSpec(memory_space=pl.ANY),
        scratch_shapes=[
            pltpu.VMEM(shape, bf16),
            pltpu.SemaphoreType.DMA((count,)),
            pltpu.SemaphoreType.DMA((count,)),
        ],
        compiler_params=pltpu.CompilerParams(vmem_limit_bytes=size + (4 << 20)),
        cost_estimate=pl.CostEstimate(flops=0, bytes_accessed=2 * size, transcendentals=0),
        name="assemble",
    )(jnp.stack([jnp.int32(v) for place in places for v in place]), *pieces)


def spread_begin(quarter_of):
    n, me = lax.axis_size("fsdp"), lax.axis_index("fsdp")
    mine = 2 * (lax.axis_index("z") % 2) + lax.axis_index("core")
    return [swap(quarter_of(me ^ k, mine), "fsdp", k) for k in range(1, n)]


def spread_pieces(got, along, across, across_along):
    n, me = lax.axis_size("fsdp"), lax.axis_index("fsdp")
    side, core = lax.axis_index("z") % 2, lax.axis_index("core")
    pieces = []
    for k in range(1, n):
        for block, quarter in (
            (got, 2 * side + core),
            (along, 2 * (1 - side) + core),
            (across, 2 * side + 1 - core),
            (across_along, 2 * (1 - side) + 1 - core),
        ):
            pieces.append((me ^ k, quarter, block[k - 1]))
    return pieces


class RowKind:
    def __init__(self, *parts):
        self.parts = parts

    def cut(self, start, size, block):
        n = lax.axis_size("fsdp")
        widths = [part.shape[1] // n for part in self.parts]
        return jnp.concatenate(
            [
                lax.dynamic_slice(part, (start, block * width), (size, width))
                for part, width in zip(self.parts, widths)
            ],
            axis=1,
        )

    def quarter(self, j, q):
        size = self.parts[0].shape[0] // 4
        return self.cut(q * size, size, j)

    def join(self, pieces):
        n, me = lax.axis_size("fsdp"), lax.axis_index("fsdp")
        rows = self.parts[0].shape[0]
        width = sum(part.shape[1] for part in self.parts) // n
        return assemble(
            (n * rows, width),
            [self.cut(0, rows, me)] + [block for _, _, block in pieces],
            [(me * rows, 0)] + [(j * rows + q * (rows // 4), 0) for j, q, _ in pieces],
        )


class ColumnKind:
    def __init__(self, part):
        self.part = part

    def quarter(self, j, q):
        rows = self.part.shape[0] // lax.axis_size("fsdp")
        return rows_of(self.part, j * rows + q * (rows // 4), rows // 4)

    def join(self, pieces):
        n, me = lax.axis_size("fsdp"), lax.axis_index("fsdp")
        rows, width = self.part.shape[0] // n, self.part.shape[1]
        return assemble(
            (rows, n * width),
            [rows_of(self.part, me * rows, rows)] + [block for _, _, block in pieces],
            [(0, me * width)] + [(q * (rows // 4), j * width) for j, q, _ in pieces],
        )


def stack_along(got):
    return swap(got, "z", 1)


class Reduction:
    def __init__(self, grad):
        self.grad = grad
        self.other = None

    def take(self, c):
        n, me = lax.axis_size("fsdp"), lax.axis_index("fsdp")
        rows, width = self.grad.shape[1:]
        return jnp.concatenate(
            [
                lax.dynamic_slice(
                    self.grad, (me ^ k, c * (rows // 2), 0), (1, rows // 2, width)
                )
                for k in range(n)
            ]
        )

    def begin(self):
        core = lax.axis_index("core")
        both = self.take(core).astype(f32) + core_swap(self.take(1 - core)).astype(f32)
        self.half = both.astype(bf16)

    def exchange(self):
        n = lax.axis_size("fsdp")
        self.half = jnp.stack(
            [self.half[0]] + [swap(self.half[k], "fsdp", k) for k in range(1, n)]
        )

    def finish(self, by_rows, start=0, size=None):
        n, me = lax.axis_size("fsdp"), lax.axis_index("fsdp")
        core = lax.axis_index("core")
        if self.other is None:
            self.other = core_swap(self.half)
        rows, width = self.half.shape[1:]
        size = width if size is None else size
        column = start // size

        def kernel(place, mine, other, out):
            @pl.when(pl.program_id(0) == 0)
            def _():
                out[...] = mine[0].astype(f32)

            @pl.when(pl.program_id(0) == 1)
            def _():
                out[...] = other[0].astype(f32)

        def mine_at(w, k, place):
            return (jnp.where(w == 0, k, n - 1), 0, column)

        def other_at(w, k, place):
            return (jnp.where(w == 0, 0, k), 0, column)

        def out_at(w, k, place):
            source = place[0] ^ k
            side = jnp.where(w == 0, place[1], 1 - place[1])
            return (side, source) if by_rows else (source * 2 + side, 0)

        return pl.pallas_call(
            kernel,
            out_shape=jax.ShapeDtypeStruct(
                (2 * rows, n * size) if by_rows else (2 * n * rows, size), f32
            ),
            grid_spec=pltpu.PrefetchScalarGridSpec(
                num_scalar_prefetch=1,
                grid=(2, n),
                in_specs=[
                    pl.BlockSpec((1, rows, size), mine_at),
                    pl.BlockSpec((1, rows, size), other_at),
                ],
                out_specs=pl.BlockSpec((rows, size), out_at),
            ),
            compiler_params=pltpu.CompilerParams(vmem_limit_bytes=32 << 20),
            cost_estimate=pl.CostEstimate(
                flops=0, bytes_accessed=2 * n * rows * size * 40, transcendentals=0
            ),
            name="place",
        )(jnp.stack([me, core]).astype(jnp.int32), self.half, self.other)


def turn(value, cos_table, sin_table):
    half = HEAD // 2
    turned = jnp.concatenate([-value[..., half:], value[..., :half]], axis=-1)
    return value * cos_table + turned * sin_table


def turn_back(value, cos_table, sin_table):
    half = HEAD // 2
    turned = jnp.concatenate(
        [value[..., half:] * sin_table[..., half:], -value[..., :half] * sin_table[..., :half]],
        axis=-1,
    )
    return value * cos_table + turned


def attention_forward(queries, keys, values, allowed):
    length, heads = queries.shape[:2]
    grouped = queries.reshape(length, heads // GROUP, GROUP, HEAD)
    scores = (
        jnp.einsum("qkgd,skd->kgqs", grouped, keys, preferred_element_type=f32) * score_scale
    )
    scores = jnp.where(allowed, scores, masked_score)
    top = jnp.max(scores, axis=-1, keepdims=True)
    shifted = jnp.exp(scores - top)
    denominator = jnp.sum(shifted, axis=-1, keepdims=True)
    log_total = top + jnp.log(denominator)
    probs = (shifted / denominator).astype(bf16)
    attended = jnp.einsum("kgqs,skd->qkgd", probs, values, preferred_element_type=f32)
    return attended.reshape(length, heads * HEAD).astype(bf16), log_total


def attention_backward(queries, keys, values, allowed, log_total, d_attended):
    length, heads = queries.shape[:2]
    grouped = queries.reshape(length, heads // GROUP, GROUP, HEAD)
    d_attended = d_attended.reshape(length, heads // GROUP, GROUP, HEAD)
    scores = (
        jnp.einsum("qkgd,skd->kgqs", grouped, keys, preferred_element_type=f32) * score_scale
    )
    again = jnp.where(
        allowed, jnp.exp(jnp.where(allowed, scores, masked_score) - log_total), 0.0
    )
    d_probs = jnp.einsum("qkgd,skd->kgqs", d_attended, values, preferred_element_type=f32)
    row_dots = jnp.sum(again * d_probs, axis=-1, keepdims=True)
    d_scores = (again * (d_probs - row_dots)).astype(bf16)
    probs_again = again.astype(bf16)
    d_queries = (
        jnp.einsum("kgqs,skd->qkgd", d_scores, keys, preferred_element_type=f32) * score_scale
    ).reshape(length, heads, HEAD)
    d_keys = (
        jnp.einsum("kgqs,qkgd->skd", d_scores, grouped, preferred_element_type=f32) * score_scale
    )
    d_values = jnp.einsum("kgqs,qkgd->skd", probs_again, d_attended, preferred_element_type=f32)
    return d_queries, d_keys, d_values


def on_device(
    tokens,
    segments,
    attn_gain,
    w_query,
    w_key,
    w_value,
    query_gain,
    key_gain,
    w_out,
    mlp_gain,
    w_gate,
    w_up,
    w_down,
    cotangent,
):
    n, me = lax.axis_size("fsdp"), lax.axis_index("fsdp")
    tok_rows, width = tokens.shape[1], tokens.shape[2]
    length = segments.shape[1]
    heads, kv_heads = HEADS // n, KV_HEADS // n
    q_width, kv_width = heads * HEAD, kv_heads * HEAD
    ff = w_gate.shape[1] // n
    rows = width // n

    def block(value, k):
        return value[k * tok_rows : (k + 1) * tok_rows]

    def by_columns(first, second):
        columns = second.shape[1] // n
        return jnp.stack(
            [
                matmul_tn(first, second[:, j * columns : (j + 1) * columns]).astype(bf16)
                for j in range(n)
            ]
        )

    def by_rows(first, second):
        return matmul_tn(first, second).astype(bf16).reshape(n, rows, second.shape[1])

    qkv_kind, out_kind = RowKind(w_query, w_key, w_value), ColumnKind(w_out)
    gu_kind, down_kind = RowKind(w_gate, w_up), ColumnKind(w_down)

    sizes = [attn_gain.shape[0], mlp_gain.shape[0], query_gain.shape[0], key_gain.shape[0]]
    packed = jnp.concatenate([attn_gain, mlp_gain, query_gain, key_gain])[None]
    gains = [packed] + [swap(packed, "fsdp", k) for k in range(1, n)]
    tok = gather_begin(tokens[0])
    qkv_got = spread_begin(qkv_kind.quarter)
    index = jnp.concatenate(
        [(me ^ k) * tok_rows + jnp.arange(tok_rows, dtype=jnp.int32) for k in range(n)]
    )
    doc_ids = jnp.concatenate(
        [rows_of(segments[0], (me ^ k) * tok_rows, tok_rows) for k in range(n)]
    )
    earlier = jnp.sum((doc_ids[None, :] < doc_ids[:, None]).astype(jnp.int32), axis=1)
    position = index - earlier
    inverse = rope_base ** (-2.0 * jnp.arange(HEAD // 2).astype(f32) / HEAD)
    angles = position.astype(f32)[:, None] * inverse[None, :]
    angles = jnp.concatenate([angles, angles], axis=-1)
    cos_table, sin_table = jnp.cos(angles)[:, None, :], jnp.sin(angles)[:, None, :]
    allowed = (doc_ids[:, None] == doc_ids[None, :]) & (index[None, :] <= index[:, None])
    gains = jnp.concatenate(gains, axis=0)
    gains = jnp.concatenate(
        [lax.dynamic_slice_in_dim(gains, me ^ j, 1, axis=0) for j in range(n)], axis=0
    ).astype(f32)
    ends = [sum(sizes[: j + 1]) for j in range(4)]
    gain_attn = gains[:, : ends[0]].reshape(-1)
    gain_mlp = gains[:, ends[0] : ends[1]].reshape(-1)
    gain_query = gains[:, ends[1] : ends[2]].reshape(-1)
    gain_key = gains[:, ends[2] : ends[3]].reshape(-1)
    qkv_got = jnp.stack(qkv_got)
    tok, qkv_got, (cos_table, sin_table, allowed), (w_out, w_gate, w_up, w_down, cotangent) = fence(
        tok,
        qkv_got,
        (cos_table, sin_table, allowed),
        (w_out, w_gate, w_up, w_down, cotangent),
    )
    out_kind = ColumnKind(w_out)
    gu_kind, down_kind = RowKind(w_gate, w_up), ColumnKind(w_down)

    tok = gather_end(tokens[0], tok)
    qkv_along, qkv_across = stack_along(qkv_got), core_swap(qkv_got)
    out_got = spread_begin(out_kind.quarter)
    tok, qkv_along, qkv_across, w_gate, w_up = fence(tok, qkv_along, qkv_across, w_gate, w_up)
    gu_kind = RowKind(w_gate, w_up)

    qkv_across_along = core_swap(qkv_along)
    gu_got = spread_begin(gu_kind.quarter)
    tokens_all = jnp.concatenate(tok, axis=0)
    stream_all = tokens_all.astype(f32)
    normed = (stream_all * rms_scale(stream_all) * gain_attn).astype(bf16)
    out_got = jnp.stack(out_got)
    out_along, out_across = stack_along(out_got), core_swap(out_got)
    full_qkv = qkv_kind.join(spread_pieces(qkv_got, qkv_along, qkv_across, qkv_across_along))
    qkv = matmul(normed, full_qkv)
    query_raw = qkv[:, :q_width].reshape(length, heads, HEAD)
    key_raw = qkv[:, q_width : q_width + kv_width].reshape(length, kv_heads, HEAD)
    values = qkv[:, q_width + kv_width :].astype(bf16).reshape(length, kv_heads, HEAD)
    query_scale, key_scale = rms_scale(query_raw), rms_scale(key_raw)
    queries = turn(query_raw * query_scale * gain_query, cos_table, sin_table).astype(bf16)
    keys = turn(key_raw * key_scale * gain_key, cos_table, sin_table).astype(bf16)
    attended, log_total = attention_forward(queries, keys, values, allowed)
    out_across_along = core_swap(out_along)
    full_out = out_kind.join(spread_pieces(out_got, out_along, out_across, out_across_along))
    gu_got = jnp.stack(gu_got)
    attended, full_out, gu_got, w_down = fence(attended, full_out, gu_got, w_down)
    down_kind = ColumnKind(w_down)

    gu_along, gu_across = stack_along(gu_got), core_swap(gu_got)
    parts = [matmul(block(attended, n - 1), full_out).astype(bf16)]
    begun = scatter_begin(parts[0])
    parts = [matmul(block(attended, k), full_out).astype(bf16) for k in range(n - 1)] + parts
    begun, parts, gu_across = fence(begun, parts, gu_across)

    stream = tokens[0].astype(f32)
    middle = stream + scatter_end(parts[0], scatter_middle(parts[1 : n - 1], begun))
    mlp_scale = rms_scale(middle)
    normed_mine = (middle * mlp_scale * gain_mlp).astype(bf16)
    middle, mlp_scale, normed_mine, gu_along, w_down = fence(
        middle, mlp_scale, normed_mine, gu_along, w_down
    )
    down_kind = ColumnKind(w_down)

    begun = gather_begin(normed_mine)
    gu_across_along = core_swap(gu_along)
    full_gu = gu_kind.join(spread_pieces(gu_got, gu_along, gu_across, gu_across_along))
    begun, full_gu, w_down, cotangent = fence(begun, full_gu, w_down, cotangent)
    down_kind = ColumnKind(w_down)

    normed_parts = gather_end(normed_mine, begun)
    gate_up_parts = [matmul(part, full_gu) for part in normed_parts[: n - 1]]
    normed_parts, gate_up_parts, w_down, cotangent = fence(
        normed_parts, gate_up_parts, w_down, cotangent
    )
    down_kind = ColumnKind(w_down)

    cot = cotangent[0]
    down_got = spread_begin(down_kind.quarter)
    cot_begun = gather_begin(cot)
    gate_up = jnp.concatenate(gate_up_parts + [matmul(normed_parts[n - 1], full_gu)], axis=0)
    normed_mlp = jnp.concatenate(normed_parts, axis=0)
    gate, up = gate_up[:, :ff], gate_up[:, ff:]
    sg = 1.0 / (1.0 + jnp.exp(-gate))
    hidden = (gate * sg * up).astype(bf16)
    down_got = jnp.stack(down_got)
    down_got, cot_begun, gate_up, hidden, normed_mlp = fence(
        down_got, cot_begun, gate_up, hidden, normed_mlp
    )

    cot_all = jnp.concatenate(gather_end(cot, cot_begun), axis=0)
    down_along, down_across = stack_along(down_got), core_swap(down_got)
    down_across_along = core_swap(down_along)
    full_down = down_kind.join(
        spread_pieces(down_got, down_along, down_across, down_across_along)
    )
    cot_all, full_down, hidden, gate_up = fence(cot_all, full_down, hidden, gate_up)

    gate, up = gate_up[:, :ff], gate_up[:, ff:]
    sg = 1.0 / (1.0 + jnp.exp(-gate))
    d_hidden = matmul_nt(cot_all, full_down)
    d_gate = (d_hidden * up * sg * (1.0 + gate * (1.0 - sg))).astype(bf16)
    d_up = (d_hidden * gate * sg).astype(bf16)
    d_gate_up = jnp.concatenate([d_gate, d_up], axis=1)
    down = Reduction(by_columns(hidden, cot_all))
    down.begin()
    down.half, d_gate_up, hidden = fence(down.half, d_gate_up, hidden)

    down.half = lax.psum(down.half, "z")
    begun = scatter_begin(matmul_nt(block(d_gate_up, n - 1), full_gu).astype(bf16))
    parts = [matmul_nt(block(d_gate_up, k), full_gu).astype(bf16) for k in range(n - 1)]
    d_normed_mlp = scatter_end(parts[0], scatter_middle(parts[1:], begun))
    d_middle, mlp_gain_rows = norm_back(middle, mlp_scale, gain_mlp, d_normed_mlp)
    mlp_gain_grad = jnp.sum(mlp_gain_rows, axis=0)
    d_middle = cot.astype(f32) + d_middle
    d_mine = d_middle.astype(bf16)
    gate_sum = Reduction(by_rows(normed_mlp, d_gate_up[:, :ff]))
    gate_sum.begin()
    up_sum = Reduction(by_rows(normed_mlp, d_gate_up[:, ff:]))
    out_parts = [matmul(block(hidden, k), full_down).astype(bf16) for k in range(n)]
    down.half, d_middle, d_mine, mlp_gain_grad, gate_sum.half, up_sum.grad, out_parts = fence(
        down.half, d_middle, d_mine, mlp_gain_grad, gate_sum.half, up_sum.grad, out_parts
    )

    gate_sum.half = lax.psum(gate_sum.half, "z")
    d_branch = jnp.concatenate(gather_end(d_mine, gather_begin(d_mine)), axis=0)
    d_attended = matmul_nt(d_branch, full_out).astype(bf16)
    up_sum.begin()
    down.exchange()
    down_full = down.finish(False)
    gate_sum.half, d_branch, d_attended, up_sum.half, down_full, out_parts = fence(
        gate_sum.half, d_branch, d_attended, up_sum.half, down_full, out_parts
    )

    up_sum.half = lax.psum(up_sum.half, "z")
    d_queries, d_keys, d_values = attention_backward(
        queries, keys, values, allowed, log_total, d_attended
    )
    d_query_raw, query_gain_rows = norm_back(
        query_raw, query_scale, gain_query, turn_back(d_queries, cos_table, sin_table)
    )
    d_key_raw, key_gain_rows = norm_back(
        key_raw, key_scale, gain_key, turn_back(d_keys, cos_table, sin_table)
    )
    head_gain_grads = [
        jnp.sum(query_gain_rows, axis=(0, 1)),
        jnp.sum(key_gain_rows, axis=(0, 1)),
    ]
    d_qkv = jnp.concatenate(
        [
            d_query_raw.astype(bf16).reshape(length, q_width),
            d_key_raw.astype(bf16).reshape(length, kv_width),
            d_values.astype(bf16).reshape(length, kv_width),
        ],
        axis=1,
    )
    out_got = scatter_middle(out_parts[1 : n - 1], scatter_begin(out_parts[n - 1]))
    output = (middle + scatter_end(out_parts[0], out_got)).astype(bf16)
    gate_sum.exchange()
    gate_full = gate_sum.finish(True)
    out_sum = Reduction(by_columns(attended, d_branch))
    out_sum.begin()
    out_sum.exchange()
    qkv_sum = Reduction(by_rows(normed, d_qkv))
    qkv_sum.begin()
    qkv_sum.exchange()
    up_sum.half, d_qkv, head_gain_grads, out_sum.half, qkv_sum.half, output, gate_full = fence(
        up_sum.half, d_qkv, head_gain_grads, out_sum.half, qkv_sum.half, output, gate_full
    )

    qkv_sum.half, out_sum.half = lax.psum((qkv_sum.half, out_sum.half), "z")
    begun = scatter_begin(matmul_nt(block(d_qkv, n - 1), full_qkv).astype(bf16))
    parts = [matmul_nt(block(d_qkv, k), full_qkv).astype(bf16) for k in range(n - 1)]
    d_normed = scatter_end(parts[0], scatter_middle(parts[1:], begun))
    d_stream, attn_gain_rows = norm_back(stream, rms_scale(stream), gain_attn, d_normed)
    input_grad = d_middle + d_stream
    gain_grads = jnp.concatenate(
        [jnp.sum(attn_gain_rows, axis=0), mlp_gain_grad] + head_gain_grads
    )
    for axis in ("core", "fsdp", "z"):
        k = 1
        while k < lax.axis_size(axis):
            gain_grads = gain_grads + swap(gain_grads, axis, k)
            k *= 2
    shares, start = [], 0
    for size in sizes:
        shares.append(rows_of(gain_grads, start + me * size, size))
        start += n * size
    up_sum.exchange()
    shares, input_grad, up_full, qkv_sum.half, out_sum.half = fence(
        shares, input_grad, up_sum.finish(True), qkv_sum.half, out_sum.half
    )
    return (
        output[None],
        input_grad[None],
        shares[0],
        qkv_sum.finish(True, 0, q_width),
        qkv_sum.finish(True, q_width, kv_width),
        qkv_sum.finish(True, q_width + kv_width, kv_width),
        shares[2],
        shares[3],
        out_sum.finish(False),
        shares[1],
        gate_full,
        up_full,
        down_full,
    )


def solution(mesh):
    n, replicas = mesh.shape["fsdp"], mesh.shape["dp"]
    split = Mesh(mesh.devices.reshape(n, replicas // 2, 2), ("fsdp", "z", "core"))
    dp = ("z", "core")
    in_specs = (
        P(dp, "fsdp", None),
        P(dp, None),
        P("fsdp"),
        P("fsdp", None),
        P("fsdp", None),
        P("fsdp", None),
        P("fsdp"),
        P("fsdp"),
        P(None, "fsdp"),
        P("fsdp"),
        P("fsdp", None),
        P("fsdp", None),
        P(None, "fsdp"),
        P(dp, "fsdp", None),
    )
    out_specs = (
        P(dp, "fsdp", None),
        P(dp, "fsdp", None),
        P("fsdp"),
        P("fsdp", None),
        P("fsdp", None),
        P("fsdp", None),
        P("fsdp"),
        P("fsdp"),
        P(None, "fsdp"),
        P("fsdp"),
        P("fsdp", None),
        P("fsdp", None),
        P(None, "fsdp"),
    )
    return jax.shard_map(
        on_device, mesh=split, in_specs=in_specs, out_specs=out_specs, check_vma=False
    )
```

```python
import math

import jax
import jax.numpy as jnp
from jax import lax
from jax.experimental import pallas as pl
from jax.experimental.layout import Layout, with_layout_constraint
from jax.experimental.pallas import tpu as pltpu
from jax.sharding import Mesh
from jax.sharding import PartitionSpec as P

HEADS = 16
KV_HEADS = 8
HEAD = 128
GROUP = HEADS // KV_HEADS

epsilon = 1e-06
rope_base = 1000000.0
masked_score = -1e30
score_scale = 1.0 / math.sqrt(HEAD)

bf16 = jnp.bfloat16
f32 = jnp.float32


def matmul(first, second):
    return jnp.dot(first, second, preferred_element_type=f32)


def matmul_tn(first, second):
    return lax.dot_general(first, second, (((0,), (0,)), ((), ())), preferred_element_type=f32)


def matmul_nt(first, second):
    return lax.dot_general(first, second, (((1,), (1,)), ((), ())), preferred_element_type=f32)


def rms_scale(vector):
    return lax.rsqrt(jnp.mean(vector * vector, axis=-1, keepdims=True) + epsilon)


def norm_back(vector, scale, gain, incoming):
    scaled = gain * incoming
    d_vector = scale * scaled - vector * (scale**3) * jnp.mean(
        vector * scaled, axis=-1, keepdims=True
    )
    return d_vector, incoming * vector * scale


def swap(value, axis, k):
    return lax.ppermute(value, axis, [(j, j ^ k) for j in range(lax.axis_size(axis))])


def core_swap(value):
    return swap(value, "core", 1)


def rows_of(value, start, size):
    return lax.dynamic_slice_in_dim(value, start, size, axis=0)


def fence(*trees):
    leaves, shape = jax.tree.flatten(trees)
    return jax.tree.unflatten(shape, lax.optimization_barrier(leaves))


def block_of_work(whole, body):
    shapes = jax.eval_shape(body)
    return lax.cond(
        whole,
        body,
        lambda: jax.tree.map(lambda leaf: jnp.zeros(leaf.shape, leaf.dtype), shapes),
    )


def gather_begin(shard):
    n = lax.axis_size("fsdp")
    if n == 4:
        return [swap(shard, "fsdp", 1), swap(shard, "fsdp", 2)]
    return [swap(shard, "fsdp", k) for k in range(1, n)]


def gather_end(shard, begun):
    if lax.axis_size("fsdp") != 4:
        return [shard] + begun
    half = shard.shape[0] // 2
    first = swap(begun[0][:half], "fsdp", 2)
    second = swap(begun[1][half:], "fsdp", 1)
    return [shard] + begun + [jnp.concatenate([first, second], axis=0)]


def scatter_begin(far):
    n = lax.axis_size("fsdp")
    if n == 4:
        half = far.shape[0] // 2
        return [swap(far[:half], "fsdp", 1), swap(far[half:], "fsdp", 2)]
    return [swap(far, "fsdp", n - 1)]


def scatter_middle(near, begun):
    n = lax.axis_size("fsdp")
    if n != 4:
        return begun + [swap(block, "fsdp", k + 1) for k, block in enumerate(near)]
    near_x, near_y = near
    first, second = begun
    half = first.shape[0]
    low = (near_x[half:].astype(f32) + second.astype(f32)).astype(bf16)
    top = (near_y[:half].astype(f32) + first.astype(f32)).astype(bf16)
    return [
        swap(jnp.concatenate([near_x[:half], low], axis=0), "fsdp", 1),
        swap(jnp.concatenate([top, near_y[half:]], axis=0), "fsdp", 2),
    ]


def scatter_end(own, got):
    total = own.astype(f32)
    for block in got:
        total = total + block.astype(f32)
    return total


def gather_direct(shard):
    n = lax.axis_size("fsdp")
    return [shard] + [swap(shard, "fsdp", k) for k in range(1, n)]


def scatter_direct(block_of):
    n = lax.axis_size("fsdp")
    got = {k: swap(block_of(k), "fsdp", k) for k in range(n - 1, 0, -1)}
    return [block_of(0)] + [got[k] for k in range(1, n)]


def add_up(blocks):
    return scatter_end(blocks[0], blocks[1:])


def assemble(shape, sources, pieces):
    count, held = len(pieces), len(sources)

    def kernel(place_ref, *refs):
        ins, out, hold = refs[:held], refs[held], refs[held + 1]
        sem_in, sem_out = refs[held + 2], refs[held + 3]

        def window(ref, k, first):
            size = pieces[k][2]
            row = pl.multiple_of(place_ref[4 * k + first], 16)
            column = pl.multiple_of(place_ref[4 * k + first + 1], 128)
            return ref.at[pl.ds(row, size[0]), pl.ds(column, size[1])]

        def source(k):
            ref, lead = ins[pieces[k][0]], pieces[k][1]
            return window(ref if lead is None else ref.at[lead], k, 0)

        loads = [
            pltpu.make_async_copy(source(k), window(hold, k, 2), sem_in.at[k])
            for k in range(count)
        ]
        stores = [
            pltpu.make_async_copy(window(hold, k, 2), window(out, k, 2), sem_out.at[k])
            for k in range(count)
        ]
        for load in loads:
            load.start()
        for load, store in zip(loads, stores):
            load.wait()
            store.start()
        for store in stores:
            store.wait()

    size = 2 * math.prod(shape)
    places = [jnp.int32(v) for piece in pieces for at in piece[3:] for v in at]
    return pl.pallas_call(
        kernel,
        out_shape=jax.ShapeDtypeStruct(shape, bf16),
        in_specs=[pl.BlockSpec(memory_space=pltpu.SMEM)]
        + [
            pl.BlockSpec(memory_space=pl.ANY if source.ndim == 3 else pltpu.HBM)
            for source in sources
        ],
        out_specs=pl.BlockSpec(memory_space=pl.ANY),
        scratch_shapes=[
            pltpu.VMEM(shape, bf16),
            pltpu.SemaphoreType.DMA((count,)),
            pltpu.SemaphoreType.DMA((count,)),
        ],
        compiler_params=pltpu.CompilerParams(vmem_limit_bytes=size + (4 << 20)),
        cost_estimate=pl.CostEstimate(flops=0, bytes_accessed=2 * size, transcendentals=0),
        name="assemble",
    )(jnp.stack(places), *sources)


class Spread:
    def __init__(self, by_rows, by_columns, along_z=True):
        self.by_rows, self.by_columns, self.along_z = by_rows, by_columns, along_z
        self.shares = 4 if along_z else 2

    def share(self, j, q):
        n = lax.axis_size("fsdp")
        cuts = []
        for part in self.by_rows:
            size, width = part.shape[0] // self.shares, part.shape[1] // n
            cuts.append(lax.dynamic_slice(part, (q * size, j * width), (size, width)))
        for part in self.by_columns:
            rows = part.shape[0] // n
            size = rows // self.shares
            cuts.append(rows_of(part, j * rows + q * size, size))
        return cuts[0] if len(cuts) == 1 else jnp.concatenate(cuts, axis=1)

    def begin(self):
        n, me = lax.axis_size("fsdp"), lax.axis_index("fsdp")
        mine = lax.axis_index("core")
        if self.along_z:
            mine = 2 * (lax.axis_index("z") % 2) + mine
        return [swap(self.share(me ^ k, mine), "fsdp", k) for k in range(1, n)]

    def pieces(self, sources):
        n, me = lax.axis_size("fsdp"), lax.axis_index("fsdp")
        side, core = lax.axis_index("z") % 2, lax.axis_index("core")
        shares = [core, 1 - core]
        if self.along_z:
            shares = [
                2 * side + core,
                2 * (1 - side) + core,
                2 * side + 1 - core,
                2 * (1 - side) + 1 - core,
            ]
        return [
            (source, k, me ^ k, shares[source])
            for k in range(1, n)
            for source in range(len(sources))
        ]

    def join_rows(self, sources):
        n, me = lax.axis_size("fsdp"), lax.axis_index("fsdp")
        rows = self.by_rows[0].shape[0]
        widths = [part.shape[1] // n for part in self.by_rows]
        total, size = sum(widths), rows // self.shares
        pieces = [
            (source, k - 1, (size, total), (0, 0), (j * rows + q * size, 0))
            for source, k, j, q in self.pieces(sources)
        ]
        start = 0
        for index, width in enumerate(widths):
            pieces.append(
                (len(sources) + index, None, (rows, width), (0, me * width), (me * rows, start))
            )
            start += width
        return assemble((n * rows, total), [*sources, *self.by_rows], pieces)

    def join_columns(self, sources):
        n, me = lax.axis_size("fsdp"), lax.axis_index("fsdp")
        start = sum(part.shape[1] // n for part in self.by_rows)
        (part,) = self.by_columns
        rows, width = part.shape[0] // n, part.shape[1]
        size = rows // self.shares
        pieces = [
            (source, k - 1, (size, width), (0, start), (q * size, j * width))
            for source, k, j, q in self.pieces(sources)
        ]
        pieces.append((len(sources), None, (rows, width), (me * rows, 0), (0, me * width)))
        return assemble((rows, n * width), [*sources, part], pieces)


class Reduction:
    def __init__(self, grad):
        self.grad = grad
        self.other = None

    def take(self, c):
        n, me = lax.axis_size("fsdp"), lax.axis_index("fsdp")
        rows, width = self.grad.shape[1:]
        return jnp.concatenate(
            [
                lax.dynamic_slice(
                    self.grad, (me ^ k, c * (rows // 2), 0), (1, rows // 2, width)
                )
                for k in range(n)
            ]
        )

    def begin(self):
        core = lax.axis_index("core")
        both = self.take(core).astype(f32) + core_swap(self.take(1 - core)).astype(f32)
        self.half = both.astype(bf16)

    def exchange(self):
        n = lax.axis_size("fsdp")
        self.half = jnp.stack(
            [self.half[0]] + [swap(self.half[k], "fsdp", k) for k in range(1, n)]
        )

    def finish(self, by_rows, start=0, size=None):
        n, me = lax.axis_size("fsdp"), lax.axis_index("fsdp")
        core = lax.axis_index("core")
        if self.other is None:
            self.other = core_swap(self.half)
        rows, width = self.half.shape[1:]
        size = width if size is None else size
        column = start // size

        def kernel(place, mine, other, out):
            @pl.when(pl.program_id(0) == 0)
            def _():
                out[...] = mine[0].astype(f32)

            @pl.when(pl.program_id(0) == 1)
            def _():
                out[...] = other[0].astype(f32)

        def mine_at(w, k, place):
            return (jnp.where(w == 0, k, n - 1), 0, column)

        def other_at(w, k, place):
            return (jnp.where(w == 0, 0, k), 0, column)

        def out_at(w, k, place):
            source = place[0] ^ k
            side = jnp.where(w == 0, place[1], 1 - place[1])
            return (side, source) if by_rows else (source * 2 + side, 0)

        return pl.pallas_call(
            kernel,
            out_shape=jax.ShapeDtypeStruct(
                (2 * rows, n * size) if by_rows else (2 * n * rows, size), f32
            ),
            grid_spec=pltpu.PrefetchScalarGridSpec(
                num_scalar_prefetch=1,
                grid=(2, n),
                in_specs=[
                    pl.BlockSpec((1, rows, size), mine_at),
                    pl.BlockSpec((1, rows, size), other_at),
                ],
                out_specs=pl.BlockSpec((rows, size), out_at),
            ),
            compiler_params=pltpu.CompilerParams(vmem_limit_bytes=32 << 20),
            cost_estimate=pl.CostEstimate(
                flops=0, bytes_accessed=2 * n * rows * size * 40, transcendentals=0
            ),
            name="place",
        )(jnp.stack([me, core]).astype(jnp.int32), self.half, self.other)


def roll_half(value):
    return pltpu.roll(value, HEAD // 2, axis=1)


def attention_specs(length, heads, kv_heads):
    wide, tall = GROUP * HEAD, heads
    return dict(
        queries=pl.BlockSpec((length, wide), lambda g, me: (0, g)),
        head=pl.BlockSpec((length, HEAD), lambda g, me: (0, g)),
        keys_in=pl.BlockSpec((length, HEAD), lambda g, me: (0, tall + g)),
        values_in=pl.BlockSpec((length, HEAD), lambda g, me: (0, tall + kv_heads + g)),
        table=pl.BlockSpec((length, HEAD), lambda g, me: (0, 0)),
        gain=pl.BlockSpec((1, HEAD), lambda g, me: (0, 0)),
        gain_out=pl.BlockSpec((1, 1, HEAD), lambda g, me: (g, 0, 0)),
    )


def attention_forward(qkv, cos_table, sin_table, gain_query, gain_key, first, heads, kv_heads):
    length = qkv.shape[0]
    n, _, size = first.shape

    def kernel(
        me_ref, q_ref, k_ref, v_ref, cos_ref, sin_ref, qg_ref, kg_ref, first_ref,
        queries_ref, keys_ref, values_ref, attended_ref, lse_ref, vt_ref,
    ):
        me = me_ref[0]

        def rows(block):
            return pl.ds(pl.multiple_of((block ^ me) * size, size), size)

        def prepare(raw, gain):
            normed = raw * rms_scale(raw) * gain
            return (normed * cos_ref[...] + roll_half(normed) * sin_ref[...]).astype(bf16)

        keys_ref[...] = prepare(k_ref[...], kg_ref[...])
        values_ref[...] = v_ref[...].astype(bf16)
        for k in range(n):
            vt_ref[k] = v_ref[k * size : (k + 1) * size, :].T.astype(bf16)
        for h in range(GROUP):
            columns = slice(h * HEAD, (h + 1) * HEAD)
            queries_ref[:, columns] = prepare(q_ref[:, columns], qg_ref[...])
        inside = lax.broadcasted_iota(jnp.int32, (size, size), 0) <= lax.broadcasted_iota(
            jnp.int32, (size, size), 1
        )
        place = lax.broadcasted_iota(jnp.int32, (size, size), 0)
        for h in range(GROUP):
            columns = slice(h * HEAD, (h + 1) * HEAD)
            for i in range(n):
                query = queries_ref[rows(i), columns]
                begin = first_ref[i ^ me]
                total = jnp.zeros((1, size), f32)
                out = jnp.zeros((HEAD, size), f32)
                for j in range(i + 1):
                    scores = matmul_nt(keys_ref[rows(j), :], query) * score_scale
                    allowed = place >= begin - j * size
                    if i == j:
                        allowed = allowed & inside
                    weight = jnp.where(allowed, jnp.exp(scores), 0.0)
                    total = total + jnp.sum(weight, axis=0, keepdims=True)
                    out = out + matmul(vt_ref[j ^ me], weight.astype(bf16))
                attended_ref[rows(i), columns] = (out / total).T.astype(bf16)
                lse_ref[0, h, i ^ me] = jnp.log(total)

    spec = attention_specs(length, heads, kv_heads)
    me = lax.axis_index("fsdp").reshape(1).astype(jnp.int32)
    return pl.pallas_call(
        kernel,
        out_shape=[
            jax.ShapeDtypeStruct((length, heads * HEAD), bf16),
            jax.ShapeDtypeStruct((length, kv_heads * HEAD), bf16),
            jax.ShapeDtypeStruct((length, kv_heads * HEAD), bf16),
            jax.ShapeDtypeStruct((length, heads * HEAD), bf16),
            jax.ShapeDtypeStruct((kv_heads, GROUP, n, 1, size), f32),
        ],
        grid_spec=pltpu.PrefetchScalarGridSpec(
            num_scalar_prefetch=1,
            grid=(kv_heads,),
            in_specs=[
                spec["queries"],
                spec["keys_in"],
                spec["values_in"],
                spec["table"],
                spec["table"],
                spec["gain"],
                spec["gain"],
                pl.BlockSpec((n, 1, size), lambda g, me: (0, 0, 0)),
            ],
            out_specs=[
                spec["queries"],
                spec["head"],
                spec["head"],
                spec["queries"],
                pl.BlockSpec((1, GROUP, n, 1, size), lambda g, me: (g, 0, 0, 0, 0)),
            ],
            scratch_shapes=[pltpu.VMEM((n, HEAD, size), bf16)],
        ),
        compiler_params=pltpu.CompilerParams(vmem_limit_bytes=48 << 20),
        cost_estimate=pl.CostEstimate(
            flops=4 * heads * length * length * HEAD,
            bytes_accessed=12 * length * heads * HEAD,
            transcendentals=heads * length * length,
        ),
        name="attention_forward",
    )(me, qkv, qkv, qkv, cos_table, sin_table, gain_query[None], gain_key[None], first)


def attention_backward(
    qkv, queries, keys, values, lse, d_attended, cos_table, sin_table, gain_query, gain_key, first
):
    length = qkv.shape[0]
    n, _, size = first.shape
    heads, kv_heads = queries.shape[1] // HEAD, keys.shape[1] // HEAD

    def kernel(
        me_ref, qr_ref, kr_ref, q_ref, k_ref, v_ref, lse_ref, da_ref, cos_ref, sin_ref,
        qg_ref, kg_ref, first_ref, dq_ref, dk_ref, dv_ref, dqg_ref, dkg_ref,
        kt_ref, probs_ref, dp_ref, dq_acc, dk_acc, dv_acc,
    ):
        me = me_ref[0]

        def rows(block):
            return pl.ds(pl.multiple_of((block ^ me) * size, size), size)

        def finish(raw, gain, incoming):
            turned = incoming * cos_ref[...] - roll_half(incoming) * sin_ref[...]
            d_raw, d_gain = norm_back(raw, rms_scale(raw), gain, turned)
            return d_raw.astype(bf16), jnp.sum(d_gain, axis=0, keepdims=True)

        for k in range(n):
            part = k_ref[k * size : (k + 1) * size, :].astype(f32)
            kt_ref[k] = part.T.astype(bf16)
        dk_acc[...] = jnp.zeros_like(dk_acc)
        dv_acc[...] = jnp.zeros_like(dv_acc)
        inside = lax.broadcasted_iota(jnp.int32, (size, size), 0) <= lax.broadcasted_iota(
            jnp.int32, (size, size), 1
        )
        place = lax.broadcasted_iota(jnp.int32, (size, size), 0)
        gain_total = jnp.zeros((1, HEAD), f32)
        for h in range(GROUP):
            columns = slice(h * HEAD, (h + 1) * HEAD)
            for i in range(n):
                query, d_out = q_ref[rows(i), columns], da_ref[rows(i), columns]
                begin, shift = first_ref[i ^ me], lse_ref[0, h, i ^ me]
                dots = jnp.zeros((1, size), f32)
                for j in range(i + 1):
                    scores = matmul_nt(k_ref[rows(j), :], query) * score_scale
                    allowed = place >= begin - j * size
                    if i == j:
                        allowed = allowed & inside
                    probs = jnp.where(allowed, jnp.exp(scores - shift), 0.0)
                    d_probs = matmul_nt(v_ref[rows(j), :], d_out)
                    dots = dots + jnp.sum(probs * d_probs, axis=0, keepdims=True)
                    probs_ref[j] = probs
                    dp_ref[j] = d_probs
                d_query = jnp.zeros((HEAD, size), f32)
                for j in range(i + 1):
                    probs = probs_ref[j]
                    d_scores = (probs * (dp_ref[j] - dots)).astype(bf16)
                    d_query = d_query + matmul(kt_ref[j ^ me], d_scores)
                    dk_acc[rows(j), :] += matmul(d_scores, query)
                    dv_acc[rows(j), :] += matmul(probs.astype(bf16), d_out)
                dq_acc[rows(i), :] = d_query.T * score_scale
            d_raw, d_gain = finish(qr_ref[:, columns], qg_ref[...], dq_acc[...])
            dq_ref[:, columns] = d_raw
            gain_total = gain_total + d_gain
        dqg_ref[0] = gain_total
        d_raw, d_gain = finish(kr_ref[...], kg_ref[...], dk_acc[...] * score_scale)
        dk_ref[...] = d_raw
        dkg_ref[0] = d_gain
        dv_ref[...] = dv_acc[...].astype(bf16)

    spec = attention_specs(length, heads, kv_heads)
    me = lax.axis_index("fsdp").reshape(1).astype(jnp.int32)
    d_query, d_key, d_value, d_query_gain, d_key_gain = pl.pallas_call(
        kernel,
        out_shape=[
            jax.ShapeDtypeStruct((length, heads * HEAD), bf16),
            jax.ShapeDtypeStruct((length, kv_heads * HEAD), bf16),
            jax.ShapeDtypeStruct((length, kv_heads * HEAD), bf16),
            jax.ShapeDtypeStruct((kv_heads, 1, HEAD), f32),
            jax.ShapeDtypeStruct((kv_heads, 1, HEAD), f32),
        ],
        grid_spec=pltpu.PrefetchScalarGridSpec(
            num_scalar_prefetch=1,
            grid=(kv_heads,),
            in_specs=[
                spec["queries"],
                spec["keys_in"],
                spec["queries"],
                spec["head"],
                spec["head"],
                pl.BlockSpec((1, GROUP, n, 1, size), lambda g, me: (g, 0, 0, 0, 0)),
                spec["queries"],
                spec["table"],
                spec["table"],
                spec["gain"],
                spec["gain"],
                pl.BlockSpec((n, 1, size), lambda g, me: (0, 0, 0)),
            ],
            out_specs=[
                spec["queries"],
                spec["head"],
                spec["head"],
                spec["gain_out"],
                spec["gain_out"],
            ],
            scratch_shapes=[
                pltpu.VMEM((n, HEAD, size), bf16),
                pltpu.VMEM((n, size, size), f32),
                pltpu.VMEM((n, size, size), f32),
                pltpu.VMEM((length, HEAD), f32),
                pltpu.VMEM((length, HEAD), f32),
                pltpu.VMEM((length, HEAD), f32),
            ],
        ),
        compiler_params=pltpu.CompilerParams(vmem_limit_bytes=48 << 20),
        cost_estimate=pl.CostEstimate(
            flops=10 * heads * length * length * HEAD,
            bytes_accessed=20 * length * heads * HEAD,
            transcendentals=heads * length * length,
        ),
        name="attention_backward",
    )(
        me, qkv, qkv, queries, keys, values, lse, d_attended, cos_table, sin_table,
        gain_query[None], gain_key[None], first,
    )
    return (
        jnp.concatenate([d_query, d_key, d_value], axis=1),
        jnp.sum(d_query_gain, axis=(0, 1)),
        jnp.sum(d_key_gain, axis=(0, 1)),
    )


def feed_forward_backward(cot, gate_up_parts, full_down, full_gu):
    n = len(gate_up_parts)
    length, width = cot.shape
    size = length // n
    ff = full_down.shape[0]
    step = 512 if ff % 512 == 0 else 256
    steps = ff // step

    def kernel(cot_ref, *refs):
        gates, ups = refs[:n], refs[n : 2 * n]
        down, wg, wu, d_gate_ref, d_up_ref, out_ref, total, d_hidden_ref = refs[2 * n :]
        f = pl.program_id(0)
        d_hidden_ref[...] = matmul_nt(cot_ref[...], down[...])
        for k in range(n):
            rows = slice(k * size, (k + 1) * size)
            d_hidden = d_hidden_ref[rows, :]
            gate, up = gates[k][...], ups[k][...]
            sg = 1.0 / (1.0 + jnp.exp(-gate))
            d_gate_ref[rows, :] = (d_hidden * up * sg * (1.0 + gate * (1.0 - sg))).astype(bf16)
            d_up_ref[rows, :] = (d_hidden * gate * sg).astype(bf16)

        @pl.when(f == 0)
        def _():
            total[...] = matmul_nt(d_gate_ref[...], wg[...])

        @pl.when(f > 0)
        def _():
            total[...] += matmul_nt(d_gate_ref[...], wg[...])

        @pl.when(f < steps - 1)
        def _():
            total[...] += matmul_nt(d_up_ref[...], wu[...])

        @pl.when(f == steps - 1)
        def _():
            out_ref[...] = (total[...] + matmul_nt(d_up_ref[...], wu[...])).astype(bf16)

    once = pl.Buffered(1)
    return pl.pallas_call(
        kernel,
        out_shape=[
            jax.ShapeDtypeStruct((length, ff), bf16),
            jax.ShapeDtypeStruct((length, ff), bf16),
            jax.ShapeDtypeStruct((length, width), bf16),
        ],
        grid=(steps,),
        in_specs=[pl.BlockSpec((length, width), lambda f: (0, 0), pipeline_mode=once)]
        + [pl.BlockSpec((size, step), lambda f: (0, f))] * n
        + [pl.BlockSpec((size, step), lambda f: (0, steps + f))] * n
        + [
            pl.BlockSpec((step, width), lambda f: (f, 0)),
            pl.BlockSpec((width, step), lambda f: (0, f)),
            pl.BlockSpec((width, step), lambda f: (0, steps + f)),
        ],
        out_specs=[
            pl.BlockSpec((length, step), lambda f: (0, f)),
            pl.BlockSpec((length, step), lambda f: (0, f)),
            pl.BlockSpec((length, width), lambda f: (0, 0), pipeline_mode=once),
        ],
        scratch_shapes=[pltpu.VMEM((length, width), f32), pltpu.VMEM((length, step), f32)],
        compiler_params=pltpu.CompilerParams(vmem_limit_bytes=60 << 20),
        cost_estimate=pl.CostEstimate(
            flops=6 * length * ff * width,
            bytes_accessed=6 * ff * width,
            transcendentals=length * ff,
        ),
        name="feed_forward_backward",
    )(cot, *gate_up_parts, *gate_up_parts, full_down, full_gu, full_gu)


def on_device(
    tokens,
    segments,
    attn_gain,
    w_query,
    w_key,
    w_value,
    query_gain,
    key_gain,
    w_out,
    mlp_gain,
    w_gate,
    w_up,
    w_down,
    cotangent,
):
    n, me = lax.axis_size("fsdp"), lax.axis_index("fsdp")
    tok_rows, width = tokens.shape[1], tokens.shape[2]
    length = segments.shape[1]
    heads, kv_heads = HEADS // n, KV_HEADS // n
    q_width, kv_width = heads * HEAD, kv_heads * HEAD
    ff = w_gate.shape[1] // n
    rows = width // n

    def block(value, k):
        return value[k * tok_rows : (k + 1) * tok_rows]

    def by_columns(first, second):
        columns = second.shape[1] // n
        return jnp.stack(
            [
                matmul_tn(first, second[:, j * columns : (j + 1) * columns]).astype(bf16)
                for j in range(n)
            ]
        )

    def by_rows(first, second):
        grad = with_layout_constraint(
            matmul_tn(first, second).astype(bf16), Layout(major_to_minor=(0, 1))
        )
        return grad.reshape(n, rows, second.shape[1])

    sizes = [attn_gain.shape[0], mlp_gain.shape[0], query_gain.shape[0], key_gain.shape[0]]
    packed = jnp.concatenate([attn_gain, mlp_gain, query_gain, key_gain])[None]
    tok = gather_begin(tokens[0])
    gains = [packed] + [swap(packed, "fsdp", k) for k in range(1, n)]
    attn_spread = Spread([w_query, w_key, w_value], [w_out])
    attn_got = attn_spread.begin()
    index = jnp.concatenate(
        [(me ^ k) * tok_rows + jnp.arange(tok_rows, dtype=jnp.int32) for k in range(n)]
    )
    doc_ids = jnp.concatenate(
        [rows_of(segments[0], (me ^ k) * tok_rows, tok_rows) for k in range(n)]
    )
    earlier = jnp.sum((doc_ids[None, :] < doc_ids[:, None]).astype(jnp.int32), axis=1)
    position = index - earlier
    inverse = rope_base ** (-2.0 * jnp.arange(HEAD // 2).astype(f32) / HEAD)
    angles = position.astype(f32)[:, None] * inverse[None, :]
    cosine, sine = jnp.cos(angles), jnp.sin(angles)
    cos_table = jnp.concatenate([cosine, cosine], axis=1)
    sin_table = jnp.concatenate([-sine, sine], axis=1)
    first = earlier.reshape(n, 1, tok_rows)
    gains = jnp.concatenate(gains, axis=0)
    gains = jnp.concatenate(
        [lax.dynamic_slice_in_dim(gains, me ^ j, 1, axis=0) for j in range(n)], axis=0
    ).astype(f32)
    ends = [sum(sizes[: j + 1]) for j in range(4)]
    gain_attn = gains[:, : ends[0]].reshape(-1)
    gain_mlp = gains[:, ends[0] : ends[1]].reshape(-1)
    gain_query = gains[:, ends[1] : ends[2]].reshape(-1)
    gain_key = gains[:, ends[2] : ends[3]].reshape(-1)
    attn_got = jnp.stack(attn_got)
    tok, attn_got, cos_table, sin_table, first, w_gate, w_up = fence(
        tok, attn_got, cos_table, sin_table, first, w_gate, w_up
    )

    tok = gather_end(tokens[0], tok)
    attn_along, attn_across = swap(attn_got, "z", 1), core_swap(attn_got)
    gu_spread = Spread([w_gate, w_up], [])
    gu_got = gu_spread.begin()
    tok, attn_along, attn_across = fence(tok, attn_along, attn_across)

    attn_sources = [attn_got, attn_along, attn_across, core_swap(attn_along)]
    stream_all = jnp.concatenate(tok, axis=0).astype(f32)
    normed = (stream_all * rms_scale(stream_all) * gain_attn).astype(bf16)
    full_qkv = attn_spread.join_rows(attn_sources)
    qkv = matmul(normed, full_qkv)
    queries, keys, values, attended, lse = attention_forward(
        qkv, cos_table, sin_table, gain_query, gain_key, first, heads, kv_heads
    )
    full_out = attn_spread.join_columns(attn_sources)
    attended, full_out, gu_got, cotangent = fence(attended, full_out, gu_got, cotangent)
    cot = cotangent[0]

    gu_got = jnp.stack(gu_got)
    gu_along, gu_across = swap(gu_got, "z", 1), core_swap(gu_got)
    begun = scatter_begin(matmul(block(attended, n - 1), full_out).astype(bf16))
    parts = [matmul(block(attended, k), full_out).astype(bf16) for k in range(n - 1)]
    stream = tokens[0].astype(f32)
    middle = stream + scatter_end(parts[0], scatter_middle(parts[1:], begun))
    mlp_scale = rms_scale(middle)
    normed_mine = (middle * mlp_scale * gain_mlp).astype(bf16)
    middle, mlp_scale, normed_mine = fence(middle, mlp_scale, normed_mine)

    begun = gather_begin(normed_mine)
    begun, gu_along, gu_across = fence(begun, gu_along, gu_across)

    def gate_and_up(part):
        both = matmul(part, full_gu)
        gate, up = both[:, :ff], both[:, ff:]
        return both, (gate / (1.0 + jnp.exp(-gate)) * up).astype(bf16)

    normed_parts = gather_end(normed_mine, begun)
    full_gu = gu_spread.join_rows([gu_got, gu_along, gu_across, core_swap(gu_along)])
    normed_parts, full_gu, cot, w_down = fence(normed_parts, full_gu, cot, w_down)

    cot_begun = gather_begin(cot)
    acts = [gate_and_up(part) for part in normed_parts]
    normed_mlp = jnp.concatenate(normed_parts, axis=0)
    hidden = jnp.concatenate([act[1] for act in acts], axis=0)
    cot_begun, acts, normed_mlp, hidden, w_down = fence(
        cot_begun, acts, normed_mlp, hidden, w_down
    )

    cot_parts = gather_end(cot, cot_begun)
    cot_all = jnp.concatenate(cot_parts, axis=0)
    cot_all, w_down = fence(cot_all, w_down)
    down = Reduction(by_columns(hidden, cot_all))
    down.begin()
    down.half, cot_all, w_down = fence(down.half, cot_all, w_down)

    whole = segments[0, 0] == 0

    def feed_forward_part():
        down_spread = Spread([], [w_down], along_z=False)
        got = jnp.stack(down_spread.begin())
        full_down = down_spread.join_columns([got, core_swap(got)])
        d_gate, d_up, d_normed_mlp = feed_forward_backward(
            cot_all, [act[0] for act in acts], full_down, full_gu
        )
        gate = Reduction(by_rows(normed_mlp, d_gate))
        gate.begin()
        gate.exchange()
        up = Reduction(by_rows(normed_mlp, d_up))
        up.begin()
        return full_down, d_normed_mlp, gate.half, up.half

    down.half = lax.psum(down.half, "z")
    full_down, d_normed_mlp, gate_half, up_half = block_of_work(whole, feed_forward_part)
    down.half, full_down, d_normed_mlp, gate_half, up_half = fence(
        down.half, full_down, d_normed_mlp, gate_half, up_half
    )

    def attention_part():
        begun = scatter_begin(block(d_normed_mlp, n - 1))
        got = scatter_middle([block(d_normed_mlp, k) for k in range(1, n - 1)], begun)
        d_normed_mine = scatter_end(block(d_normed_mlp, 0), got)
        d_middle, mlp_gain_rows = norm_back(middle, mlp_scale, gain_mlp, d_normed_mine)
        mlp_gain_grad = jnp.sum(mlp_gain_rows, axis=0)
        d_middle = cot.astype(f32) + d_middle
        d_mine = d_middle.astype(bf16)
        out_parts = [matmul(block(hidden, k), full_down).astype(bf16) for k in range(n)]
        d_branch = jnp.concatenate(gather_end(d_mine, gather_begin(d_mine)), axis=0)
        d_attended = matmul_nt(d_branch, full_out).astype(bf16)
        d_attended, down_half, out_parts = fence(d_attended, down.half, out_parts)
        d_qkv, *head_gain_grads = attention_backward(
            qkv,
            queries,
            keys,
            values,
            lse,
            d_attended,
            cos_table,
            sin_table,
            gain_query,
            gain_key,
            first,
        )
        out_sum = Reduction(by_columns(attended, d_branch))
        out_sum.begin()
        out_sum.exchange()
        qkv_sum = Reduction(by_rows(normed, d_qkv))
        qkv_sum.begin()
        qkv_sum.exchange()
        out_got = scatter_middle(out_parts[1 : n - 1], scatter_begin(out_parts[n - 1]))
        output = (middle + scatter_end(out_parts[0], out_got)).astype(bf16)
        down_sum = Reduction(None)
        down_sum.half = down_half
        down_sum.exchange()
        return (
            d_middle,
            mlp_gain_grad,
            d_qkv,
            head_gain_grads,
            out_sum.half,
            qkv_sum.half,
            output,
            down_sum.finish(False),
        )

    gate_half, up_half = lax.psum((gate_half, up_half), "z")
    gate_half, up_half, done = fence(gate_half, up_half, block_of_work(whole, attention_part))
    d_middle, mlp_gain_grad, d_qkv, head_gain_grads, out_half, qkv_half, output, down_full = done

    def input_part():
        begun = scatter_begin(matmul_nt(block(d_qkv, n - 1), full_qkv).astype(bf16))
        parts = [matmul_nt(block(d_qkv, k), full_qkv).astype(bf16) for k in range(n - 1)]
        d_normed = scatter_end(parts[0], scatter_middle(parts[1:], begun))
        d_stream, attn_gain_rows = norm_back(stream, rms_scale(stream), gain_attn, d_normed)
        gain_grads = jnp.concatenate(
            [jnp.sum(attn_gain_rows, axis=0), mlp_gain_grad] + head_gain_grads
        )
        for axis in ("core", "fsdp", "z"):
            k = 1
            while k < lax.axis_size(axis):
                gain_grads = gain_grads + swap(gain_grads, axis, k)
                k *= 2
        shares, start = [], 0
        for size in sizes:
            shares.append(rows_of(gain_grads, start + me * size, size))
            start += n * size
        gate, up = Reduction(None), Reduction(None)
        gate.half, up.half = gate_half, up_half
        up.exchange()
        return shares, d_middle + d_stream, gate.finish(True), up.finish(True)

    qkv_sum, out_sum = Reduction(None), Reduction(None)
    qkv_sum.half, out_sum.half = lax.psum((qkv_half, out_half), "z")
    qkv_sum.half, out_sum.half, done = fence(
        qkv_sum.half, out_sum.half, block_of_work(whole, input_part)
    )
    shares, input_grad, gate_full, up_full = done
    return (
        output[None],
        input_grad[None],
        shares[0],
        qkv_sum.finish(True, 0, q_width),
        qkv_sum.finish(True, q_width, kv_width),
        qkv_sum.finish(True, q_width + kv_width, kv_width),
        shares[2],
        shares[3],
        out_sum.finish(False),
        shares[1],
        gate_full,
        up_full,
        down_full,
    )


def solution(mesh):
    n, replicas = mesh.shape["fsdp"], mesh.shape["dp"]
    split = Mesh(mesh.devices.reshape(n, replicas // 2, 2), ("fsdp", "z", "core"))
    dp = ("z", "core")
    in_specs = (
        P(dp, "fsdp", None),
        P(dp, None),
        P("fsdp"),
        P("fsdp", None),
        P("fsdp", None),
        P("fsdp", None),
        P("fsdp"),
        P("fsdp"),
        P(None, "fsdp"),
        P("fsdp"),
        P("fsdp", None),
        P("fsdp", None),
        P(None, "fsdp"),
        P(dp, "fsdp", None),
    )
    out_specs = (
        P(dp, "fsdp", None),
        P(dp, "fsdp", None),
        P("fsdp"),
        P("fsdp", None),
        P("fsdp", None),
        P("fsdp", None),
        P("fsdp"),
        P("fsdp"),
        P(None, "fsdp"),
        P("fsdp"),
        P("fsdp", None),
        P("fsdp", None),
        P(None, "fsdp"),
    )
    return jax.shard_map(
        on_device, mesh=split, in_specs=in_specs, out_specs=out_specs, check_vma=False
    )
```

```python
import math

import jax
import jax.numpy as jnp
from jax import lax
from jax.experimental import pallas as pl
from jax.experimental.layout import Layout, with_layout_constraint
from jax.experimental.pallas import tpu as pltpu
from jax.sharding import Mesh
from jax.sharding import PartitionSpec as P

HEADS = 16
KV_HEADS = 8
HEAD = 128
GROUP = HEADS // KV_HEADS

epsilon = 1e-06
rope_base = 1000000.0
masked_score = -1e30
score_scale = 1.0 / math.sqrt(HEAD)

bf16 = jnp.bfloat16
f32 = jnp.float32


def matmul(first, second):
    return jnp.dot(first, second, preferred_element_type=f32)


def matmul_tn(first, second):
    return lax.dot_general(first, second, (((0,), (0,)), ((), ())), preferred_element_type=f32)


def matmul_nt(first, second):
    return lax.dot_general(first, second, (((1,), (1,)), ((), ())), preferred_element_type=f32)


def rms_scale(vector):
    return lax.rsqrt(jnp.mean(vector * vector, axis=-1, keepdims=True) + epsilon)


def norm_back(vector, scale, gain, incoming):
    scaled = gain * incoming
    d_vector = scale * scaled - vector * (scale**3) * jnp.mean(
        vector * scaled, axis=-1, keepdims=True
    )
    return d_vector, incoming * vector * scale


def swap(value, axis, k):
    return lax.ppermute(value, axis, [(j, j ^ k) for j in range(lax.axis_size(axis))])


def core_swap(value):
    return swap(value, "core", 1)


def rows_of(value, start, size):
    return lax.dynamic_slice_in_dim(value, start, size, axis=0)


def fence(*trees):
    leaves, shape = jax.tree.flatten(trees)
    return jax.tree.unflatten(shape, lax.optimization_barrier(leaves))


def block_of_work(whole, body):
    shapes = jax.eval_shape(body)
    return lax.cond(
        whole,
        body,
        lambda: jax.tree.map(lambda leaf: jnp.zeros(leaf.shape, leaf.dtype), shapes),
    )


def gather(shard, beside=None):
    n = lax.axis_size("fsdp")
    if n != 4:
        return fence([shard] + [swap(shard, "fsdp", k) for k in range(1, n)], beside)
    half = shard.shape[0] // 2
    top, low = shard[:half], shard[half:]
    x_top, y_low = swap(top, "fsdp", 1), swap(low, "fsdp", 2)
    x_low, y_top = swap(low, "fsdp", 1), swap(top, "fsdp", 2)
    x_top, y_low, beside = fence(x_top, y_low, beside)
    far = [swap(x_top, "fsdp", 2), swap(y_low, "fsdp", 1)]
    blocks = [
        shard,
        jnp.concatenate([x_top, x_low], axis=0),
        jnp.concatenate([y_top, y_low], axis=0),
        jnp.concatenate(far, axis=0),
    ]
    return blocks, beside


def scatter(part_of):
    n = lax.axis_size("fsdp")
    if n != 4:
        halves = []
        for h in range(2):
            total = part_of(0, h).astype(f32)
            for k in range(1, n):
                total = total + swap(part_of(k, h), "fsdp", k).astype(f32)
            halves.append(total)
        return jnp.concatenate(halves, axis=0)
    from_x, from_y = swap(part_of(3, 0), "fsdp", 1), swap(part_of(3, 1), "fsdp", 2)
    x_top, y_low = swap(part_of(1, 0), "fsdp", 1), swap(part_of(2, 1), "fsdp", 2)
    low = (part_of(1, 1).astype(f32) + from_y.astype(f32)).astype(bf16)
    top = (part_of(2, 0).astype(f32) + from_x.astype(f32)).astype(bf16)
    x_low, y_top = swap(low, "fsdp", 1), swap(top, "fsdp", 2)
    return jnp.concatenate(
        [
            part_of(0, 0).astype(f32) + x_top.astype(f32) + y_top.astype(f32),
            part_of(0, 1).astype(f32) + x_low.astype(f32) + y_low.astype(f32),
        ],
        axis=0,
    )


def scatter_direct(block_of):
    n = lax.axis_size("fsdp")
    got = {k: swap(block_of(k), "fsdp", k) for k in range(n - 1, 0, -1)}
    return [block_of(0)] + [got[k] for k in range(1, n)]


def add_up(blocks):
    total = blocks[0].astype(f32)
    for block in blocks[1:]:
        total = total + block.astype(f32)
    return total


def assemble(shape, sources, pieces):
    count, held = len(pieces), len(sources)

    def kernel(place_ref, *refs):
        ins, out, hold = refs[:held], refs[held], refs[held + 1]
        sem_in, sem_out = refs[held + 2], refs[held + 3]

        def window(ref, k, first):
            size = pieces[k][2]
            row = pl.multiple_of(place_ref[4 * k + first], 16)
            column = pl.multiple_of(place_ref[4 * k + first + 1], 128)
            return ref.at[pl.ds(row, size[0]), pl.ds(column, size[1])]

        def source(k):
            ref, lead = ins[pieces[k][0]], pieces[k][1]
            return window(ref if lead is None else ref.at[lead], k, 0)

        loads = [
            pltpu.make_async_copy(source(k), window(hold, k, 2), sem_in.at[k])
            for k in range(count)
        ]
        stores = [
            pltpu.make_async_copy(window(hold, k, 2), window(out, k, 2), sem_out.at[k])
            for k in range(count)
        ]
        for load in loads:
            load.start()
        for load, store in zip(loads, stores):
            load.wait()
            store.start()
        for store in stores:
            store.wait()

    size = 2 * math.prod(shape)
    places = [jnp.int32(v) for piece in pieces for at in piece[3:] for v in at]
    return pl.pallas_call(
        kernel,
        out_shape=jax.ShapeDtypeStruct(shape, bf16),
        in_specs=[pl.BlockSpec(memory_space=pltpu.SMEM)]
        + [
            pl.BlockSpec(memory_space=pl.ANY if source.ndim == 3 else pltpu.HBM)
            for source in sources
        ],
        out_specs=pl.BlockSpec(memory_space=pl.ANY),
        scratch_shapes=[
            pltpu.VMEM(shape, bf16),
            pltpu.SemaphoreType.DMA((count,)),
            pltpu.SemaphoreType.DMA((count,)),
        ],
        compiler_params=pltpu.CompilerParams(vmem_limit_bytes=size + (4 << 20)),
        cost_estimate=pl.CostEstimate(flops=0, bytes_accessed=2 * size, transcendentals=0),
        name="assemble",
    )(jnp.stack(places), *sources)


class Spread:
    def __init__(self, by_rows, by_columns, along_z=True):
        self.by_rows, self.by_columns, self.along_z = by_rows, by_columns, along_z
        self.shares = 4 if along_z else 2

    def share(self, j, q):
        n = lax.axis_size("fsdp")
        cuts = []
        for part in self.by_rows:
            size, width = part.shape[0] // self.shares, part.shape[1] // n
            cuts.append(lax.dynamic_slice(part, (q * size, j * width), (size, width)))
        for part in self.by_columns:
            rows = part.shape[0] // n
            size = rows // self.shares
            cuts.append(rows_of(part, j * rows + q * size, size))
        return cuts[0] if len(cuts) == 1 else jnp.concatenate(cuts, axis=1)

    def begin(self):
        n, me = lax.axis_size("fsdp"), lax.axis_index("fsdp")
        mine = lax.axis_index("core")
        if self.along_z:
            mine = 2 * (lax.axis_index("z") % 2) + mine
        return [swap(self.share(me ^ k, mine), "fsdp", k) for k in range(1, n)]

    def pieces(self, sources):
        n, me = lax.axis_size("fsdp"), lax.axis_index("fsdp")
        side, core = lax.axis_index("z") % 2, lax.axis_index("core")
        shares = [core, 1 - core]
        if self.along_z:
            shares = [
                2 * side + core,
                2 * (1 - side) + core,
                2 * side + 1 - core,
                2 * (1 - side) + 1 - core,
            ]
        return [
            (source, k, me ^ k, shares[source])
            for k in range(1, n)
            for source in range(len(sources))
        ]

    def join_rows(self, sources):
        n, me = lax.axis_size("fsdp"), lax.axis_index("fsdp")
        rows = self.by_rows[0].shape[0]
        widths = [part.shape[1] // n for part in self.by_rows]
        total, size = sum(widths), rows // self.shares
        pieces = [
            (source, k - 1, (size, total), (0, 0), (j * rows + q * size, 0))
            for source, k, j, q in self.pieces(sources)
        ]
        start = 0
        for index, width in enumerate(widths):
            pieces.append(
                (len(sources) + index, None, (rows, width), (0, me * width), (me * rows, start))
            )
            start += width
        return assemble((n * rows, total), [*sources, *self.by_rows], pieces)

    def join_columns(self, sources):
        n, me = lax.axis_size("fsdp"), lax.axis_index("fsdp")
        start = sum(part.shape[1] // n for part in self.by_rows)
        (part,) = self.by_columns
        rows, width = part.shape[0] // n, part.shape[1]
        size = rows // self.shares
        pieces = [
            (source, k - 1, (size, width), (0, start), (q * size, j * width))
            for source, k, j, q in self.pieces(sources)
        ]
        pieces.append((len(sources), None, (rows, width), (me * rows, 0), (0, me * width)))
        return assemble((rows, n * width), [*sources, part], pieces)


class Reduction:
    def __init__(self, grad):
        self.grad = grad

    def begin(self):
        core = lax.axis_index("core")
        rows = self.grad.shape[1] // 2

        def take(c):
            return lax.dynamic_slice_in_dim(self.grad, c * rows, rows, axis=1)

        both = take(core).astype(f32) + core_swap(take(1 - core)).astype(f32)
        self.half = both.astype(bf16)

    def exchange(self):
        n, me = lax.axis_size("fsdp"), lax.axis_index("fsdp")
        parts = [
            lax.dynamic_index_in_dim(self.half, me ^ k, 0, keepdims=False) for k in range(n)
        ]
        self.half = jnp.stack([parts[0]] + [swap(parts[k], "fsdp", k) for k in range(1, n)])

    def finish(self, by_rows, sizes=None):
        n, me = lax.axis_size("fsdp"), lax.axis_index("fsdp")
        core = lax.axis_index("core")
        other = core_swap(self.half)
        rows, width = self.half.shape[1:]
        sizes = [width] if sizes is None else sizes

        def kernel(place, mine, other, *outs):
            def write(ref):
                start = 0
                for out, size in zip(outs, sizes):
                    out[...] = ref[0, :, start : start + size].astype(f32)
                    start += size

            @pl.when(pl.program_id(0) == 0)
            def _():
                write(mine)

            @pl.when(pl.program_id(0) == 1)
            def _():
                write(other)

        def mine_at(w, k, place):
            return (jnp.where(w == 0, k, n - 1), 0, 0)

        def other_at(w, k, place):
            return (jnp.where(w == 0, 0, k), 0, 0)

        def out_at(w, k, place):
            source = place[0] ^ k
            side = jnp.where(w == 0, place[1], 1 - place[1])
            return (side, source) if by_rows else (source * 2 + side, 0)

        result = pl.pallas_call(
            kernel,
            out_shape=[
                jax.ShapeDtypeStruct(
                    (2 * rows, n * size) if by_rows else (2 * n * rows, size), f32
                )
                for size in sizes
            ],
            grid_spec=pltpu.PrefetchScalarGridSpec(
                num_scalar_prefetch=1,
                grid=(2, n),
                in_specs=[
                    pl.BlockSpec((1, rows, width), mine_at),
                    pl.BlockSpec((1, rows, width), other_at),
                ],
                out_specs=[pl.BlockSpec((rows, size), out_at) for size in sizes],
            ),
            compiler_params=pltpu.CompilerParams(vmem_limit_bytes=32 << 20),
            cost_estimate=pl.CostEstimate(
                flops=0, bytes_accessed=2 * n * rows * width * 6, transcendentals=0
            ),
            name="place",
        )(jnp.stack([me, core]).astype(jnp.int32), self.half, other)
        return result if len(sizes) > 1 else result[0]


def roll_half(value):
    return pltpu.roll(value, HEAD // 2, axis=1)


def attention_specs(length, heads, kv_heads):
    wide, tall = GROUP * HEAD, heads
    return dict(
        queries=pl.BlockSpec((length, wide), lambda g, me: (0, g)),
        head=pl.BlockSpec((length, HEAD), lambda g, me: (0, g)),
        keys_in=pl.BlockSpec((length, HEAD), lambda g, me: (0, tall + g)),
        values_in=pl.BlockSpec((length, HEAD), lambda g, me: (0, tall + kv_heads + g)),
        table=pl.BlockSpec((length, HEAD), lambda g, me: (0, 0)),
        gain=pl.BlockSpec((1, HEAD), lambda g, me: (0, 0)),
        gain_out=pl.BlockSpec((1, 1, HEAD), lambda g, me: (g, 0, 0)),
    )


def attention_forward(qkv, cos_table, sin_table, gain_query, gain_key, first, heads, kv_heads):
    length = qkv.shape[0]
    n, _, size = first.shape

    def kernel(
        me_ref, q_ref, k_ref, v_ref, cos_ref, sin_ref, qg_ref, kg_ref, first_ref,
        queries_ref, keys_ref, values_ref, attended_ref, lse_ref, vt_ref,
    ):
        me = me_ref[0]

        def rows(block):
            return pl.ds(pl.multiple_of((block ^ me) * size, size), size)

        def prepare(raw, gain):
            normed = raw * rms_scale(raw) * gain
            return (normed * cos_ref[...] + roll_half(normed) * sin_ref[...]).astype(bf16)

        keys_ref[...] = prepare(k_ref[...], kg_ref[...])
        values_ref[...] = v_ref[...].astype(bf16)
        for k in range(n):
            vt_ref[k] = v_ref[k * size : (k + 1) * size, :].T.astype(bf16)
        for h in range(GROUP):
            columns = slice(h * HEAD, (h + 1) * HEAD)
            queries_ref[:, columns] = prepare(q_ref[:, columns], qg_ref[...])
        inside = lax.broadcasted_iota(jnp.int32, (size, size), 0) <= lax.broadcasted_iota(
            jnp.int32, (size, size), 1
        )
        place = lax.broadcasted_iota(jnp.int32, (size, size), 0)
        for h in range(GROUP):
            columns = slice(h * HEAD, (h + 1) * HEAD)
            for i in range(n):
                query = queries_ref[rows(i), columns]
                begin = first_ref[i ^ me]
                total = jnp.zeros((1, size), f32)
                out = jnp.zeros((HEAD, size), f32)
                for j in range(i + 1):
                    scores = matmul_nt(keys_ref[rows(j), :], query) * score_scale
                    allowed = place >= begin - j * size
                    if i == j:
                        allowed = allowed & inside
                    weight = jnp.where(allowed, jnp.exp(scores), 0.0)
                    total = total + jnp.sum(weight, axis=0, keepdims=True)
                    out = out + matmul(vt_ref[j ^ me], weight.astype(bf16))
                attended_ref[rows(i), columns] = (out / total).T.astype(bf16)
                lse_ref[0, h, i ^ me] = jnp.log(total)

    spec = attention_specs(length, heads, kv_heads)
    me = lax.axis_index("fsdp").reshape(1).astype(jnp.int32)
    return pl.pallas_call(
        kernel,
        out_shape=[
            jax.ShapeDtypeStruct((length, heads * HEAD), bf16),
            jax.ShapeDtypeStruct((length, kv_heads * HEAD), bf16),
            jax.ShapeDtypeStruct((length, kv_heads * HEAD), bf16),
            jax.ShapeDtypeStruct((length, heads * HEAD), bf16),
            jax.ShapeDtypeStruct((kv_heads, GROUP, n, 1, size), f32),
        ],
        grid_spec=pltpu.PrefetchScalarGridSpec(
            num_scalar_prefetch=1,
            grid=(kv_heads,),
            in_specs=[
                spec["queries"],
                spec["keys_in"],
                spec["values_in"],
                spec["table"],
                spec["table"],
                spec["gain"],
                spec["gain"],
                pl.BlockSpec((n, 1, size), lambda g, me: (0, 0, 0)),
            ],
            out_specs=[
                spec["queries"],
                spec["head"],
                spec["head"],
                spec["queries"],
                pl.BlockSpec((1, GROUP, n, 1, size), lambda g, me: (g, 0, 0, 0, 0)),
            ],
            scratch_shapes=[pltpu.VMEM((n, HEAD, size), bf16)],
        ),
        compiler_params=pltpu.CompilerParams(vmem_limit_bytes=48 << 20),
        cost_estimate=pl.CostEstimate(
            flops=4 * heads * length * length * HEAD,
            bytes_accessed=12 * length * heads * HEAD,
            transcendentals=heads * length * length,
        ),
        name="attention_forward",
    )(me, qkv, qkv, qkv, cos_table, sin_table, gain_query[None], gain_key[None], first)


def attention_backward(
    qkv, queries, keys, values, lse, d_attended, cos_table, sin_table, gain_query, gain_key, first
):
    length = qkv.shape[0]
    n, _, size = first.shape
    heads, kv_heads = queries.shape[1] // HEAD, keys.shape[1] // HEAD

    def kernel(
        me_ref, qr_ref, kr_ref, q_ref, k_ref, v_ref, lse_ref, da_ref, cos_ref, sin_ref,
        qg_ref, kg_ref, first_ref, dq_ref, dk_ref, dv_ref, dqg_ref, dkg_ref,
        kt_ref, probs_ref, dp_ref, dq_acc, dk_acc, dv_acc,
    ):
        me = me_ref[0]

        def rows(block):
            return pl.ds(pl.multiple_of((block ^ me) * size, size), size)

        def finish(raw, gain, incoming):
            turned = incoming * cos_ref[...] - roll_half(incoming) * sin_ref[...]
            d_raw, d_gain = norm_back(raw, rms_scale(raw), gain, turned)
            return d_raw.astype(bf16), jnp.sum(d_gain, axis=0, keepdims=True)

        for k in range(n):
            part = k_ref[k * size : (k + 1) * size, :].astype(f32)
            kt_ref[k] = part.T.astype(bf16)
        dk_acc[...] = jnp.zeros_like(dk_acc)
        dv_acc[...] = jnp.zeros_like(dv_acc)
        inside = lax.broadcasted_iota(jnp.int32, (size, size), 0) <= lax.broadcasted_iota(
            jnp.int32, (size, size), 1
        )
        place = lax.broadcasted_iota(jnp.int32, (size, size), 0)
        gain_total = jnp.zeros((1, HEAD), f32)
        for h in range(GROUP):
            columns = slice(h * HEAD, (h + 1) * HEAD)
            for i in range(n):
                query, d_out = q_ref[rows(i), columns], da_ref[rows(i), columns]
                begin, shift = first_ref[i ^ me], lse_ref[0, h, i ^ me]
                dots = jnp.zeros((1, size), f32)
                for j in range(i + 1):
                    scores = matmul_nt(k_ref[rows(j), :], query) * score_scale
                    allowed = place >= begin - j * size
                    if i == j:
                        allowed = allowed & inside
                    probs = jnp.where(allowed, jnp.exp(scores - shift), 0.0)
                    d_probs = matmul_nt(v_ref[rows(j), :], d_out)
                    dots = dots + jnp.sum(probs * d_probs, axis=0, keepdims=True)
                    probs_ref[j] = probs
                    dp_ref[j] = d_probs
                d_query = jnp.zeros((HEAD, size), f32)
                for j in range(i + 1):
                    probs = probs_ref[j]
                    d_scores = (probs * (dp_ref[j] - dots)).astype(bf16)
                    d_query = d_query + matmul(kt_ref[j ^ me], d_scores)
                    dk_acc[rows(j), :] += matmul(d_scores, query)
                    dv_acc[rows(j), :] += matmul(probs.astype(bf16), d_out)
                dq_acc[rows(i), :] = d_query.T * score_scale
            d_raw, d_gain = finish(qr_ref[:, columns], qg_ref[...], dq_acc[...])
            dq_ref[:, columns] = d_raw
            gain_total = gain_total + d_gain
        dqg_ref[0] = gain_total
        d_raw, d_gain = finish(kr_ref[...], kg_ref[...], dk_acc[...] * score_scale)
        dk_ref[...] = d_raw
        dkg_ref[0] = d_gain
        dv_ref[...] = dv_acc[...].astype(bf16)

    spec = attention_specs(length, heads, kv_heads)
    me = lax.axis_index("fsdp").reshape(1).astype(jnp.int32)
    d_query, d_key, d_value, d_query_gain, d_key_gain = pl.pallas_call(
        kernel,
        out_shape=[
            jax.ShapeDtypeStruct((length, heads * HEAD), bf16),
            jax.ShapeDtypeStruct((length, kv_heads * HEAD), bf16),
            jax.ShapeDtypeStruct((length, kv_heads * HEAD), bf16),
            jax.ShapeDtypeStruct((kv_heads, 1, HEAD), f32),
            jax.ShapeDtypeStruct((kv_heads, 1, HEAD), f32),
        ],
        grid_spec=pltpu.PrefetchScalarGridSpec(
            num_scalar_prefetch=1,
            grid=(kv_heads,),
            in_specs=[
                spec["queries"],
                spec["keys_in"],
                spec["queries"],
                spec["head"],
                spec["head"],
                pl.BlockSpec((1, GROUP, n, 1, size), lambda g, me: (g, 0, 0, 0, 0)),
                spec["queries"],
                spec["table"],
                spec["table"],
                spec["gain"],
                spec["gain"],
                pl.BlockSpec((n, 1, size), lambda g, me: (0, 0, 0)),
            ],
            out_specs=[
                spec["queries"],
                spec["head"],
                spec["head"],
                spec["gain_out"],
                spec["gain_out"],
            ],
            scratch_shapes=[
                pltpu.VMEM((n, HEAD, size), bf16),
                pltpu.VMEM((n, size, size), f32),
                pltpu.VMEM((n, size, size), f32),
                pltpu.VMEM((length, HEAD), f32),
                pltpu.VMEM((length, HEAD), f32),
                pltpu.VMEM((length, HEAD), f32),
            ],
        ),
        compiler_params=pltpu.CompilerParams(vmem_limit_bytes=48 << 20),
        cost_estimate=pl.CostEstimate(
            flops=10 * heads * length * length * HEAD,
            bytes_accessed=20 * length * heads * HEAD,
            transcendentals=heads * length * length,
        ),
        name="attention_backward",
    )(
        me, qkv, qkv, queries, keys, values, lse, d_attended, cos_table, sin_table,
        gain_query[None], gain_key[None], first,
    )
    return (
        jnp.concatenate([d_query, d_key, d_value], axis=1),
        jnp.sum(d_query_gain, axis=(0, 1)),
        jnp.sum(d_key_gain, axis=(0, 1)),
    )


def feed_forward_backward(cot, gate_up_parts, full_down, full_gu):
    n = len(gate_up_parts)
    length, width = cot.shape
    size = length // n
    ff = full_down.shape[0]
    step = 512 if ff % 512 == 0 else 256
    first = ff // step
    tile = 256

    def kernel(cot_ref, *refs):
        gates, ups = refs[:n], refs[n : 2 * n]
        down, wgu, d_gate_ref, d_up_ref, out_ref, both, d_hidden_ref = refs[2 * n :]
        f = pl.program_id(0)

        @pl.when(f < first)
        def _():
            d_hidden_ref[...] = matmul_nt(cot_ref[...], down[...])
            for k in range(n):
                rows = slice(k * size, (k + 1) * size)
                d_hidden = d_hidden_ref[rows, :]
                gate, up = gates[k][...].astype(f32), ups[k][...].astype(f32)
                sg = 1.0 / (1.0 + jnp.exp(-gate))
                d_gate = (d_hidden * up * sg * (1.0 + gate * (1.0 - sg))).astype(bf16)
                d_up = (d_hidden * gate * sg).astype(bf16)
                d_gate_ref[rows, :] = d_gate
                d_up_ref[rows, :] = d_up
                at = pl.multiple_of(f * step, step)
                both[rows, pl.ds(at, step)] = d_gate
                both[rows, pl.ds(ff + at, step)] = d_up

        @pl.when(f >= first)
        def _():
            out_ref[...] = matmul_nt(both[...], wgu[...]).astype(bf16)

    once = pl.Buffered(1)

    def early(f):
        return jnp.minimum(f, first - 1)

    def late(f):
        return jnp.maximum(f - first, 0)

    return pl.pallas_call(
        kernel,
        out_shape=[
            jax.ShapeDtypeStruct((length, ff), bf16),
            jax.ShapeDtypeStruct((length, ff), bf16),
            jax.ShapeDtypeStruct((length, width), bf16),
        ],
        grid=(first + width // tile,),
        in_specs=[pl.BlockSpec((length, width), lambda f: (0, 0), pipeline_mode=once)]
        + [pl.BlockSpec((size, step), lambda f: (0, early(f)))] * n
        + [pl.BlockSpec((size, step), lambda f: (0, first + early(f)))] * n
        + [
            pl.BlockSpec((step, width), lambda f: (early(f), 0)),
            pl.BlockSpec((tile, 2 * ff), lambda f: (late(f), 0)),
        ],
        out_specs=[
            pl.BlockSpec((length, step), lambda f: (0, early(f))),
            pl.BlockSpec((length, step), lambda f: (0, early(f))),
            pl.BlockSpec((length, tile), lambda f: (0, late(f))),
        ],
        scratch_shapes=[pltpu.VMEM((length, 2 * ff), bf16), pltpu.VMEM((length, step), f32)],
        compiler_params=pltpu.CompilerParams(vmem_limit_bytes=60 << 20),
        cost_estimate=pl.CostEstimate(
            flops=6 * length * ff * width,
            bytes_accessed=6 * ff * width,
            transcendentals=length * ff,
        ),
        name="feed_forward_backward",
    )(cot, *gate_up_parts, *gate_up_parts, full_down, full_gu)


def on_device(
    tokens,
    segments,
    attn_gain,
    w_query,
    w_key,
    w_value,
    query_gain,
    key_gain,
    w_out,
    mlp_gain,
    w_gate,
    w_up,
    w_down,
    cotangent,
):
    n, me = lax.axis_size("fsdp"), lax.axis_index("fsdp")
    tok_rows, width = tokens.shape[1], tokens.shape[2]
    length = segments.shape[1]
    heads, kv_heads = HEADS // n, KV_HEADS // n
    q_width, kv_width = heads * HEAD, kv_heads * HEAD
    ff = w_gate.shape[1] // n
    rows = width // n

    def block(value, k):
        return value[k * tok_rows : (k + 1) * tok_rows]

    def half_block(value, k, h):
        start = k * tok_rows + h * (tok_rows // 2)
        return value[start : start + tok_rows // 2]

    def by_columns(first, second):
        columns = second.shape[1] // n
        grad = jnp.stack(
            [
                matmul_tn(first, second[:, j * columns : (j + 1) * columns]).astype(bf16)
                for j in range(n)
            ]
        )
        return with_layout_constraint(grad, Layout(major_to_minor=(0, 1, 2)))

    def by_rows(first, second):
        grad = with_layout_constraint(
            matmul_tn(first, second).astype(bf16), Layout(major_to_minor=(0, 1))
        )
        return grad.reshape(n, rows, second.shape[1])

    sizes = [attn_gain.shape[0], mlp_gain.shape[0], query_gain.shape[0], key_gain.shape[0]]
    packed = jnp.concatenate([attn_gain, mlp_gain, query_gain, key_gain])[None]
    tok, _ = gather(tokens[0])
    gains = [packed] + [swap(packed, "fsdp", k) for k in range(1, n)]
    gains, w_query, w_key, w_value, w_out = fence(gains, w_query, w_key, w_value, w_out)
    attn_spread = Spread([w_query, w_key, w_value], [w_out])
    attn_got = attn_spread.begin()
    index = jnp.concatenate(
        [(me ^ k) * tok_rows + jnp.arange(tok_rows, dtype=jnp.int32) for k in range(n)]
    )
    doc_ids = jnp.concatenate(
        [rows_of(segments[0], (me ^ k) * tok_rows, tok_rows) for k in range(n)]
    )
    earlier = jnp.sum((doc_ids[None, :] < doc_ids[:, None]).astype(jnp.int32), axis=1)
    position = index - earlier
    inverse = rope_base ** (-2.0 * jnp.arange(HEAD // 2).astype(f32) / HEAD)
    angles = position.astype(f32)[:, None] * inverse[None, :]
    cosine, sine = jnp.cos(angles), jnp.sin(angles)
    cos_table = jnp.concatenate([cosine, cosine], axis=1)
    sin_table = jnp.concatenate([-sine, sine], axis=1)
    first = earlier.reshape(n, 1, tok_rows)
    gains = jnp.concatenate(gains, axis=0)
    gains = jnp.concatenate(
        [lax.dynamic_slice_in_dim(gains, me ^ j, 1, axis=0) for j in range(n)], axis=0
    ).astype(f32)
    ends = [sum(sizes[: j + 1]) for j in range(4)]
    gain_attn = gains[:, : ends[0]].reshape(-1)
    gain_mlp = gains[:, ends[0] : ends[1]].reshape(-1)
    gain_query = gains[:, ends[1] : ends[2]].reshape(-1)
    gain_key = gains[:, ends[2] : ends[3]].reshape(-1)
    attn_got = jnp.stack(attn_got)
    attn_along, attn_across = swap(attn_got, "z", 1), core_swap(attn_got)
    whole = segments[0, 0] == 0
    tok, cos_table, sin_table, first, w_gate, w_up, whole = fence(
        tok, cos_table, sin_table, first, w_gate, w_up, whole
    )

    gu_spread = Spread([w_gate, w_up], [])
    gu_got = gu_spread.begin()
    attn_sources = [attn_got, attn_along, attn_across, core_swap(attn_along)]

    def normed_block(part):
        part = part.astype(f32)
        return (part * rms_scale(part) * gain_attn).astype(bf16)

    normed = jnp.concatenate([normed_block(part) for part in tok], axis=0)
    full_qkv = attn_spread.join_rows(attn_sources)
    qkv = matmul(normed, full_qkv)
    queries, keys, values, attended, lse = attention_forward(
        qkv, cos_table, sin_table, gain_query, gain_key, first, heads, kv_heads
    )
    full_out = attn_spread.join_columns(attn_sources)
    attended, full_out, gu_got, cotangent = fence(attended, full_out, gu_got, cotangent)
    cot = cotangent[0]

    gu_got = jnp.stack(gu_got)
    gu_along, gu_across = swap(gu_got, "z", 1), core_swap(gu_got)
    def out_part(k, h):
        return matmul(half_block(attended, k, h), full_out).astype(bf16)

    stream = tokens[0].astype(f32)
    middle = stream + scatter(out_part)
    mlp_scale = rms_scale(middle)
    normed_mine = (middle * mlp_scale * gain_mlp).astype(bf16)
    middle, mlp_scale, normed_mine, w_down = fence(middle, mlp_scale, normed_mine, w_down)

    normed_parts, _ = gather(normed_mine)
    down_spread = Spread([], [w_down])
    down_got = jnp.stack(down_spread.begin())
    normed_parts, gu_along, gu_across, cot, down_got = fence(
        normed_parts, gu_along, gu_across, cot, down_got
    )

    def gate_and_up(part):
        both = matmul(part, full_gu)
        gate, up = both[:, :ff], both[:, ff:]
        return both, (gate / (1.0 + jnp.exp(-gate)) * up).astype(bf16)

    full_gu = gu_spread.join_rows([gu_got, gu_along, gu_across, core_swap(gu_along)])

    down_along, down_across = swap(down_got, "z", 1), core_swap(down_got)
    own_act = gate_and_up(normed_parts[0])
    cot_parts, (own_act, full_gu) = gather(cot, beside=(own_act, full_gu))
    acts = [own_act] + [gate_and_up(part) for part in normed_parts[1:]]
    acts, down_along, down_across = fence(acts, down_along, down_across)
    normed_mlp = jnp.concatenate(normed_parts, axis=0)
    hidden = jnp.concatenate([act[1] for act in acts], axis=0)
    cot_all = jnp.concatenate(cot_parts, axis=0)
    full_down = down_spread.join_columns(
        [down_got, down_along, down_across, core_swap(down_along)]
    )
    cot_all, full_down, hidden, normed_mlp, acts = fence(
        cot_all, full_down, hidden, normed_mlp, acts
    )

    core = lax.axis_index("core")

    def down_grad(c):
        part = lax.dynamic_slice_in_dim(hidden, c * (ff // 2), ff // 2, axis=1)
        return by_columns(part, cot_all)

    down = Reduction(None)
    other = core_swap(down_grad(1 - core))
    down.half = (down_grad(core).astype(f32) + other.astype(f32)).astype(bf16)
    down.half, cot_all, full_down = fence(down.half, cot_all, full_down)

    def feed_forward_part():
        out_partial, cots = fence(matmul(hidden, full_down).astype(bf16), cot_all)
        out_got = scatter_direct(lambda k: block(out_partial, k))
        d_gate, d_up, d_normed_mlp = feed_forward_backward(
            cots, [act[0] for act in acts], full_down, full_gu
        )
        grad_gate, d_up, out_got = fence(by_rows(normed_mlp, d_gate), d_up, out_got)
        output = (middle + add_up(out_got)).astype(bf16)
        gate = Reduction(grad_gate)
        gate.begin()
        gate.exchange()
        up = Reduction(by_rows(normed_mlp, d_up))
        up.begin()
        return output, d_normed_mlp, gate.half, up.half

    down.half = lax.psum(down.half, "z")
    output, d_normed_mlp, gate_half, up_half = block_of_work(whole, feed_forward_part)
    down.half, output, d_normed_mlp, gate_half, up_half = fence(
        down.half, output, d_normed_mlp, gate_half, up_half
    )

    def attention_part():
        d_normed_mine = scatter(lambda k, h: half_block(d_normed_mlp, k, h))
        d_middle, mlp_gain_rows = norm_back(middle, mlp_scale, gain_mlp, d_normed_mine)
        mlp_gain_grad = jnp.sum(mlp_gain_rows, axis=0)
        d_middle = cot.astype(f32) + d_middle
        d_mine = d_middle.astype(bf16)
        d_branch = jnp.concatenate(gather(d_mine)[0], axis=0)
        d_attended = matmul_nt(d_branch, full_out).astype(bf16)
        d_attended, down_half = fence(d_attended, down.half)
        d_qkv, *head_gain_grads = attention_backward(
            qkv,
            queries,
            keys,
            values,
            lse,
            d_attended,
            cos_table,
            sin_table,
            gain_query,
            gain_key,
            first,
        )
        out_sum = Reduction(by_columns(attended, d_branch))
        out_sum.begin()
        out_sum.exchange()
        qkv_sum = Reduction(by_rows(normed, d_qkv))
        qkv_sum.begin()
        qkv_sum.exchange()
        down_sum = Reduction(None)
        down_sum.half = down_half
        down_sum.exchange()
        return (
            d_middle,
            mlp_gain_grad,
            matmul_nt(d_qkv, full_qkv).astype(bf16),
            head_gain_grads,
            out_sum.half,
            qkv_sum.half,
            down_sum.finish(False),
        )

    gate_half, up_half = lax.psum((gate_half, up_half), "z")
    gate_half, up_half, done = fence(gate_half, up_half, block_of_work(whole, attention_part))
    d_middle, mlp_gain_grad, partial, head_gain_grads, out_half, qkv_half, down_full = done

    def input_part():
        d_normed = scatter(lambda k, h: half_block(partial, k, h))
        gate, up = Reduction(None), Reduction(None)
        gate.half, up.half = gate_half, up_half
        up.exchange()
        d_normed, gate_full = fence(d_normed, gate.finish(True))
        stream = tokens[0].astype(f32)
        d_stream, attn_gain_rows = norm_back(stream, rms_scale(stream), gain_attn, d_normed)
        gain_grads = jnp.concatenate(
            [jnp.sum(attn_gain_rows, axis=0), mlp_gain_grad] + head_gain_grads
        )
        for axis in ("core", "fsdp", "z"):
            k = 1
            while k < lax.axis_size(axis):
                gain_grads = gain_grads + swap(gain_grads, axis, k)
                k *= 2
        shares, start = [], 0
        for size in sizes:
            shares.append(rows_of(gain_grads, start + me * size, size))
            start += n * size
        return shares, d_middle + d_stream, gate_full, up.finish(True)

    qkv_sum, out_sum = Reduction(None), Reduction(None)
    qkv_sum.half, out_sum.half = lax.psum((qkv_half, out_half), "z")
    qkv_sum.half, out_sum.half, done = fence(
        qkv_sum.half, out_sum.half, block_of_work(whole, input_part)
    )
    shares, input_grad, gate_full, up_full = done
    query_full, key_full, value_full = qkv_sum.finish(True, [q_width, kv_width, kv_width])
    return (
        output[None],
        input_grad[None],
        shares[0],
        query_full,
        key_full,
        value_full,
        shares[2],
        shares[3],
        out_sum.finish(False),
        shares[1],
        gate_full,
        up_full,
        down_full,
    )


def solution(mesh):
    n, replicas = mesh.shape["fsdp"], mesh.shape["dp"]
    split = Mesh(mesh.devices.reshape(n, replicas // 2, 2), ("fsdp", "z", "core"))
    dp = ("z", "core")
    in_specs = (
        P(dp, "fsdp", None),
        P(dp, None),
        P("fsdp"),
        P("fsdp", None),
        P("fsdp", None),
        P("fsdp", None),
        P("fsdp"),
        P("fsdp"),
        P(None, "fsdp"),
        P("fsdp"),
        P("fsdp", None),
        P("fsdp", None),
        P(None, "fsdp"),
        P(dp, "fsdp", None),
    )
    out_specs = (
        P(dp, "fsdp", None),
        P(dp, "fsdp", None),
        P("fsdp"),
        P("fsdp", None),
        P("fsdp", None),
        P("fsdp", None),
        P("fsdp"),
        P("fsdp"),
        P(None, "fsdp"),
        P("fsdp"),
        P("fsdp", None),
        P("fsdp", None),
        P(None, "fsdp"),
    )
    return jax.shard_map(
        on_device, mesh=split, in_specs=in_specs, out_specs=out_specs, check_vma=False
    )
```

```python
import math

import jax
import jax.numpy as jnp
from jax import lax
from jax.experimental import pallas as pl
from jax.experimental.layout import Layout, with_layout_constraint
from jax.experimental.pallas import tpu as pltpu
from jax.sharding import Mesh
from jax.sharding import PartitionSpec as P

HEADS = 16
KV_HEADS = 8
HEAD = 128
GROUP = HEADS // KV_HEADS

epsilon = 1e-06
rope_base = 1000000.0
masked_score = -1e30
score_scale = 1.0 / math.sqrt(HEAD)

bf16 = jnp.bfloat16
f32 = jnp.float32


def matmul(first, second):
    return jnp.dot(first, second, preferred_element_type=f32)


def matmul_tn(first, second):
    return lax.dot_general(first, second, (((0,), (0,)), ((), ())), preferred_element_type=f32)


def matmul_nt(first, second):
    return lax.dot_general(first, second, (((1,), (1,)), ((), ())), preferred_element_type=f32)


def rms_scale(vector):
    return lax.rsqrt(jnp.mean(vector * vector, axis=-1, keepdims=True) + epsilon)


def norm_back(vector, scale, gain, incoming):
    scaled = gain * incoming
    d_vector = scale * scaled - vector * (scale**3) * jnp.mean(
        vector * scaled, axis=-1, keepdims=True
    )
    return d_vector, incoming * vector * scale


def swap(value, axis, k):
    return lax.ppermute(value, axis, [(j, j ^ k) for j in range(lax.axis_size(axis))])


def core_swap(value):
    return swap(value, "core", 1)


def rows_of(value, start, size):
    return lax.dynamic_slice_in_dim(value, start, size, axis=0)


def fence(*trees):
    leaves, shape = jax.tree.flatten(trees)
    return jax.tree.unflatten(shape, lax.optimization_barrier(leaves))


def block_of_work(whole, body):
    shapes = jax.eval_shape(body)
    return lax.cond(
        whole,
        body,
        lambda: jax.tree.map(lambda leaf: jnp.zeros(leaf.shape, leaf.dtype), shapes),
    )


def gather(shard, beside=None, last=None):
    n = lax.axis_size("fsdp")
    if n != 4:
        return fence([shard] + [swap(shard, "fsdp", k) for k in range(1, n)], beside, last)
    half = shard.shape[0] // 2
    top, low = shard[:half], shard[half:]
    x_top, y_low = swap(top, "fsdp", 1), swap(low, "fsdp", 2)
    x_low, y_top = swap(low, "fsdp", 1), swap(top, "fsdp", 2)
    x_top, y_low, beside = fence(x_top, y_low, beside)
    far = [swap(x_top, "fsdp", 2), swap(y_low, "fsdp", 1)]
    if last is not None:
        far, last = fence(far, last)
    blocks = [
        shard,
        jnp.concatenate([x_top, x_low], axis=0),
        jnp.concatenate([y_top, y_low], axis=0),
        jnp.concatenate(far, axis=0),
    ]
    return blocks, beside, last


def scatter(part_of):
    n = lax.axis_size("fsdp")
    if n != 4:
        halves = []
        for h in range(2):
            total = part_of(0, h).astype(f32)
            for k in range(1, n):
                total = total + swap(part_of(k, h), "fsdp", k).astype(f32)
            halves.append(total)
        return jnp.concatenate(halves, axis=0)
    from_x, from_y = swap(part_of(3, 0), "fsdp", 1), swap(part_of(3, 1), "fsdp", 2)
    x_top, y_low = swap(part_of(1, 0), "fsdp", 1), swap(part_of(2, 1), "fsdp", 2)
    low = (part_of(1, 1).astype(f32) + from_y.astype(f32)).astype(bf16)
    top = (part_of(2, 0).astype(f32) + from_x.astype(f32)).astype(bf16)
    x_low, y_top = swap(low, "fsdp", 1), swap(top, "fsdp", 2)
    return jnp.concatenate(
        [
            part_of(0, 0).astype(f32) + x_top.astype(f32) + y_top.astype(f32),
            part_of(0, 1).astype(f32) + x_low.astype(f32) + y_low.astype(f32),
        ],
        axis=0,
    )


def scatter_direct(block_of):
    n = lax.axis_size("fsdp")
    got = {k: swap(block_of(k), "fsdp", k) for k in range(n - 1, 0, -1)}
    return [block_of(0)] + [got[k] for k in range(1, n)]


def add_up(blocks):
    total = blocks[0].astype(f32)
    for block in blocks[1:]:
        total = total + block.astype(f32)
    return total


def assemble(shape, sources, pieces):
    count, held = len(pieces), len(sources)

    def kernel(place_ref, *refs):
        ins, out, hold = refs[:held], refs[held], refs[held + 1]
        sem_in, sem_out = refs[held + 2], refs[held + 3]

        def window(ref, k, first):
            size = pieces[k][2]
            row = pl.multiple_of(place_ref[4 * k + first], 16)
            column = pl.multiple_of(place_ref[4 * k + first + 1], 128)
            return ref.at[pl.ds(row, size[0]), pl.ds(column, size[1])]

        def source(k):
            ref, lead = ins[pieces[k][0]], pieces[k][1]
            return window(ref if lead is None else ref.at[lead], k, 0)

        loads = [
            pltpu.make_async_copy(source(k), window(hold, k, 2), sem_in.at[k])
            for k in range(count)
        ]
        stores = [
            pltpu.make_async_copy(window(hold, k, 2), window(out, k, 2), sem_out.at[k])
            for k in range(count)
        ]
        for load in loads:
            load.start()
        for load, store in zip(loads, stores):
            load.wait()
            store.start()
        for store in stores:
            store.wait()

    size = 2 * math.prod(shape)
    places = [jnp.int32(v) for piece in pieces for at in piece[3:] for v in at]
    return pl.pallas_call(
        kernel,
        out_shape=jax.ShapeDtypeStruct(shape, bf16),
        in_specs=[pl.BlockSpec(memory_space=pltpu.SMEM)]
        + [
            pl.BlockSpec(memory_space=pl.ANY if source.ndim == 3 else pltpu.HBM)
            for source in sources
        ],
        out_specs=pl.BlockSpec(memory_space=pl.ANY),
        scratch_shapes=[
            pltpu.VMEM(shape, bf16),
            pltpu.SemaphoreType.DMA((count,)),
            pltpu.SemaphoreType.DMA((count,)),
        ],
        compiler_params=pltpu.CompilerParams(vmem_limit_bytes=size + (4 << 20)),
        cost_estimate=pl.CostEstimate(flops=0, bytes_accessed=2 * size, transcendentals=0),
        name="assemble",
    )(jnp.stack(places), *sources)


class Spread:
    def __init__(self, by_rows, by_columns, along_z=True):
        self.by_rows, self.by_columns, self.along_z = by_rows, by_columns, along_z
        self.shares = 4 if along_z else 2

    def share(self, j, q):
        n = lax.axis_size("fsdp")
        cuts = []
        for part in self.by_rows:
            size, width = part.shape[0] // self.shares, part.shape[1] // n
            cuts.append(lax.dynamic_slice(part, (q * size, j * width), (size, width)))
        for part in self.by_columns:
            rows = part.shape[0] // n
            size = rows // self.shares
            cuts.append(rows_of(part, j * rows + q * size, size))
        return cuts[0] if len(cuts) == 1 else jnp.concatenate(cuts, axis=1)

    def begin(self):
        n, me = lax.axis_size("fsdp"), lax.axis_index("fsdp")
        mine = lax.axis_index("core")
        if self.along_z:
            mine = 2 * (lax.axis_index("z") % 2) + mine
        return [swap(self.share(me ^ k, mine), "fsdp", k) for k in range(1, n)]

    def pieces(self, sources):
        n, me = lax.axis_size("fsdp"), lax.axis_index("fsdp")
        side, core = lax.axis_index("z") % 2, lax.axis_index("core")
        shares = [core, 1 - core]
        if self.along_z:
            shares = [
                2 * side + core,
                2 * (1 - side) + core,
                2 * side + 1 - core,
                2 * (1 - side) + 1 - core,
            ]
        return [
            (source, k, me ^ k, shares[source])
            for k in range(1, n)
            for source in range(len(sources))
        ]

    def join_rows(self, sources):
        n, me = lax.axis_size("fsdp"), lax.axis_index("fsdp")
        rows = self.by_rows[0].shape[0]
        widths = [part.shape[1] // n for part in self.by_rows]
        total, size = sum(widths), rows // self.shares
        pieces = [
            (source, k - 1, (size, total), (0, 0), (j * rows + q * size, 0))
            for source, k, j, q in self.pieces(sources)
        ]
        start = 0
        for index, width in enumerate(widths):
            pieces.append(
                (len(sources) + index, None, (rows, width), (0, me * width), (me * rows, start))
            )
            start += width
        return assemble((n * rows, total), [*sources, *self.by_rows], pieces)

    def join_columns(self, sources):
        n, me = lax.axis_size("fsdp"), lax.axis_index("fsdp")
        start = sum(part.shape[1] // n for part in self.by_rows)
        (part,) = self.by_columns
        rows, width = part.shape[0] // n, part.shape[1]
        size = rows // self.shares
        pieces = [
            (source, k - 1, (size, width), (0, start), (q * size, j * width))
            for source, k, j, q in self.pieces(sources)
        ]
        pieces.append((len(sources), None, (rows, width), (me * rows, 0), (0, me * width)))
        return assemble((rows, n * width), [*sources, part], pieces)


class Reduction:
    def __init__(self, grad):
        self.grad = grad

    def begin(self):
        core = lax.axis_index("core")
        axis = self.grad.ndim - 2
        rows = self.grad.shape[axis] // 2

        def take(c):
            return lax.dynamic_slice_in_dim(self.grad, c * rows, rows, axis=axis)

        both = take(core).astype(f32) + core_swap(take(1 - core)).astype(f32)
        self.half = both.astype(bf16)

    def exchange(self):
        n, me = lax.axis_size("fsdp"), lax.axis_index("fsdp")

        def part(j):
            if self.half.ndim == 2:
                width = self.half.shape[1] // n
                return lax.dynamic_slice_in_dim(self.half, j * width, width, axis=1)
            return lax.dynamic_index_in_dim(self.half, j, 0, keepdims=False)

        self.half = jnp.stack(
            [part(me)] + [swap(part(me ^ k), "fsdp", k) for k in range(1, n)]
        )

    def finish(self, by_rows, sizes=None, split=False):
        n, me = lax.axis_size("fsdp"), lax.axis_index("fsdp")
        core = lax.axis_index("core")
        other = core_swap(self.half)
        rows, width = self.half.shape[1:]
        sizes = [width] if sizes is None else sizes
        count = len(sizes)
        place = jnp.stack([me, core]).astype(jnp.int32)

        def write(ref, outs):
            start = 0
            for out, size in zip(outs, sizes):
                out[...] = ref[0, :, start : start + size].astype(f32)
                start += size

        def out_at(w, k, place):
            source = place[0] ^ k
            side = jnp.where(w == 0, place[1], 1 - place[1])
            return (side, source) if by_rows else (source * 2 + side, 0)

        def call(kernel, grid, in_specs, out_index, aliases, operands):
            return pl.pallas_call(
                kernel,
                out_shape=[
                    jax.ShapeDtypeStruct(
                        (2 * rows, n * size) if by_rows else (2 * n * rows, size), f32
                    )
                    for size in sizes
                ],
                grid_spec=pltpu.PrefetchScalarGridSpec(
                    num_scalar_prefetch=1,
                    grid=grid,
                    in_specs=in_specs,
                    out_specs=[pl.BlockSpec((rows, size), out_index) for size in sizes],
                ),
                input_output_aliases=aliases,
                compiler_params=pltpu.CompilerParams(vmem_limit_bytes=32 << 20),
                cost_estimate=pl.CostEstimate(
                    flops=0, bytes_accessed=math.prod(grid) * rows * width * 6, transcendentals=0
                ),
                name="place",
            )(place, *operands)

        if split:
            one = pl.BlockSpec((1, rows, width), lambda k, place: (k, 0, 0))

            def own(place, mine, *outs):
                write(mine, outs)

            def rest(place, other, *refs):
                write(other, refs[count:])

            result = call(own, (n,), [one], lambda k, place: out_at(0, k, place), {}, [self.half])
            result = call(
                rest,
                (n,),
                [one] + [pl.BlockSpec(memory_space=pl.ANY)] * count,
                lambda k, place: out_at(1, k, place),
                {2 + i: i for i in range(count)},
                [other, *result],
            )
        else:

            def both(place, mine, other, *outs):
                @pl.when(pl.program_id(0) == 0)
                def _():
                    write(mine, outs)

                @pl.when(pl.program_id(0) == 1)
                def _():
                    write(other, outs)

            result = call(
                both,
                (2, n),
                [
                    pl.BlockSpec(
                        (1, rows, width),
                        lambda w, k, place: (jnp.where(w == 0, k, n - 1), 0, 0),
                    ),
                    pl.BlockSpec(
                        (1, rows, width), lambda w, k, place: (jnp.where(w == 0, 0, k), 0, 0)
                    ),
                ],
                out_at,
                {},
                [self.half, other],
            )
        return result if count > 1 else result[0]


def roll_half(value):
    return pltpu.roll(value, HEAD // 2, axis=1)


def attention_specs(length, heads, kv_heads):
    wide, tall = GROUP * HEAD, heads
    return dict(
        queries=pl.BlockSpec((length, wide), lambda g, me: (0, g)),
        head=pl.BlockSpec((length, HEAD), lambda g, me: (0, g)),
        keys_in=pl.BlockSpec((length, HEAD), lambda g, me: (0, tall + g)),
        values_in=pl.BlockSpec((length, HEAD), lambda g, me: (0, tall + kv_heads + g)),
        table=pl.BlockSpec((length, HEAD), lambda g, me: (0, 0)),
        gain=pl.BlockSpec((1, HEAD), lambda g, me: (0, 0)),
        gain_out=pl.BlockSpec((1, 1, HEAD), lambda g, me: (g, 0, 0)),
    )


def attention_forward(qkv, cos_table, sin_table, gain_query, gain_key, first, heads, kv_heads):
    length = qkv.shape[0]
    n, _, size = first.shape

    def kernel(
        me_ref, q_ref, k_ref, v_ref, cos_ref, sin_ref, qg_ref, kg_ref, first_ref,
        queries_ref, keys_ref, values_ref, attended_ref, lse_ref, vt_ref,
    ):
        me = me_ref[0]

        def rows(block):
            return pl.ds(pl.multiple_of((block ^ me) * size, size), size)

        def prepare(raw, gain):
            normed = raw * rms_scale(raw) * gain
            return (normed * cos_ref[...] + roll_half(normed) * sin_ref[...]).astype(bf16)

        keys_ref[...] = prepare(k_ref[...], kg_ref[...])
        values_ref[...] = v_ref[...].astype(bf16)
        for k in range(n):
            vt_ref[k] = v_ref[k * size : (k + 1) * size, :].T.astype(bf16)
        for h in range(GROUP):
            columns = slice(h * HEAD, (h + 1) * HEAD)
            queries_ref[:, columns] = prepare(q_ref[:, columns], qg_ref[...])
        inside = lax.broadcasted_iota(jnp.int32, (size, size), 0) <= lax.broadcasted_iota(
            jnp.int32, (size, size), 1
        )
        place = lax.broadcasted_iota(jnp.int32, (size, size), 0)
        for h in range(GROUP):
            columns = slice(h * HEAD, (h + 1) * HEAD)
            for i in range(n):
                query = queries_ref[rows(i), columns]
                begin = first_ref[i ^ me]
                total = jnp.zeros((1, size), f32)
                out = jnp.zeros((HEAD, size), f32)
                for j in range(i + 1):
                    scores = matmul_nt(keys_ref[rows(j), :], query) * score_scale
                    allowed = place >= begin - j * size
                    if i == j:
                        allowed = allowed & inside
                    weight = jnp.where(allowed, jnp.exp(scores), 0.0)
                    total = total + jnp.sum(weight, axis=0, keepdims=True)
                    out = out + matmul(vt_ref[j ^ me], weight.astype(bf16))
                attended_ref[rows(i), columns] = (out / total).T.astype(bf16)
                lse_ref[0, h, i ^ me] = jnp.log(total)

    spec = attention_specs(length, heads, kv_heads)
    me = lax.axis_index("fsdp").reshape(1).astype(jnp.int32)
    return pl.pallas_call(
        kernel,
        out_shape=[
            jax.ShapeDtypeStruct((length, heads * HEAD), bf16),
            jax.ShapeDtypeStruct((length, kv_heads * HEAD), bf16),
            jax.ShapeDtypeStruct((length, kv_heads * HEAD), bf16),
            jax.ShapeDtypeStruct((length, heads * HEAD), bf16),
            jax.ShapeDtypeStruct((kv_heads, GROUP, n, 1, size), f32),
        ],
        grid_spec=pltpu.PrefetchScalarGridSpec(
            num_scalar_prefetch=1,
            grid=(kv_heads,),
            in_specs=[
                spec["queries"],
                spec["keys_in"],
                spec["values_in"],
                spec["table"],
                spec["table"],
                spec["gain"],
                spec["gain"],
                pl.BlockSpec((n, 1, size), lambda g, me: (0, 0, 0)),
            ],
            out_specs=[
                spec["queries"],
                spec["head"],
                spec["head"],
                spec["queries"],
                pl.BlockSpec((1, GROUP, n, 1, size), lambda g, me: (g, 0, 0, 0, 0)),
            ],
            scratch_shapes=[pltpu.VMEM((n, HEAD, size), bf16)],
        ),
        compiler_params=pltpu.CompilerParams(vmem_limit_bytes=48 << 20),
        cost_estimate=pl.CostEstimate(
            flops=4 * heads * length * length * HEAD,
            bytes_accessed=12 * length * heads * HEAD,
            transcendentals=heads * length * length,
        ),
        name="attention_forward",
    )(me, qkv, qkv, qkv, cos_table, sin_table, gain_query[None], gain_key[None], first)


def attention_backward(
    qkv, queries, keys, values, lse, d_attended, cos_table, sin_table, gain_query, gain_key, first
):
    length = qkv.shape[0]
    n, _, size = first.shape
    heads, kv_heads = queries.shape[1] // HEAD, keys.shape[1] // HEAD

    def kernel(
        me_ref, qr_ref, kr_ref, q_ref, k_ref, v_ref, lse_ref, da_ref, cos_ref, sin_ref,
        qg_ref, kg_ref, first_ref, dq_ref, dk_ref, dv_ref, dqg_ref, dkg_ref,
        kt_ref, probs_ref, dp_ref, dq_acc, dk_acc, dv_acc,
    ):
        me = me_ref[0]

        def rows(block):
            return pl.ds(pl.multiple_of((block ^ me) * size, size), size)

        def finish(raw, gain, incoming):
            turned = incoming * cos_ref[...] - roll_half(incoming) * sin_ref[...]
            d_raw, d_gain = norm_back(raw, rms_scale(raw), gain, turned)
            return d_raw.astype(bf16), jnp.sum(d_gain, axis=0, keepdims=True)

        for k in range(n):
            part = k_ref[k * size : (k + 1) * size, :].astype(f32)
            kt_ref[k] = part.T.astype(bf16)
        dk_acc[...] = jnp.zeros_like(dk_acc)
        dv_acc[...] = jnp.zeros_like(dv_acc)
        inside = lax.broadcasted_iota(jnp.int32, (size, size), 0) <= lax.broadcasted_iota(
            jnp.int32, (size, size), 1
        )
        place = lax.broadcasted_iota(jnp.int32, (size, size), 0)
        gain_total = jnp.zeros((1, HEAD), f32)
        for h in range(GROUP):
            columns = slice(h * HEAD, (h + 1) * HEAD)
            for i in range(n):
                query, d_out = q_ref[rows(i), columns], da_ref[rows(i), columns]
                begin, shift = first_ref[i ^ me], lse_ref[0, h, i ^ me]
                dots = jnp.zeros((1, size), f32)
                for j in range(i + 1):
                    scores = matmul_nt(k_ref[rows(j), :], query) * score_scale
                    allowed = place >= begin - j * size
                    if i == j:
                        allowed = allowed & inside
                    probs = jnp.where(allowed, jnp.exp(scores - shift), 0.0)
                    d_probs = matmul_nt(v_ref[rows(j), :], d_out)
                    dots = dots + jnp.sum(probs * d_probs, axis=0, keepdims=True)
                    probs_ref[j] = probs
                    dp_ref[j] = d_probs
                d_query = jnp.zeros((HEAD, size), f32)
                for j in range(i + 1):
                    probs = probs_ref[j]
                    d_scores = (probs * (dp_ref[j] - dots)).astype(bf16)
                    d_query = d_query + matmul(kt_ref[j ^ me], d_scores)
                    dk_acc[rows(j), :] += matmul(d_scores, query)
                    dv_acc[rows(j), :] += matmul(probs.astype(bf16), d_out)
                dq_acc[rows(i), :] = d_query.T * score_scale
            d_raw, d_gain = finish(qr_ref[:, columns], qg_ref[...], dq_acc[...])
            dq_ref[:, columns] = d_raw
            gain_total = gain_total + d_gain
        dqg_ref[0] = gain_total
        d_raw, d_gain = finish(kr_ref[...], kg_ref[...], dk_acc[...] * score_scale)
        dk_ref[...] = d_raw
        dkg_ref[0] = d_gain
        dv_ref[...] = dv_acc[...].astype(bf16)

    spec = attention_specs(length, heads, kv_heads)
    me = lax.axis_index("fsdp").reshape(1).astype(jnp.int32)
    d_query, d_key, d_value, d_query_gain, d_key_gain = pl.pallas_call(
        kernel,
        out_shape=[
            jax.ShapeDtypeStruct((length, heads * HEAD), bf16),
            jax.ShapeDtypeStruct((length, kv_heads * HEAD), bf16),
            jax.ShapeDtypeStruct((length, kv_heads * HEAD), bf16),
            jax.ShapeDtypeStruct((kv_heads, 1, HEAD), f32),
            jax.ShapeDtypeStruct((kv_heads, 1, HEAD), f32),
        ],
        grid_spec=pltpu.PrefetchScalarGridSpec(
            num_scalar_prefetch=1,
            grid=(kv_heads,),
            in_specs=[
                spec["queries"],
                spec["keys_in"],
                spec["queries"],
                spec["head"],
                spec["head"],
                pl.BlockSpec((1, GROUP, n, 1, size), lambda g, me: (g, 0, 0, 0, 0)),
                spec["queries"],
                spec["table"],
                spec["table"],
                spec["gain"],
                spec["gain"],
                pl.BlockSpec((n, 1, size), lambda g, me: (0, 0, 0)),
            ],
            out_specs=[
                spec["queries"],
                spec["head"],
                spec["head"],
                spec["gain_out"],
                spec["gain_out"],
            ],
            scratch_shapes=[
                pltpu.VMEM((n, HEAD, size), bf16),
                pltpu.VMEM((n, size, size), f32),
                pltpu.VMEM((n, size, size), f32),
                pltpu.VMEM((length, HEAD), f32),
                pltpu.VMEM((length, HEAD), f32),
                pltpu.VMEM((length, HEAD), f32),
            ],
        ),
        compiler_params=pltpu.CompilerParams(vmem_limit_bytes=48 << 20),
        cost_estimate=pl.CostEstimate(
            flops=10 * heads * length * length * HEAD,
            bytes_accessed=20 * length * heads * HEAD,
            transcendentals=heads * length * length,
        ),
        name="attention_backward",
    )(
        me, qkv, qkv, queries, keys, values, lse, d_attended, cos_table, sin_table,
        gain_query[None], gain_key[None], first,
    )
    return (
        jnp.concatenate([d_query, d_key, d_value], axis=1),
        jnp.sum(d_query_gain, axis=(0, 1)),
        jnp.sum(d_key_gain, axis=(0, 1)),
    )


def feed_forward_backward(cot, gate_up_parts, full_down, full_gu):
    n = len(gate_up_parts)
    length, width = cot.shape
    size = length // n
    ff = full_down.shape[0]
    step = 512 if ff % 512 == 0 else 256
    first = ff // step
    tile = 256

    def kernel(cot_ref, *refs):
        gates, ups = refs[:n], refs[n : 2 * n]
        down, wgu, d_gate_ref, d_up_ref, out_ref, both, d_hidden_ref = refs[2 * n :]
        f = pl.program_id(0)

        @pl.when(f < first)
        def _():
            d_hidden_ref[...] = matmul_nt(cot_ref[...], down[...])
            for k in range(n):
                rows = slice(k * size, (k + 1) * size)
                d_hidden = d_hidden_ref[rows, :]
                gate, up = gates[k][...].astype(f32), ups[k][...].astype(f32)
                sg = 1.0 / (1.0 + jnp.exp(-gate))
                d_gate = (d_hidden * up * sg * (1.0 + gate * (1.0 - sg))).astype(bf16)
                d_up = (d_hidden * gate * sg).astype(bf16)
                d_gate_ref[rows, :] = d_gate
                d_up_ref[rows, :] = d_up
                at = pl.multiple_of(f * step, step)
                both[rows, pl.ds(at, step)] = d_gate
                both[rows, pl.ds(ff + at, step)] = d_up

        @pl.when(f >= first)
        def _():
            out_ref[...] = matmul_nt(both[...], wgu[...]).astype(bf16)

    once = pl.Buffered(1)

    def early(f):
        return jnp.minimum(f, first - 1)

    def late(f):
        return jnp.maximum(f - first, 0)

    return pl.pallas_call(
        kernel,
        out_shape=[
            jax.ShapeDtypeStruct((length, ff), bf16),
            jax.ShapeDtypeStruct((length, ff), bf16),
            jax.ShapeDtypeStruct((length, width), bf16),
        ],
        grid=(first + width // tile,),
        in_specs=[pl.BlockSpec((length, width), lambda f: (0, 0), pipeline_mode=once)]
        + [pl.BlockSpec((size, step), lambda f: (0, early(f)))] * n
        + [pl.BlockSpec((size, step), lambda f: (0, first + early(f)))] * n
        + [
            pl.BlockSpec((step, width), lambda f: (early(f), 0)),
            pl.BlockSpec((tile, 2 * ff), lambda f: (late(f), 0)),
        ],
        out_specs=[
            pl.BlockSpec((length, step), lambda f: (0, early(f))),
            pl.BlockSpec((length, step), lambda f: (0, early(f))),
            pl.BlockSpec((length, tile), lambda f: (0, late(f))),
        ],
        scratch_shapes=[pltpu.VMEM((length, 2 * ff), bf16), pltpu.VMEM((length, step), f32)],
        compiler_params=pltpu.CompilerParams(vmem_limit_bytes=60 << 20),
        cost_estimate=pl.CostEstimate(
            flops=6 * length * ff * width,
            bytes_accessed=6 * ff * width,
            transcendentals=length * ff,
        ),
        name="feed_forward_backward",
    )(cot, *gate_up_parts, *gate_up_parts, full_down, full_gu)


def on_device(
    tokens,
    segments,
    attn_gain,
    w_query,
    w_key,
    w_value,
    query_gain,
    key_gain,
    w_out,
    mlp_gain,
    w_gate,
    w_up,
    w_down,
    cotangent,
):
    n, me = lax.axis_size("fsdp"), lax.axis_index("fsdp")
    tok_rows, width = tokens.shape[1], tokens.shape[2]
    length = segments.shape[1]
    heads, kv_heads = HEADS // n, KV_HEADS // n
    q_width, kv_width = heads * HEAD, kv_heads * HEAD
    ff = w_gate.shape[1] // n
    rows = width // n

    def block(value, k):
        return value[k * tok_rows : (k + 1) * tok_rows]

    def half_block(value, k, h):
        start = k * tok_rows + h * (tok_rows // 2)
        return value[start : start + tok_rows // 2]

    def by_columns(first, second):
        return with_layout_constraint(
            matmul_tn(first, second).astype(bf16), Layout(major_to_minor=(0, 1))
        )

    def by_rows(first, second):
        grad = with_layout_constraint(
            matmul_tn(first, second).astype(bf16), Layout(major_to_minor=(0, 1))
        )
        return grad.reshape(n, rows, second.shape[1])

    sizes = [attn_gain.shape[0], mlp_gain.shape[0], query_gain.shape[0], key_gain.shape[0]]
    packed = jnp.concatenate([attn_gain, mlp_gain, query_gain, key_gain])[None]
    tok, _, _ = gather(tokens[0])
    gains = [packed] + [swap(packed, "fsdp", k) for k in range(1, n)]
    index = jnp.concatenate(
        [(me ^ k) * tok_rows + jnp.arange(tok_rows, dtype=jnp.int32) for k in range(n)]
    )
    doc_ids = jnp.concatenate(
        [rows_of(segments[0], (me ^ k) * tok_rows, tok_rows) for k in range(n)]
    )
    earlier = jnp.sum((doc_ids[None, :] < doc_ids[:, None]).astype(jnp.int32), axis=1)
    position = index - earlier
    inverse = rope_base ** (-2.0 * jnp.arange(HEAD // 2).astype(f32) / HEAD)
    angles = position.astype(f32)[:, None] * inverse[None, :]
    cosine, sine = jnp.cos(angles), jnp.sin(angles)
    cos_table = jnp.concatenate([cosine, cosine], axis=1)
    sin_table = jnp.concatenate([-sine, sine], axis=1)
    first = earlier.reshape(n, 1, tok_rows)
    cos_table, sin_table, w_query, w_key, w_value, w_out = fence(
        cos_table, sin_table, w_query, w_key, w_value, w_out
    )
    attn_spread = Spread([w_query, w_key, w_value], [w_out])
    attn_got = attn_spread.begin()
    gains = jnp.concatenate(gains, axis=0)
    gains = jnp.concatenate(
        [lax.dynamic_slice_in_dim(gains, me ^ j, 1, axis=0) for j in range(n)], axis=0
    ).astype(f32)
    ends = [sum(sizes[: j + 1]) for j in range(4)]
    gain_attn = gains[:, : ends[0]].reshape(-1)
    gain_mlp = gains[:, ends[0] : ends[1]].reshape(-1)
    gain_query = gains[:, ends[1] : ends[2]].reshape(-1)
    gain_key = gains[:, ends[2] : ends[3]].reshape(-1)
    attn_got = jnp.stack(attn_got)
    attn_along, attn_across = swap(attn_got, "z", 1), core_swap(attn_got)
    whole = segments[0, 0] == 0
    tok, cos_table, sin_table, first, w_gate, w_up, whole = fence(
        tok, cos_table, sin_table, first, w_gate, w_up, whole
    )

    gu_spread = Spread([w_gate, w_up], [])
    gu_got = gu_spread.begin()
    attn_sources = [attn_got, attn_along, attn_across, core_swap(attn_along)]

    def normed_block(part):
        part = part.astype(f32)
        return (part * rms_scale(part) * gain_attn).astype(bf16)

    normed = jnp.concatenate([normed_block(part) for part in tok], axis=0)
    full_qkv = attn_spread.join_rows(attn_sources)
    qkv = matmul(normed, full_qkv)
    queries, keys, values, attended, lse = attention_forward(
        qkv, cos_table, sin_table, gain_query, gain_key, first, heads, kv_heads
    )
    full_out = attn_spread.join_columns(attn_sources)
    attended, full_out, gu_got, cotangent = fence(attended, full_out, gu_got, cotangent)
    cot = cotangent[0]

    gu_got = jnp.stack(gu_got)
    gu_along, gu_across = swap(gu_got, "z", 1), core_swap(gu_got)
    def out_part(k, h):
        return matmul(half_block(attended, k, h), full_out).astype(bf16)

    stream = tokens[0].astype(f32)
    middle = stream + scatter(out_part)
    mlp_scale = rms_scale(middle)
    normed_mine = (middle * mlp_scale * gain_mlp).astype(bf16)
    middle, mlp_scale, normed_mine, w_down, normed = fence(
        middle, mlp_scale, normed_mine, w_down, normed
    )

    normed_parts, _, _ = gather(normed_mine)
    down_spread = Spread([], [w_down])
    down_got = jnp.stack(down_spread.begin())
    normed_parts, gu_along, gu_across, cot, down_got = fence(
        normed_parts, gu_along, gu_across, cot, down_got
    )

    def gate_and_up(part):
        both = matmul(part, full_gu)
        gate, up = both[:, :ff], both[:, ff:]
        return both, (gate / (1.0 + jnp.exp(-gate)) * up).astype(bf16)

    full_gu = gu_spread.join_rows([gu_got, gu_along, gu_across, core_swap(gu_along)])

    down_along, down_across = swap(down_got, "z", 1), core_swap(down_got)
    own_act = gate_and_up(normed_parts[0])
    cot_parts, (own_act, full_gu, normed_parts), last = gather(
        cot, beside=(own_act, full_gu, normed_parts), last=normed_parts[n - 1]
    )
    acts = [own_act] + [gate_and_up(part) for part in [*normed_parts[1 : n - 1], last]]
    acts, down_along, down_across = fence(acts, down_along, down_across)
    normed_mlp = jnp.concatenate(normed_parts, axis=0)
    hidden = jnp.concatenate([act[1] for act in acts], axis=0)
    cot_all = jnp.concatenate(cot_parts, axis=0)
    full_down = down_spread.join_columns(
        [down_got, down_along, down_across, core_swap(down_along)]
    )
    cot_all, full_down, hidden, normed_mlp, acts = fence(
        cot_all, full_down, hidden, normed_mlp, acts
    )

    core = lax.axis_index("core")

    def down_grad(c):
        part = lax.dynamic_slice_in_dim(hidden, c * (ff // 2), ff // 2, axis=1)
        return by_columns(part, cot_all)

    down = Reduction(None)
    other, own = fence(core_swap(down_grad(1 - core)), down_grad(core))
    down.half = (own.astype(f32) + other.astype(f32)).astype(bf16)
    down.half, cot_all, full_down = fence(down.half, cot_all, full_down)

    def feed_forward_part():
        out_partial, cots = fence(matmul(hidden, full_down).astype(bf16), cot_all)
        out_got = scatter_direct(lambda k: block(out_partial, k))
        d_gate, d_up, d_normed_mlp = feed_forward_backward(
            cots, [act[0] for act in acts], full_down, full_gu
        )
        grad_gate, d_up, out_got = fence(by_rows(normed_mlp, d_gate), d_up, out_got)
        output = (middle + add_up(out_got)).astype(bf16)
        gate = Reduction(grad_gate)
        gate.begin()
        gate.exchange()
        up = Reduction(by_rows(normed_mlp, d_up))
        up.begin()
        return output, d_normed_mlp, gate.half, up.half

    down.half = lax.psum(down.half, "z")
    output, d_normed_mlp, gate_half, up_half = block_of_work(whole, feed_forward_part)
    down.half, output, d_normed_mlp, gate_half, up_half = fence(
        down.half, output, d_normed_mlp, gate_half, up_half
    )

    def attention_part():
        d_normed_mine = scatter(lambda k, h: half_block(d_normed_mlp, k, h))
        d_middle, mlp_gain_rows = norm_back(middle, mlp_scale, gain_mlp, d_normed_mine)
        mlp_gain_grad = jnp.sum(mlp_gain_rows, axis=0)
        d_middle = cot.astype(f32) + d_middle
        d_mine = d_middle.astype(bf16)
        d_branch = jnp.concatenate(gather(d_mine)[0], axis=0)
        d_attended = matmul_nt(d_branch, full_out).astype(bf16)
        d_attended, down_half = fence(d_attended, down.half)
        d_qkv, *head_gain_grads = attention_backward(
            qkv,
            queries,
            keys,
            values,
            lse,
            d_attended,
            cos_table,
            sin_table,
            gain_query,
            gain_key,
            first,
        )
        out_sum = Reduction(by_columns(attended, d_branch))
        out_sum.begin()
        out_sum.exchange()
        qkv_sum = Reduction(by_rows(normed, d_qkv))
        qkv_sum.begin()
        qkv_sum.exchange()
        down_sum = Reduction(None)
        down_sum.half = down_half
        down_sum.exchange()
        return (
            d_middle,
            mlp_gain_grad,
            matmul_nt(d_qkv, full_qkv).astype(bf16),
            head_gain_grads,
            out_sum.half,
            qkv_sum.half,
            down_sum.finish(False),
        )

    gate_half, up_half = lax.psum((gate_half, up_half), "z")
    gate_half, up_half, done = fence(gate_half, up_half, block_of_work(whole, attention_part))
    d_middle, mlp_gain_grad, partial, head_gain_grads, out_half, qkv_half, down_full = done

    def input_part():
        d_normed = scatter(lambda k, h: half_block(partial, k, h))
        gate, up = Reduction(None), Reduction(None)
        gate.half, up.half = gate_half, up_half
        up.exchange()
        d_normed, gate_full = fence(d_normed, gate.finish(True))
        stream = tokens[0].astype(f32)
        d_stream, attn_gain_rows = norm_back(stream, rms_scale(stream), gain_attn, d_normed)
        gain_grads = jnp.concatenate(
            [jnp.sum(attn_gain_rows, axis=0), mlp_gain_grad] + head_gain_grads
        )
        for axis in ("core", "fsdp", "z"):
            k = 1
            while k < lax.axis_size(axis):
                gain_grads = gain_grads + swap(gain_grads, axis, k)
                k *= 2
        shares, start = [], 0
        for size in sizes:
            shares.append(rows_of(gain_grads, start + me * size, size))
            start += n * size
        return shares, d_middle + d_stream, gate_full, up.finish(True)

    qkv_sum, out_sum = Reduction(None), Reduction(None)
    qkv_sum.half, out_sum.half = lax.psum((qkv_half, out_half), "z")
    qkv_sum.half, out_sum.half, done = fence(
        qkv_sum.half, out_sum.half, block_of_work(whole, input_part)
    )
    shares, input_grad, gate_full, up_full = done
    query_full, key_full, value_full = qkv_sum.finish(
        True, [q_width, kv_width, kv_width], split=True
    )
    return (
        output[None],
        input_grad[None],
        shares[0],
        query_full,
        key_full,
        value_full,
        shares[2],
        shares[3],
        out_sum.finish(False, split=True),
        shares[1],
        gate_full,
        up_full,
        down_full,
    )


def solution(mesh):
    n, replicas = mesh.shape["fsdp"], mesh.shape["dp"]
    split = Mesh(mesh.devices.reshape(n, replicas // 2, 2), ("fsdp", "z", "core"))
    dp = ("z", "core")
    in_specs = (
        P(dp, "fsdp", None),
        P(dp, None),
        P("fsdp"),
        P("fsdp", None),
        P("fsdp", None),
        P("fsdp", None),
        P("fsdp"),
        P("fsdp"),
        P(None, "fsdp"),
        P("fsdp"),
        P("fsdp", None),
        P("fsdp", None),
        P(None, "fsdp"),
        P(dp, "fsdp", None),
    )
    out_specs = (
        P(dp, "fsdp", None),
        P(dp, "fsdp", None),
        P("fsdp"),
        P("fsdp", None),
        P("fsdp", None),
        P("fsdp", None),
        P("fsdp"),
        P("fsdp"),
        P(None, "fsdp"),
        P("fsdp"),
        P("fsdp", None),
        P("fsdp", None),
        P(None, "fsdp"),
    )
    return jax.shard_map(
        on_device, mesh=split, in_specs=in_specs, out_specs=out_specs, check_vma=False
    )
```

```python
import math

import jax
import jax.numpy as jnp
from jax import lax
from jax.experimental import pallas as pl
from jax.experimental.layout import Layout, with_layout_constraint
from jax.experimental.pallas import tpu as pltpu
from jax.sharding import Mesh
from jax.sharding import PartitionSpec as P

HEADS = 16
KV_HEADS = 8
HEAD = 128
GROUP = HEADS // KV_HEADS

epsilon = 1e-06
rope_base = 1000000.0
masked_score = -1e30
score_scale = 1.0 / math.sqrt(HEAD)

bf16 = jnp.bfloat16
f32 = jnp.float32


def matmul(first, second):
    return jnp.dot(first, second, preferred_element_type=f32)


def matmul_tn(first, second):
    return lax.dot_general(first, second, (((0,), (0,)), ((), ())), preferred_element_type=f32)


def matmul_nt(first, second):
    return lax.dot_general(first, second, (((1,), (1,)), ((), ())), preferred_element_type=f32)


def rms_scale(vector):
    return lax.rsqrt(jnp.mean(vector * vector, axis=-1, keepdims=True) + epsilon)


def norm_back(vector, scale, gain, incoming):
    scaled = gain * incoming
    d_vector = scale * scaled - vector * (scale**3) * jnp.mean(
        vector * scaled, axis=-1, keepdims=True
    )
    return d_vector, incoming * vector * scale


def swap(value, axis, k):
    return lax.ppermute(value, axis, [(j, j ^ k) for j in range(lax.axis_size(axis))])


def core_swap(value):
    return swap(value, "core", 1)


def rows_of(value, start, size):
    return lax.dynamic_slice_in_dim(value, start, size, axis=0)


def fence(*trees):
    leaves, shape = jax.tree.flatten(trees)
    return jax.tree.unflatten(shape, lax.optimization_barrier(leaves))


def block_of_work(whole, body):
    shapes = jax.eval_shape(body)
    return lax.cond(
        whole,
        body,
        lambda: jax.tree.map(lambda leaf: jnp.zeros(leaf.shape, leaf.dtype), shapes),
    )


def gather(shard, beside=None, last=None):
    n = lax.axis_size("fsdp")
    if n != 4:
        return fence([shard] + [swap(shard, "fsdp", k) for k in range(1, n)], beside, last)
    half = shard.shape[0] // 2
    top, low = shard[:half], shard[half:]
    x_top, y_low = swap(top, "fsdp", 1), swap(low, "fsdp", 2)
    x_low, y_top = swap(low, "fsdp", 1), swap(top, "fsdp", 2)
    x_top, y_low, beside = fence(x_top, y_low, beside)
    far = [swap(x_top, "fsdp", 2), swap(y_low, "fsdp", 1)]
    if last is not None:
        far, last = fence(far, last)
    blocks = [
        shard,
        jnp.concatenate([x_top, x_low], axis=0),
        jnp.concatenate([y_top, y_low], axis=0),
        jnp.concatenate(far, axis=0),
    ]
    return blocks, beside, last


def scatter(part_of):
    n = lax.axis_size("fsdp")
    if n != 4:
        halves = []
        for h in range(2):
            total = part_of(0, h).astype(f32)
            for k in range(1, n):
                total = total + swap(part_of(k, h), "fsdp", k).astype(f32)
            halves.append(total)
        return jnp.concatenate(halves, axis=0)
    from_x, from_y = swap(part_of(3, 0), "fsdp", 1), swap(part_of(3, 1), "fsdp", 2)
    x_top, y_low = swap(part_of(1, 0), "fsdp", 1), swap(part_of(2, 1), "fsdp", 2)
    low = (part_of(1, 1).astype(f32) + from_y.astype(f32)).astype(bf16)
    top = (part_of(2, 0).astype(f32) + from_x.astype(f32)).astype(bf16)
    x_low, y_top = swap(low, "fsdp", 1), swap(top, "fsdp", 2)
    return jnp.concatenate(
        [
            part_of(0, 0).astype(f32) + x_top.astype(f32) + y_top.astype(f32),
            part_of(0, 1).astype(f32) + x_low.astype(f32) + y_low.astype(f32),
        ],
        axis=0,
    )


def scatter_direct(block_of):
    n = lax.axis_size("fsdp")
    got = {k: swap(block_of(k), "fsdp", k) for k in range(n - 1, 0, -1)}
    return [block_of(0)] + [got[k] for k in range(1, n)]


def add_up(blocks):
    total = blocks[0].astype(f32)
    for block in blocks[1:]:
        total = total + block.astype(f32)
    return total


def assemble(shape, sources, pieces):
    count, held = len(pieces), len(sources)

    def kernel(place_ref, *refs):
        ins, out, hold = refs[:held], refs[held], refs[held + 1]
        sem_in, sem_out = refs[held + 2], refs[held + 3]

        def window(ref, k, first):
            size = pieces[k][2]
            row = pl.multiple_of(place_ref[4 * k + first], 16)
            column = pl.multiple_of(place_ref[4 * k + first + 1], 128)
            return ref.at[pl.ds(row, size[0]), pl.ds(column, size[1])]

        def source(k):
            ref, lead = ins[pieces[k][0]], pieces[k][1]
            return window(ref if lead is None else ref.at[lead], k, 0)

        loads = [
            pltpu.make_async_copy(source(k), window(hold, k, 2), sem_in.at[k])
            for k in range(count)
        ]
        stores = [
            pltpu.make_async_copy(window(hold, k, 2), window(out, k, 2), sem_out.at[k])
            for k in range(count)
        ]
        for load in loads:
            load.start()
        for load, store in zip(loads, stores):
            load.wait()
            store.start()
        for store in stores:
            store.wait()

    size = 2 * math.prod(shape)
    places = [jnp.int32(v) for piece in pieces for at in piece[3:] for v in at]
    return pl.pallas_call(
        kernel,
        out_shape=jax.ShapeDtypeStruct(shape, bf16),
        in_specs=[pl.BlockSpec(memory_space=pltpu.SMEM)]
        + [
            pl.BlockSpec(memory_space=pl.ANY if source.ndim == 3 else pltpu.HBM)
            for source in sources
        ],
        out_specs=pl.BlockSpec(memory_space=pl.ANY),
        scratch_shapes=[
            pltpu.VMEM(shape, bf16),
            pltpu.SemaphoreType.DMA((count,)),
            pltpu.SemaphoreType.DMA((count,)),
        ],
        compiler_params=pltpu.CompilerParams(vmem_limit_bytes=size + (4 << 20)),
        cost_estimate=pl.CostEstimate(flops=0, bytes_accessed=2 * size, transcendentals=0),
        name="assemble",
    )(jnp.stack(places), *sources)


class Spread:
    def __init__(self, by_rows, by_columns, along_z=True):
        self.by_rows, self.by_columns, self.along_z = by_rows, by_columns, along_z
        self.shares = 4 if along_z else 2

    def share(self, j, q):
        n = lax.axis_size("fsdp")
        cuts = []
        for part in self.by_rows:
            size, width = part.shape[0] // self.shares, part.shape[1] // n
            cuts.append(lax.dynamic_slice(part, (q * size, j * width), (size, width)))
        for part in self.by_columns:
            rows = part.shape[0] // n
            size = rows // self.shares
            cuts.append(rows_of(part, j * rows + q * size, size))
        return cuts[0] if len(cuts) == 1 else jnp.concatenate(cuts, axis=1)

    def begin(self):
        n, me = lax.axis_size("fsdp"), lax.axis_index("fsdp")
        mine = lax.axis_index("core")
        if self.along_z:
            mine = 2 * (lax.axis_index("z") % 2) + mine
        return [swap(self.share(me ^ k, mine), "fsdp", k) for k in range(1, n)]

    def pieces(self, sources):
        n, me = lax.axis_size("fsdp"), lax.axis_index("fsdp")
        side, core = lax.axis_index("z") % 2, lax.axis_index("core")
        shares = [core, 1 - core]
        if self.along_z:
            shares = [
                2 * side + core,
                2 * (1 - side) + core,
                2 * side + 1 - core,
                2 * (1 - side) + 1 - core,
            ]
        return [
            (source, k, me ^ k, shares[source])
            for k in range(1, n)
            for source in range(len(sources))
        ]

    def join_rows(self, sources):
        n, me = lax.axis_size("fsdp"), lax.axis_index("fsdp")
        rows = self.by_rows[0].shape[0]
        widths = [part.shape[1] // n for part in self.by_rows]
        total, size = sum(widths), rows // self.shares
        pieces = [
            (source, k - 1, (size, total), (0, 0), (j * rows + q * size, 0))
            for source, k, j, q in self.pieces(sources)
        ]
        start = 0
        for index, width in enumerate(widths):
            pieces.append(
                (len(sources) + index, None, (rows, width), (0, me * width), (me * rows, start))
            )
            start += width
        return assemble((n * rows, total), [*sources, *self.by_rows], pieces)

    def join_columns(self, sources):
        n, me = lax.axis_size("fsdp"), lax.axis_index("fsdp")
        start = sum(part.shape[1] // n for part in self.by_rows)
        (part,) = self.by_columns
        rows, width = part.shape[0] // n, part.shape[1]
        size = rows // self.shares
        pieces = [
            (source, k - 1, (size, width), (0, start), (q * size, j * width))
            for source, k, j, q in self.pieces(sources)
        ]
        pieces.append((len(sources), None, (rows, width), (me * rows, 0), (0, me * width)))
        return assemble((rows, n * width), [*sources, part], pieces)


class Reduction:
    def __init__(self, grad):
        self.grad = grad

    def begin(self):
        core = lax.axis_index("core")
        axis = self.grad.ndim - 2
        rows = self.grad.shape[axis] // 2

        def take(c):
            return lax.dynamic_slice_in_dim(self.grad, c * rows, rows, axis=axis)

        both = take(core).astype(f32) + core_swap(take(1 - core)).astype(f32)
        self.half = both.astype(bf16)

    def exchange(self):
        n, me = lax.axis_size("fsdp"), lax.axis_index("fsdp")

        def part(j):
            if self.half.ndim == 2:
                width = self.half.shape[1] // n
                return lax.dynamic_slice_in_dim(self.half, j * width, width, axis=1)
            return lax.dynamic_index_in_dim(self.half, j, 0, keepdims=False)

        self.half = jnp.stack(
            [part(me)] + [swap(part(me ^ k), "fsdp", k) for k in range(1, n)]
        )

    def finish(self, by_rows, sizes=None, split=False):
        n, me = lax.axis_size("fsdp"), lax.axis_index("fsdp")
        core = lax.axis_index("core")
        other = core_swap(self.half)
        rows, width = self.half.shape[1:]
        sizes = [width] if sizes is None else sizes
        count = len(sizes)
        place = jnp.stack([me, core]).astype(jnp.int32)

        def write(ref, outs):
            start = 0
            for out, size in zip(outs, sizes):
                out[...] = ref[0, :, start : start + size].astype(f32)
                start += size

        def out_at(w, k, place):
            source = place[0] ^ k
            side = jnp.where(w == 0, place[1], 1 - place[1])
            return (side, source) if by_rows else (source * 2 + side, 0)

        def call(kernel, grid, in_specs, out_index, aliases, operands):
            return pl.pallas_call(
                kernel,
                out_shape=[
                    jax.ShapeDtypeStruct(
                        (2 * rows, n * size) if by_rows else (2 * n * rows, size), f32
                    )
                    for size in sizes
                ],
                grid_spec=pltpu.PrefetchScalarGridSpec(
                    num_scalar_prefetch=1,
                    grid=grid,
                    in_specs=in_specs,
                    out_specs=[pl.BlockSpec((rows, size), out_index) for size in sizes],
                ),
                input_output_aliases=aliases,
                compiler_params=pltpu.CompilerParams(vmem_limit_bytes=32 << 20),
                cost_estimate=pl.CostEstimate(
                    flops=0, bytes_accessed=math.prod(grid) * rows * width * 6, transcendentals=0
                ),
                name="place",
            )(place, *operands)

        if split:
            one = pl.BlockSpec((1, rows, width), lambda k, place: (k, 0, 0))

            def own(place, mine, *outs):
                write(mine, outs)

            def rest(place, other, *refs):
                write(other, refs[count:])

            result = call(own, (n,), [one], lambda k, place: out_at(0, k, place), {}, [self.half])
            result = call(
                rest,
                (n,),
                [one] + [pl.BlockSpec(memory_space=pl.ANY)] * count,
                lambda k, place: out_at(1, k, place),
                {2 + i: i for i in range(count)},
                [other, *result],
            )
        else:

            def both(place, mine, other, *outs):
                @pl.when(pl.program_id(0) == 0)
                def _():
                    write(mine, outs)

                @pl.when(pl.program_id(0) == 1)
                def _():
                    write(other, outs)

            result = call(
                both,
                (2, n),
                [
                    pl.BlockSpec(
                        (1, rows, width),
                        lambda w, k, place: (jnp.where(w == 0, k, n - 1), 0, 0),
                    ),
                    pl.BlockSpec(
                        (1, rows, width), lambda w, k, place: (jnp.where(w == 0, 0, k), 0, 0)
                    ),
                ],
                out_at,
                {},
                [self.half, other],
            )
        return result if count > 1 else result[0]


def roll_half(value):
    return pltpu.roll(value, HEAD // 2, axis=1)


def attention_specs(length, heads, kv_heads):
    wide, tall = GROUP * HEAD, heads
    return dict(
        queries=pl.BlockSpec((length, wide), lambda g, me: (0, g)),
        head=pl.BlockSpec((length, HEAD), lambda g, me: (0, g)),
        keys_in=pl.BlockSpec((length, HEAD), lambda g, me: (0, tall + g)),
        values_in=pl.BlockSpec((length, HEAD), lambda g, me: (0, tall + kv_heads + g)),
        table=pl.BlockSpec((length, HEAD), lambda g, me: (0, 0)),
        gain=pl.BlockSpec((1, HEAD), lambda g, me: (0, 0)),
        gain_out=pl.BlockSpec((1, 1, HEAD), lambda g, me: (g, 0, 0)),
    )


def attention_forward(qkv, cos_table, sin_table, gain_query, gain_key, first, heads, kv_heads):
    length = qkv.shape[0]
    n, _, size = first.shape

    def kernel(
        me_ref, q_ref, k_ref, v_ref, cos_ref, sin_ref, qg_ref, kg_ref, first_ref,
        queries_ref, keys_ref, values_ref, attended_ref, lse_ref, vt_ref,
    ):
        me = me_ref[0]

        def rows(block):
            return pl.ds(pl.multiple_of((block ^ me) * size, size), size)

        def prepare(raw, gain):
            normed = raw * rms_scale(raw) * gain
            return (normed * cos_ref[...] + roll_half(normed) * sin_ref[...]).astype(bf16)

        keys_ref[...] = prepare(k_ref[...], kg_ref[...])
        values_ref[...] = v_ref[...].astype(bf16)
        for k in range(n):
            vt_ref[k] = v_ref[k * size : (k + 1) * size, :].T.astype(bf16)
        for h in range(GROUP):
            columns = slice(h * HEAD, (h + 1) * HEAD)
            queries_ref[:, columns] = prepare(q_ref[:, columns], qg_ref[...])
        inside = lax.broadcasted_iota(jnp.int32, (size, size), 0) <= lax.broadcasted_iota(
            jnp.int32, (size, size), 1
        )
        place = lax.broadcasted_iota(jnp.int32, (size, size), 0)
        for h in range(GROUP):
            columns = slice(h * HEAD, (h + 1) * HEAD)
            for i in range(n):
                query = queries_ref[rows(i), columns]
                begin = first_ref[i ^ me]
                total = jnp.zeros((1, size), f32)
                out = jnp.zeros((HEAD, size), f32)
                for j in range(i + 1):
                    scores = matmul_nt(keys_ref[rows(j), :], query) * score_scale
                    allowed = place >= begin - j * size
                    if i == j:
                        allowed = allowed & inside
                    weight = jnp.where(allowed, jnp.exp(scores), 0.0)
                    total = total + jnp.sum(weight, axis=0, keepdims=True)
                    out = out + matmul(vt_ref[j ^ me], weight.astype(bf16))
                attended_ref[rows(i), columns] = (out / total).T.astype(bf16)
                lse_ref[0, h, i ^ me] = jnp.log(total)

    spec = attention_specs(length, heads, kv_heads)
    me = lax.axis_index("fsdp").reshape(1).astype(jnp.int32)
    return pl.pallas_call(
        kernel,
        out_shape=[
            jax.ShapeDtypeStruct((length, heads * HEAD), bf16),
            jax.ShapeDtypeStruct((length, kv_heads * HEAD), bf16),
            jax.ShapeDtypeStruct((length, kv_heads * HEAD), bf16),
            jax.ShapeDtypeStruct((length, heads * HEAD), bf16),
            jax.ShapeDtypeStruct((kv_heads, GROUP, n, 1, size), f32),
        ],
        grid_spec=pltpu.PrefetchScalarGridSpec(
            num_scalar_prefetch=1,
            grid=(kv_heads,),
            in_specs=[
                spec["queries"],
                spec["keys_in"],
                spec["values_in"],
                spec["table"],
                spec["table"],
                spec["gain"],
                spec["gain"],
                pl.BlockSpec((n, 1, size), lambda g, me: (0, 0, 0)),
            ],
            out_specs=[
                spec["queries"],
                spec["head"],
                spec["head"],
                spec["queries"],
                pl.BlockSpec((1, GROUP, n, 1, size), lambda g, me: (g, 0, 0, 0, 0)),
            ],
            scratch_shapes=[pltpu.VMEM((n, HEAD, size), bf16)],
        ),
        compiler_params=pltpu.CompilerParams(vmem_limit_bytes=48 << 20),
        cost_estimate=pl.CostEstimate(
            flops=4 * heads * length * length * HEAD,
            bytes_accessed=12 * length * heads * HEAD,
            transcendentals=heads * length * length,
        ),
        name="attention_forward",
    )(me, qkv, qkv, qkv, cos_table, sin_table, gain_query[None], gain_key[None], first)


def attention_backward(
    qkv, queries, keys, values, lse, d_attended, cos_table, sin_table, gain_query, gain_key, first
):
    length = qkv.shape[0]
    n, _, size = first.shape
    heads, kv_heads = queries.shape[1] // HEAD, keys.shape[1] // HEAD

    def kernel(
        me_ref, qr_ref, kr_ref, q_ref, k_ref, v_ref, lse_ref, da_ref, cos_ref, sin_ref,
        qg_ref, kg_ref, first_ref, dq_ref, dk_ref, dv_ref, dqg_ref, dkg_ref,
        kt_ref, probs_ref, dp_ref, dq_acc, dk_acc, dv_acc,
    ):
        me = me_ref[0]

        def rows(block):
            return pl.ds(pl.multiple_of((block ^ me) * size, size), size)

        def finish(raw, gain, incoming):
            turned = incoming * cos_ref[...] - roll_half(incoming) * sin_ref[...]
            d_raw, d_gain = norm_back(raw, rms_scale(raw), gain, turned)
            return d_raw.astype(bf16), jnp.sum(d_gain, axis=0, keepdims=True)

        for k in range(n):
            part = k_ref[k * size : (k + 1) * size, :].astype(f32)
            kt_ref[k] = part.T.astype(bf16)
        dk_acc[...] = jnp.zeros_like(dk_acc)
        dv_acc[...] = jnp.zeros_like(dv_acc)
        inside = lax.broadcasted_iota(jnp.int32, (size, size), 0) <= lax.broadcasted_iota(
            jnp.int32, (size, size), 1
        )
        place = lax.broadcasted_iota(jnp.int32, (size, size), 0)
        gain_total = jnp.zeros((1, HEAD), f32)
        for h in range(GROUP):
            columns = slice(h * HEAD, (h + 1) * HEAD)
            for i in range(n):
                query, d_out = q_ref[rows(i), columns], da_ref[rows(i), columns]
                begin, shift = first_ref[i ^ me], lse_ref[0, h, i ^ me]
                dots = jnp.zeros((1, size), f32)
                for j in range(i + 1):
                    scores = matmul_nt(k_ref[rows(j), :], query) * score_scale
                    allowed = place >= begin - j * size
                    if i == j:
                        allowed = allowed & inside
                    probs = jnp.where(allowed, jnp.exp(scores - shift), 0.0)
                    d_probs = matmul_nt(v_ref[rows(j), :], d_out)
                    dots = dots + jnp.sum(probs * d_probs, axis=0, keepdims=True)
                    probs_ref[j] = probs
                    dp_ref[j] = d_probs
                d_query = jnp.zeros((HEAD, size), f32)
                for j in range(i + 1):
                    probs = probs_ref[j]
                    d_scores = (probs * (dp_ref[j] - dots)).astype(bf16)
                    d_query = d_query + matmul(kt_ref[j ^ me], d_scores)
                    dk_acc[rows(j), :] += matmul(d_scores, query)
                    dv_acc[rows(j), :] += matmul(probs.astype(bf16), d_out)
                dq_acc[rows(i), :] = d_query.T * score_scale
            d_raw, d_gain = finish(qr_ref[:, columns], qg_ref[...], dq_acc[...])
            dq_ref[:, columns] = d_raw
            gain_total = gain_total + d_gain
        dqg_ref[0] = gain_total
        d_raw, d_gain = finish(kr_ref[...], kg_ref[...], dk_acc[...] * score_scale)
        dk_ref[...] = d_raw
        dkg_ref[0] = d_gain
        dv_ref[...] = dv_acc[...].astype(bf16)

    spec = attention_specs(length, heads, kv_heads)
    me = lax.axis_index("fsdp").reshape(1).astype(jnp.int32)
    d_query, d_key, d_value, d_query_gain, d_key_gain = pl.pallas_call(
        kernel,
        out_shape=[
            jax.ShapeDtypeStruct((length, heads * HEAD), bf16),
            jax.ShapeDtypeStruct((length, kv_heads * HEAD), bf16),
            jax.ShapeDtypeStruct((length, kv_heads * HEAD), bf16),
            jax.ShapeDtypeStruct((kv_heads, 1, HEAD), f32),
            jax.ShapeDtypeStruct((kv_heads, 1, HEAD), f32),
        ],
        grid_spec=pltpu.PrefetchScalarGridSpec(
            num_scalar_prefetch=1,
            grid=(kv_heads,),
            in_specs=[
                spec["queries"],
                spec["keys_in"],
                spec["queries"],
                spec["head"],
                spec["head"],
                pl.BlockSpec((1, GROUP, n, 1, size), lambda g, me: (g, 0, 0, 0, 0)),
                spec["queries"],
                spec["table"],
                spec["table"],
                spec["gain"],
                spec["gain"],
                pl.BlockSpec((n, 1, size), lambda g, me: (0, 0, 0)),
            ],
            out_specs=[
                spec["queries"],
                spec["head"],
                spec["head"],
                spec["gain_out"],
                spec["gain_out"],
            ],
            scratch_shapes=[
                pltpu.VMEM((n, HEAD, size), bf16),
                pltpu.VMEM((n, size, size), f32),
                pltpu.VMEM((n, size, size), f32),
                pltpu.VMEM((length, HEAD), f32),
                pltpu.VMEM((length, HEAD), f32),
                pltpu.VMEM((length, HEAD), f32),
            ],
        ),
        compiler_params=pltpu.CompilerParams(vmem_limit_bytes=48 << 20),
        cost_estimate=pl.CostEstimate(
            flops=10 * heads * length * length * HEAD,
            bytes_accessed=20 * length * heads * HEAD,
            transcendentals=heads * length * length,
        ),
        name="attention_backward",
    )(
        me, qkv, qkv, queries, keys, values, lse, d_attended, cos_table, sin_table,
        gain_query[None], gain_key[None], first,
    )
    return (
        jnp.concatenate([d_query, d_key, d_value], axis=1),
        jnp.sum(d_query_gain, axis=(0, 1)),
        jnp.sum(d_key_gain, axis=(0, 1)),
    )


def feed_forward_backward(cot, gate_up_parts, full_down, full_gu):
    n = len(gate_up_parts)
    length, width = cot.shape
    size = length // n
    ff = full_down.shape[0]
    step = 512 if ff % 512 == 0 else 256
    first = ff // step
    tile = 256

    def kernel(cot_ref, *refs):
        gates, ups = refs[:n], refs[n : 2 * n]
        down, wgu, d_gate_ref, d_up_ref, out_ref, both, d_hidden_ref = refs[2 * n :]
        f = pl.program_id(0)

        @pl.when(f < first)
        def _():
            d_hidden_ref[...] = matmul_nt(cot_ref[...], down[...])
            for k in range(n):
                rows = slice(k * size, (k + 1) * size)
                d_hidden = d_hidden_ref[rows, :]
                gate, up = gates[k][...].astype(f32), ups[k][...].astype(f32)
                sg = 1.0 / (1.0 + jnp.exp(-gate))
                d_gate = (d_hidden * up * sg * (1.0 + gate * (1.0 - sg))).astype(bf16)
                d_up = (d_hidden * gate * sg).astype(bf16)
                d_gate_ref[rows, :] = d_gate
                d_up_ref[rows, :] = d_up
                at = pl.multiple_of(f * step, step)
                both[rows, pl.ds(at, step)] = d_gate
                both[rows, pl.ds(ff + at, step)] = d_up

        @pl.when(f >= first)
        def _():
            out_ref[...] = matmul_nt(both[...], wgu[...]).astype(bf16)

    once = pl.Buffered(1)

    def early(f):
        return jnp.minimum(f, first - 1)

    def late(f):
        return jnp.maximum(f - first, 0)

    return pl.pallas_call(
        kernel,
        out_shape=[
            jax.ShapeDtypeStruct((length, ff), bf16),
            jax.ShapeDtypeStruct((length, ff), bf16),
            jax.ShapeDtypeStruct((length, width), bf16),
        ],
        grid=(first + width // tile,),
        in_specs=[pl.BlockSpec((length, width), lambda f: (0, 0), pipeline_mode=once)]
        + [pl.BlockSpec((size, step), lambda f: (0, early(f)))] * n
        + [pl.BlockSpec((size, step), lambda f: (0, first + early(f)))] * n
        + [
            pl.BlockSpec((step, width), lambda f: (early(f), 0)),
            pl.BlockSpec((tile, 2 * ff), lambda f: (late(f), 0)),
        ],
        out_specs=[
            pl.BlockSpec((length, step), lambda f: (0, early(f))),
            pl.BlockSpec((length, step), lambda f: (0, early(f))),
            pl.BlockSpec((length, tile), lambda f: (0, late(f))),
        ],
        scratch_shapes=[pltpu.VMEM((length, 2 * ff), bf16), pltpu.VMEM((length, step), f32)],
        compiler_params=pltpu.CompilerParams(vmem_limit_bytes=60 << 20),
        cost_estimate=pl.CostEstimate(
            flops=6 * length * ff * width,
            bytes_accessed=6 * ff * width,
            transcendentals=length * ff,
        ),
        name="feed_forward_backward",
    )(cot, *gate_up_parts, *gate_up_parts, full_down, full_gu)


def on_device(
    tokens,
    segments,
    attn_gain,
    w_query,
    w_key,
    w_value,
    query_gain,
    key_gain,
    w_out,
    mlp_gain,
    w_gate,
    w_up,
    w_down,
    cotangent,
):
    n, me = lax.axis_size("fsdp"), lax.axis_index("fsdp")
    tok_rows, width = tokens.shape[1], tokens.shape[2]
    length = segments.shape[1]
    heads, kv_heads = HEADS // n, KV_HEADS // n
    q_width, kv_width = heads * HEAD, kv_heads * HEAD
    ff = w_gate.shape[1] // n
    rows = width // n

    def block(value, k):
        return value[k * tok_rows : (k + 1) * tok_rows]

    def half_block(value, k, h):
        start = k * tok_rows + h * (tok_rows // 2)
        return value[start : start + tok_rows // 2]

    def by_columns(first, second):
        return with_layout_constraint(
            matmul_tn(first, second).astype(bf16), Layout(major_to_minor=(0, 1))
        )

    def by_rows(first, second):
        grad = with_layout_constraint(
            matmul_tn(first, second).astype(bf16), Layout(major_to_minor=(0, 1))
        )
        return grad.reshape(n, rows, second.shape[1])

    sizes = [attn_gain.shape[0], mlp_gain.shape[0], query_gain.shape[0], key_gain.shape[0]]
    packed = jnp.concatenate([attn_gain, mlp_gain, query_gain, key_gain])[None]
    tok, _, _ = gather(tokens[0])
    gains = [packed] + [swap(packed, "fsdp", k) for k in range(1, n)]
    index = jnp.concatenate(
        [(me ^ k) * tok_rows + jnp.arange(tok_rows, dtype=jnp.int32) for k in range(n)]
    )
    doc_ids = jnp.concatenate(
        [rows_of(segments[0], (me ^ k) * tok_rows, tok_rows) for k in range(n)]
    )
    earlier = jnp.sum((doc_ids[None, :] < doc_ids[:, None]).astype(jnp.int32), axis=1)
    position = index - earlier
    inverse = rope_base ** (-2.0 * jnp.arange(HEAD // 2).astype(f32) / HEAD)
    angles = position.astype(f32)[:, None] * inverse[None, :]
    cosine, sine = jnp.cos(angles), jnp.sin(angles)
    cos_table = jnp.concatenate([cosine, cosine], axis=1)
    sin_table = jnp.concatenate([-sine, sine], axis=1)
    first = earlier.reshape(n, 1, tok_rows)
    cos_table, sin_table, w_query, w_key, w_value, w_out = fence(
        cos_table, sin_table, w_query, w_key, w_value, w_out
    )
    attn_spread = Spread([w_query, w_key, w_value], [w_out])
    attn_got = attn_spread.begin()
    gains = jnp.concatenate(gains, axis=0)
    gains = jnp.concatenate(
        [lax.dynamic_slice_in_dim(gains, me ^ j, 1, axis=0) for j in range(n)], axis=0
    ).astype(f32)
    ends = [sum(sizes[: j + 1]) for j in range(4)]
    gain_attn = gains[:, : ends[0]].reshape(-1)
    gain_mlp = gains[:, ends[0] : ends[1]].reshape(-1)
    gain_query = gains[:, ends[1] : ends[2]].reshape(-1)
    gain_key = gains[:, ends[2] : ends[3]].reshape(-1)
    attn_got = jnp.stack(attn_got)
    attn_along, attn_across = swap(attn_got, "z", 1), core_swap(attn_got)
    whole = segments[0, 0] == 0
    tok, cos_table, sin_table, first, w_gate, w_up, whole = fence(
        tok, cos_table, sin_table, first, w_gate, w_up, whole
    )

    gu_spread = Spread([w_gate, w_up], [])
    gu_got = gu_spread.begin()
    attn_sources = [attn_got, attn_along, attn_across, core_swap(attn_along)]

    def normed_block(part):
        part = part.astype(f32)
        return (part * rms_scale(part) * gain_attn).astype(bf16)

    normed = jnp.concatenate([normed_block(part) for part in tok], axis=0)
    full_qkv = attn_spread.join_rows(attn_sources)
    qkv = matmul(normed, full_qkv)
    queries, keys, values, attended, lse = attention_forward(
        qkv, cos_table, sin_table, gain_query, gain_key, first, heads, kv_heads
    )
    full_out = attn_spread.join_columns(attn_sources)
    attended, full_out, gu_got, cotangent = fence(attended, full_out, gu_got, cotangent)
    cot = cotangent[0]

    gu_got = jnp.stack(gu_got)
    gu_along, gu_across = swap(gu_got, "z", 1), core_swap(gu_got)
    def out_part(k, h):
        return matmul(half_block(attended, k, h), full_out).astype(bf16)

    stream = tokens[0].astype(f32)
    middle = stream + scatter(out_part)
    mlp_scale = rms_scale(middle)
    normed_mine = (middle * mlp_scale * gain_mlp).astype(bf16)
    middle, mlp_scale, normed_mine, w_down, normed = fence(
        middle, mlp_scale, normed_mine, w_down, normed
    )

    normed_parts, _, _ = gather(normed_mine)
    down_spread = Spread([], [w_down])
    down_got = jnp.stack(down_spread.begin())
    normed_parts, gu_along, gu_across, cot, down_got = fence(
        normed_parts, gu_along, gu_across, cot, down_got
    )

    def gate_and_up(part):
        both = matmul(part, full_gu)
        gate, up = both[:, :ff], both[:, ff:]
        return both, (gate / (1.0 + jnp.exp(-gate)) * up).astype(bf16)

    full_gu = gu_spread.join_rows([gu_got, gu_along, gu_across, core_swap(gu_along)])

    down_along, down_across = swap(down_got, "z", 1), core_swap(down_got)
    own_act = gate_and_up(normed_parts[0])
    cot_parts, (own_act, full_gu, normed_parts), last = gather(
        cot, beside=(own_act, full_gu, normed_parts), last=normed_parts[n - 1]
    )
    acts = [own_act] + [gate_and_up(part) for part in [*normed_parts[1 : n - 1], last]]
    acts, down_along, down_across = fence(acts, down_along, down_across)
    normed_mlp = jnp.concatenate(normed_parts, axis=0)
    hidden = jnp.concatenate([act[1] for act in acts], axis=0)
    cot_all = jnp.concatenate(cot_parts, axis=0)
    down_last = core_swap(down_along)
    cot_all, down_across, down_last, hidden, normed_mlp, acts = fence(
        cot_all, down_across, down_last, hidden, normed_mlp, acts
    )

    core = lax.axis_index("core")

    def down_grad(c):
        part = lax.dynamic_slice_in_dim(hidden, c * (ff // 2), ff // 2, axis=1)
        return by_columns(part, cot_all)

    down = Reduction(None)
    other, own = fence(core_swap(down_grad(1 - core)), down_grad(core))
    down.half = (own.astype(f32) + other.astype(f32)).astype(bf16)
    down.half, cot_all = fence(down.half, cot_all)

    def feed_forward_part():
        full_down = down_spread.join_columns([down_got, down_along, down_across, down_last])
        out_partial, cots = fence(matmul(hidden, full_down).astype(bf16), cot_all)
        out_got = scatter_direct(lambda k: block(out_partial, k))
        d_gate, d_up, d_normed_mlp = feed_forward_backward(
            cots, [act[0] for act in acts], full_down, full_gu
        )
        grad_gate, d_up, out_got = fence(by_rows(normed_mlp, d_gate), d_up, out_got)
        gate = Reduction(grad_gate)
        gate.begin()
        gate.exchange()
        up = Reduction(by_rows(normed_mlp, d_up))
        up.begin()
        return out_got, d_normed_mlp, gate.half, up.half

    down.half = lax.psum(down.half, "z")
    out_got, d_normed_mlp, gate_half, up_half = block_of_work(whole, feed_forward_part)
    down.half, out_got, d_normed_mlp, gate_half, up_half = fence(
        down.half, out_got, d_normed_mlp, gate_half, up_half
    )

    def attention_part():
        d_normed_mine = scatter(lambda k, h: half_block(d_normed_mlp, k, h))
        d_middle, mlp_gain_rows = norm_back(middle, mlp_scale, gain_mlp, d_normed_mine)
        mlp_gain_grad = jnp.sum(mlp_gain_rows, axis=0)
        d_middle = cot.astype(f32) + d_middle
        d_mine = d_middle.astype(bf16)
        d_branch = jnp.concatenate(gather(d_mine)[0], axis=0)
        d_attended = matmul_nt(d_branch, full_out).astype(bf16)
        d_attended, down_half = fence(d_attended, down.half)
        d_qkv, *head_gain_grads = attention_backward(
            qkv,
            queries,
            keys,
            values,
            lse,
            d_attended,
            cos_table,
            sin_table,
            gain_query,
            gain_key,
            first,
        )
        out_sum = Reduction(by_columns(attended, d_branch))
        out_sum.begin()
        out_sum.exchange()
        qkv_sum = Reduction(by_rows(normed, d_qkv))
        qkv_sum.begin()
        qkv_sum.exchange()
        down_sum = Reduction(None)
        down_sum.half = down_half
        down_sum.exchange()
        return (
            (middle + add_up(out_got)).astype(bf16),
            d_middle,
            mlp_gain_grad,
            matmul_nt(d_qkv, full_qkv).astype(bf16),
            head_gain_grads,
            out_sum.half,
            qkv_sum.half,
            down_sum.finish(False),
        )

    gate_half, up_half = lax.psum((gate_half, up_half), "z")
    gate_half, up_half, done = fence(gate_half, up_half, block_of_work(whole, attention_part))
    output, d_middle, mlp_gain_grad, partial, head_gain_grads, out_half, qkv_half, down_full = done

    def input_part():
        d_normed = scatter(lambda k, h: half_block(partial, k, h))
        gate, up = Reduction(None), Reduction(None)
        gate.half, up.half = gate_half, up_half
        up.exchange()
        d_normed, gate_full = fence(d_normed, gate.finish(True))
        stream = tokens[0].astype(f32)
        d_stream, attn_gain_rows = norm_back(stream, rms_scale(stream), gain_attn, d_normed)
        gain_grads = jnp.concatenate(
            [jnp.sum(attn_gain_rows, axis=0), mlp_gain_grad] + head_gain_grads
        )
        for axis in ("core", "fsdp", "z"):
            k = 1
            while k < lax.axis_size(axis):
                gain_grads = gain_grads + swap(gain_grads, axis, k)
                k *= 2
        shares, start = [], 0
        for size in sizes:
            shares.append(rows_of(gain_grads, start + me * size, size))
            start += n * size
        return shares, d_middle + d_stream, gate_full, up.finish(True)

    qkv_sum, out_sum = Reduction(None), Reduction(None)
    qkv_sum.half, out_sum.half = lax.psum((qkv_half, out_half), "z")
    qkv_sum.half, out_sum.half, done = fence(
        qkv_sum.half, out_sum.half, block_of_work(whole, input_part)
    )
    shares, input_grad, gate_full, up_full = done
    query_full, key_full, value_full = qkv_sum.finish(
        True, [q_width, kv_width, kv_width], split=True
    )
    return (
        output[None],
        input_grad[None],
        shares[0],
        query_full,
        key_full,
        value_full,
        shares[2],
        shares[3],
        out_sum.finish(False, split=True),
        shares[1],
        gate_full,
        up_full,
        down_full,
    )


def solution(mesh):
    n, replicas = mesh.shape["fsdp"], mesh.shape["dp"]
    split = Mesh(mesh.devices.reshape(n, replicas // 2, 2), ("fsdp", "z", "core"))
    dp = ("z", "core")
    in_specs = (
        P(dp, "fsdp", None),
        P(dp, None),
        P("fsdp"),
        P("fsdp", None),
        P("fsdp", None),
        P("fsdp", None),
        P("fsdp"),
        P("fsdp"),
        P(None, "fsdp"),
        P("fsdp"),
        P("fsdp", None),
        P("fsdp", None),
        P(None, "fsdp"),
        P(dp, "fsdp", None),
    )
    out_specs = (
        P(dp, "fsdp", None),
        P(dp, "fsdp", None),
        P("fsdp"),
        P("fsdp", None),
        P("fsdp", None),
        P("fsdp", None),
        P("fsdp"),
        P("fsdp"),
        P(None, "fsdp"),
        P("fsdp"),
        P("fsdp", None),
        P("fsdp", None),
        P(None, "fsdp"),
    )
    return jax.shard_map(
        on_device, mesh=split, in_specs=in_specs, out_specs=out_specs, check_vma=False
    )
```
